32 devices in a mesh: row: 4 (over z), col: 2 (over x), layer: 4 (over y, core).
Axes of the slice: x: 2, y: 2, z: 4, core: 2. Of those that a mesh axis runs over, the one named last changes fastest.
Arguments:
- p_slabs: bfloat16 [4, 1024, 256], P('layer', 'row', 'col'), may hold values from -0.1875 to 0.1875
- p_mask: int32 [4, 32, 8], P('layer', 'row', 'col'), may hold values 0 or 1
- h_slabs: bfloat16 [4, 256, 1024], P('layer', 'row', 'col'), may hold values from -12 to 12
- h_mask: int32 [4, 8, 32], P('layer', 'row', 'col'), may hold values from 0 to 1, as said below
- gauss_row: int32 [32768], P(('row', 'col', 'layer')), may hold values from 0 to 255
- gauss_col: int32 [32768], P(('row', 'col', 'layer')), may hold values from 0 to 1023
- gauss_cell: int32 [32768], P(('row', 'col', 'layer')), may hold values from 0 to 32767
- gauss_expo: float32 [32768], P(('row', 'col', 'layer')), may hold values from 0.05 to 0.6
- gauss_pref: float32 [32768], P(('row', 'col', 'layer')), may hold values from -96 to 96
Outputs:
- product: bfloat16 [1024, 1024], P('row', ('col', 'layer'))
- density: float32 [64, 32, 512], P('row', 'col', 'layer')
The draws below stay inside these ranges and needn't reach their ends.
Inputs may be any that keep to these rules, and one draw needn't show every extreme that they name: Each device's tile of h_mask (block rows l, r * 2 to r * 2 + 1, block columns c * 16 to c * 16 + 15) has at most 16 ones; some tile has exactly 16.
All inputs are finite; a program needn't handle non-finite values. No bound on the sum of `p_mask` on one device may be relied on, other than what follows from the above.
Results may differ from the reference program's by a relative error of at most 0.001.
Values may be sent and summed in bfloat16 or wider, within the bound.
No kernel may reach another device: no remote copies, remote signals or barrier semaphores. Data moves between devices by JAX's collectives and lax.ppermute only.
A program may use at most 64 MiB of HBM per device.

```python
import math
import jax
import jax.numpy as jnp
from jax import lax

BS = 32
HB = 2
N = 1024
LAYERS = 4
HCB = 16
HCAP = 16
BAND = 256
GX = 16
GY = 16
GZ = 128
R = 4
NG = 1024
GAUSS = 32768
N_ROW = 4
N_COL = 2
N_LAYER = 4


def draw_h_mask(key, part):
    row_tiles = N // (LAYERS * BS * HB)
    col_tiles = N // BS // HCB
    tiles = LAYERS * row_tiles * col_tiles
    blocks = HB * HCB
    count_key = jax.random.fold_in(key, 11)
    pick_key = jax.random.fold_in(key, 12)
    perm_key = jax.random.fold_in(key, 13)
    counts = jax.random.randint(count_key, (tiles,), HCAP // 2, HCAP + 1)
    full_tile = jax.random.randint(pick_key, (), 0, tiles)
    counts = counts.at[full_tile].set(HCAP)
    keys = jax.random.split(perm_key, tiles)

    def one_tile(tile_key, count):
        order = jax.random.permutation(tile_key, blocks)
        rank = jnp.zeros((blocks,), jnp.int32).at[order].set(jnp.arange(blocks, dtype=jnp.int32))
        return (rank < count).astype(jnp.int32)
    flat = jax.vmap(one_tile)(keys, counts)
    grid = flat.reshape(LAYERS, row_tiles, col_tiles, HB, HCB)
    return jnp.transpose(grid, (0, 1, 3, 2, 4)).reshape(LAYERS, row_tiles * HB, col_tiles * HCB)


def with_ends(entries, stream_key, low, high):
    spot = [jax.random.randint(jax.random.fold_in(stream_key, axis), (), 0, length) for axis, length in enumerate(entries.shape)]
    main_axis = entries.shape.index(max(entries.shape))
    beside = spot[:main_axis] + [(spot[main_axis] + 1) % entries.shape[main_axis]] + spot[main_axis + 1:]
    return entries.at[tuple(spot)].set(low).at[tuple(beside)].set(high)


def block_scale(own_key, shape, pieces, low, largest):
    loudness = 1.0
    for axis_at, blocks in pieces:
        heights = jax.random.uniform(jax.random.fold_in(jax.random.fold_in(own_key, 6), axis_at), (blocks,), jnp.float32, low / len(pieces), largest / len(pieces))
        loudness = loudness * jnp.repeat(jnp.exp(heights), shape[axis_at] // blocks).reshape((-1,) + (1,) * (len(shape) - 1 - axis_at))
    return loudness


def bell_draw(key, extent, scale, limit, pieces=(), kind=jnp.bfloat16):
    values = scale * jax.random.normal(key, extent, jnp.float32)
    if pieces:
        values = values * block_scale(key, extent, pieces, -0.22, 0.18)
    return jnp.clip(values, -limit, limit).astype(kind)


def setup_inputs(seed: int = 0) -> dict:
    arg_keys = jax.random.split(jax.random.key(seed), 10)
    p_slabs = bell_draw(arg_keys[0], (LAYERS, N, N // LAYERS), N ** -0.5, 0.1875, ((0, 4), (1, 4), (2, 2)))
    p_mask = with_ends((jax.random.randint(arg_keys[1], (LAYERS, N // BS, N // (LAYERS * BS)), 0, 2) < 1).astype(jnp.int32), jax.random.fold_in(arg_keys[1], 1), 0, 1)
    h_slabs = bell_draw(arg_keys[2], (LAYERS, N // LAYERS, N), 2.0, 12.0, ((0, 4), (1, 4), (2, 2)))
    h_mask = draw_h_mask(jax.random.fold_in(arg_keys[9], 71), 0)
    gauss_row = with_ends(jax.random.randint(arg_keys[4], (GAUSS,), 0, BAND), jax.random.fold_in(arg_keys[4], 1), 0, BAND - 1).astype(jnp.int32)
    gauss_col = with_ends(jax.random.randint(arg_keys[5], (GAUSS,), 0, N), jax.random.fold_in(arg_keys[5], 1), 0, N - 1).astype(jnp.int32)
    gauss_cell = with_ends(jax.random.randint(arg_keys[6], (GAUSS,), 0, GX * GY * GZ), jax.random.fold_in(arg_keys[6], 1), 0, (GX * GY * GZ) - 1).astype(jnp.int32)
    gauss_expo = jnp.clip(jnp.exp(math.log(0.6) - 2.4849067 * jax.random.uniform(arg_keys[7], (GAUSS,), jnp.float32) ** block_scale(arg_keys[7], (GAUSS,), ((0, 32),), -0.2, 0.2)), 0.05, 0.6)
    gauss_pref = bell_draw(arg_keys[8], (GAUSS,), (N // 64), 96.0, ((0, 32),), jnp.float32)
    return dict(p_slabs=p_slabs, p_mask=p_mask, h_slabs=h_slabs, h_mask=h_mask, gauss_row=gauss_row, gauss_col=gauss_col, gauss_cell=gauss_cell, gauss_expo=gauss_expo, gauss_pref=gauss_pref)


def expand(mask):
    return jnp.repeat(jnp.repeat(mask, BS, axis=1), BS, axis=2) > 0


def profile(center, expo, length):
    pos = jnp.arange(length + 2 * R, dtype=jnp.int32) - R
    dist = pos[:, None] - center[None, :]
    dist_f = dist.astype(jnp.float32)
    value = jnp.exp(-expo[None, :] * dist_f * dist_f)
    return jnp.where(jnp.abs(dist) <= R, value, jnp.zeros_like(value))


def collocate(cell, expo, coef):
    cx = cell // (GY * GZ)
    cy = (cell // GZ) % GY
    cz = cell % GZ
    ex = profile(cx, expo, GX)
    ey = profile(cy, expo, GY)
    ez = profile(cz, expo, GZ)
    plane = (ex[:, None, :] * ey[None, :, :]).reshape((GX + 2 * R) * (GY + 2 * R), -1)
    depth = ez * coef[None, :]
    dens = lax.dot_general(plane, depth, (((1,), (1,)), ((), ())), precision=lax.Precision.HIGHEST, preferred_element_type=jnp.float32)
    return dens.reshape(GX + 2 * R, GY + 2 * R, GZ + 2 * R)


def fold(bricks, dev_axis, cell_axis, cells):
    core = lax.slice_in_dim(bricks, R, R + cells, axis=cell_axis)
    low = lax.slice_in_dim(jnp.roll(bricks, 1, dev_axis), cells + R, cells + 2 * R, axis=cell_axis)
    high = lax.slice_in_dim(jnp.roll(bricks, -1, dev_axis), 0, R, axis=cell_axis)
    widths_low = [(0, 0)] * bricks.ndim
    widths_low[cell_axis] = (0, cells - R)
    widths_high = [(0, 0)] * bricks.ndim
    widths_high[cell_axis] = (cells - R, 0)
    return core + jnp.pad(low, widths_low) + jnp.pad(high, widths_high)


def reference(p_slabs, p_mask, h_slabs, h_mask, gauss_row, gauss_col, gauss_cell, gauss_expo, gauss_pref):
    p_eff = jnp.where(expand(p_mask), p_slabs, jnp.zeros_like(p_slabs)).astype(jnp.float32)
    p_mat = jnp.transpose(p_eff, (1, 0, 2)).reshape(N, N)
    h_mat = jnp.where(expand(h_mask), h_slabs, jnp.zeros_like(h_slabs)).astype(jnp.float32).reshape(N, N)
    product = jnp.dot(p_mat, h_mat, precision=lax.Precision.HIGHEST, preferred_element_type=jnp.float32).astype(jnp.bfloat16)
    devices = N_ROW * N_COL * N_LAYER
    band_rows = N // N_ROW
    rows_in = gauss_row.reshape(devices, NG)
    cols_in = gauss_col.reshape(devices, NG)
    cell = gauss_cell.reshape(devices, NG)
    expo = gauss_expo.reshape(devices, NG)
    pref = gauss_pref.reshape(devices, NG)

    def brick(index):
        r_pos = index // (N_COL * N_LAYER)
        grow = r_pos * band_rows + rows_in[index]
        gcol = cols_in[index]
        coef = pref[index] * p_mat[grow, gcol]
        return collocate(cell[index], expo[index], coef)

    bricks = lax.map(brick, jnp.arange(devices, dtype=jnp.int32))
    bricks = bricks.reshape(N_ROW, N_COL, N_LAYER, GX + 2 * R, GY + 2 * R, GZ + 2 * R)
    bricks = fold(bricks, 0, 3, GX)
    bricks = fold(bricks, 1, 4, GY)
    bricks = fold(bricks, 2, 5, GZ)
    density = jnp.transpose(bricks, (0, 3, 1, 4, 2, 5)).reshape(GX * N_ROW, GY * N_COL, GZ * N_LAYER)
    return product, density
```

```python
import functools

import jax
import jax.numpy as jnp
from jax import lax
from jax.experimental import pallas as pl
from jax.experimental.pallas import tpu as pltpu
from jax.sharding import PartitionSpec as P

BS = 32
GX = 16
GY = 16
GZ = 128
R = 4
LANES = 128
F32 = jnp.float32
BF16 = jnp.bfloat16
HALO = R * GY
CORE = GX * GY
FIELDS = 12
VMEM = pl.BlockSpec(memory_space=pltpu.VMEM)
SMEM = pl.BlockSpec(memory_space=pltpu.SMEM)


def split3(value):
    first = value.astype(BF16)
    rest = value - first.astype(F32)
    second = rest.astype(BF16)
    third = (rest - second.astype(F32)).astype(BF16)
    return first, second, third


def masked(values, mask_ref, block_row, first_block):
    lane = lax.broadcasted_iota(jnp.int32, values.shape, 1) // BS
    keep = jnp.zeros(values.shape, jnp.int32)
    for piece in range(LANES // BS):
        keep = jnp.where(lane == piece, mask_ref[block_row, first_block + piece], keep)
    return jnp.where(keep > 0, values.astype(F32), 0.0)


def prepare_kernel(p_ref, pm_ref, h_ref, hm_ref, row_ref, col_ref, cell_ref, expo_ref, pref_ref, out_ref, hout_ref, tmp):
    layer = lax.axis_index("layer")
    count = lax.axis_size("layer")
    band = p_ref.shape[0]
    for block in range(band // BS):
        rows = pl.ds(block * BS, BS)
        tmp[rows, :] = masked(p_ref[rows, :], pm_ref, block, 0)
    out_ref[0:LANES, :] = tmp[...].T.astype(BF16)
    col = col_ref[...]
    cell = cell_ref[...]
    fields = [
        row_ref[...].astype(F32).astype(BF16),
        (col // LANES).astype(F32).astype(BF16),
        (col % LANES).astype(F32).astype(BF16),
        (cell // (GY * GZ)).astype(F32).astype(BF16),
        (cell // GZ % GY).astype(F32).astype(BF16),
        (cell % GZ).astype(F32).astype(BF16),
        *split3(expo_ref[...]),
        *split3(pref_ref[...]),
    ]
    for pair in range(FIELDS // 2):
        both = jnp.concatenate([fields[2 * pair].astype(F32), fields[2 * pair + 1].astype(F32)], axis=0)
        tall = both.astype(BF16)
        spot = (pair // 2) * 16
        lanes = pl.ds((pair % 2) * LANES, LANES)
        out_ref[LANES + spot : LANES + spot + 16, lanes] = tall
    for chunk in range(h_ref.shape[1] // LANES):
        slot = lax.rem(chunk - layer + count, count)
        for block in range(h_ref.shape[0] // BS):
            rows = pl.ds(block * BS, BS)
            cols = pl.ds(chunk * LANES, LANES)
            value = masked(h_ref[rows, cols], hm_ref, block, chunk * (LANES // BS))
            hout_ref[slot, rows, :] = value.astype(BF16)


def prepare(p, p_mask, h, h_mask, row, col, cell, expo, pref):
    return pl.pallas_call(
        prepare_kernel,
        out_shape=(
            jax.ShapeDtypeStruct((LANES + 48, p.shape[0]), BF16),
            jax.ShapeDtypeStruct((h.shape[1] // LANES, h.shape[0], LANES), BF16),
        ),
        in_specs=[VMEM, SMEM, VMEM, SMEM, VMEM, VMEM, VMEM, VMEM, VMEM],
        out_specs=(VMEM, VMEM),
        scratch_shapes=[pltpu.VMEM(p.shape, F32)],
        name="prepare",
    )(p, p_mask, h, h_mask, row, col, cell, expo, pref)


def bell(dist, expo):
    square = dist * dist
    return jnp.where(square < (R + 0.5) ** 2, jnp.exp(-expo * square), 0.0)


CHUNK = 256


def collocate_kernel(num_col, num_layer, g_ref, core_ref, low_ref, high_ref, acc, onehot, coefs, fld, planeh, planel, depth):
    col = lax.axis_index("col")
    layer = lax.axis_index("layer")
    col_shifts = [0, 1] if num_col == 2 else [0, -1, 1]
    layer_shifts = [0, -1, 1]
    wide = len(layer_shifts) * len(col_shifts)
    acc[...] = jnp.zeros_like(acc)
    band = g_ref.shape[2]

    def one(step, carry):
        which_l = step // len(col_shifts)
        which_c = lax.rem(step, len(col_shifts))
        shift_l = jnp.where(which_l == 0, 0, jnp.where(which_l == 1, -1, 1))
        shift_c = jnp.where(which_c == 0, 0, jnp.where(which_c == 1, col_shifts[1], 1))
        block = lax.rem(layer + shift_l + num_layer, num_layer) * num_col + lax.rem(col + shift_c + num_col, num_col)
        for pair in range(FIELDS // 2):
            rows = pl.ds(LANES + (pair // 2) * 16, 16)
            lanes = pl.ds((pair % 2) * LANES, LANES)
            fld[16 * pair : 16 * pair + 16, :] = g_ref[block, rows, lanes].astype(F32)

        def field(index, part):
            return fld[8 * index + part : 8 * index + part + 1, :]

        for part in range(8):
            lanes = pl.ds(part * LANES, LANES)
            at = lax.broadcasted_iota(jnp.int32, (band, LANES), 0).astype(F32)
            onehot[:, lanes] = jnp.where(at == field(0, part), 1.0, 0.0).astype(BF16)
        for part in range(8):
            lanes = pl.ds(part * LANES, LANES)
            block_of = field(1, part)
            lane_of = field(2, part)
            picked = jnp.zeros((LANES, LANES), F32)
            for other in range(num_col * num_layer):
                found = jnp.dot(g_ref[other, 0:LANES, :], onehot[:, lanes], preferred_element_type=F32)
                picked = jnp.where(block_of == float(other), found, picked)
            at = lax.broadcasted_iota(jnp.int32, (LANES, LANES), 0).astype(F32)
            value = jnp.sum(jnp.where(at == lane_of, picked, 0.0), axis=0, keepdims=True)
            pref = field(9, part) + field(10, part) + field(11, part)
            coefs[0:1, lanes] = pref * value
        for part in range(8):
            lanes = pl.ds(part * LANES, LANES)
            expo = field(6, part) + field(7, part) + field(8, part)
            x_at = lax.broadcasted_iota(jnp.int32, (GX + 2 * R, LANES), 0).astype(F32) - float(R)
            ex = bell(x_at - field(3, part), expo)
            y_at = lax.broadcasted_iota(jnp.int32, (GY, LANES), 0).astype(F32)
            dy = y_at - field(4, part) - (shift_c * GY).astype(F32)
            if num_col == 2:
                dy = jnp.where(dy < -float(GY), dy + 2.0 * GY, dy)
            ey = bell(dy, expo)
            z_at = lax.broadcasted_iota(jnp.int32, (GZ, LANES), 0).astype(F32)
            dz = z_at - field(5, part) - (shift_l * GZ).astype(F32)
            ez = bell(dz, expo) * coefs[0:1, lanes]
            ez_hi = ez.astype(BF16)
            depth[0:GZ, lanes] = ez_hi
            depth[GZ : 2 * GZ, lanes] = (ez - ez_hi.astype(F32)).astype(BF16)
            for x in range(GX + 2 * R):
                plane = ex[x : x + 1, :] * ey
                plane_hi = plane.astype(BF16)
                planeh[x * GY : x * GY + GY, lanes] = plane_hi
                planel[x * GY : x * GY + GY, lanes] = (plane - plane_hi.astype(F32)).astype(BF16)
        contract = (((1,), (1,)), ((), ()))
        first = lax.dot_general(planeh[...], depth[...], contract, preferred_element_type=F32)
        second = lax.dot_general(planel[...], depth[0:GZ, :], contract, preferred_element_type=F32)
        acc[...] += first[:, 0:GZ] + first[:, GZ : 2 * GZ] + second
        return carry

    lax.fori_loop(0, wide, one, 0)
    low_ref[...] = acc[0:HALO, :]
    core_ref[...] = acc[HALO : HALO + CORE, :]
    high_ref[...] = acc[HALO + CORE : CORE + 2 * HALO, :]


def collocate(gathered, num_col, num_layer):
    full = CORE + 2 * HALO
    return pl.pallas_call(
        functools.partial(collocate_kernel, num_col, num_layer),
        out_shape=(
            jax.ShapeDtypeStruct((CORE, GZ), F32),
            jax.ShapeDtypeStruct((HALO, GZ), F32),
            jax.ShapeDtypeStruct((HALO, GZ), F32),
        ),
        in_specs=[VMEM],
        out_specs=(VMEM, VMEM, VMEM),
        scratch_shapes=[
            pltpu.VMEM((full, GZ), F32),
            pltpu.VMEM((gathered.shape[2], 1024), BF16),
            pltpu.VMEM((8, 1024), F32),
            pltpu.VMEM((8 * FIELDS, LANES), F32),
            pltpu.VMEM((full, 1024), BF16),
            pltpu.VMEM((full, 1024), BF16),
            pltpu.VMEM((2 * GZ, 1024), BF16),
        ],
        compiler_params=pltpu.CompilerParams(vmem_limit_bytes=40 * 1024 * 1024),
        cost_estimate=pl.CostEstimate(flops=8_000_000_000, bytes_accessed=1_000_000, transcendentals=0),
        name="collocate",
    )(gathered)


def product_kernel(num_row, num_col, num_layer, g_ref, *refs):
    h_refs, out_ref, slab = refs[:num_row], refs[num_row], refs[num_row + 1]
    row = lax.axis_index("row")
    layer = lax.axis_index("layer")
    rows = h_refs[0].shape[1]
    total = jnp.zeros(out_ref.shape, F32)
    for back in range(num_layer):
        for step in range(num_row):
            start = pl.multiple_of(lax.rem(row - step + num_row, num_row) * rows, rows)
            slab[back, pl.ds(start, rows), :] = h_refs[step][back]
    for back in range(num_layer):
        source = lax.rem(layer - back + num_layer, num_layer)
        for piece in range(num_col):
            left = g_ref[source * num_col + piece, 0:LANES, :]
            total += lax.dot_general(
                left,
                slab[back, piece * LANES : piece * LANES + LANES, :],
                (((0,), (0,)), ((), ())),
                preferred_element_type=F32,
            )
    out_ref[...] = total.astype(BF16)


def multiply(gathered, parts, num_row, num_col, num_layer):
    return pl.pallas_call(
        functools.partial(product_kernel, num_row, num_col, num_layer),
        out_shape=jax.ShapeDtypeStruct((gathered.shape[2], LANES), BF16),
        in_specs=[VMEM] * (num_row + 1),
        out_specs=VMEM,
        scratch_shapes=[pltpu.VMEM((num_layer, num_col * LANES, LANES), BF16)],
        compiler_params=pltpu.CompilerParams(vmem_limit_bytes=40 * 1024 * 1024),
        cost_estimate=pl.CostEstimate(flops=500_000_000, bytes_accessed=1_000_000, transcendentals=0),
        name="multiply",
    )(gathered, *parts)


def fold_kernel(core_ref, below_ref, above_ref, out_ref):
    out_ref[0:HALO, :] = core_ref[0:HALO, :] + below_ref[...]
    out_ref[HALO : CORE - HALO, :] = core_ref[HALO : CORE - HALO, :]
    out_ref[CORE - HALO : CORE, :] = core_ref[CORE - HALO : CORE, :] + above_ref[...]


def fold(core, below, above):
    return pl.pallas_call(
        fold_kernel,
        out_shape=jax.ShapeDtypeStruct((CORE, GZ), F32),
        in_specs=[VMEM, VMEM, VMEM],
        out_specs=VMEM,
        name="fold",
    )(core, below, above)


def shifted(value, axis, count, step):
    return lax.ppermute(value, axis, [(i, (i + step) % count) for i in range(count)])


def on_device(p_slabs, p_mask, h_slabs, h_mask, gauss_row, gauss_col, gauss_cell, gauss_expo, gauss_pref):
    num_row, num_col, num_layer = (lax.axis_size(axis) for axis in ("row", "col", "layer"))
    flat = [x.reshape(8, LANES) for x in (gauss_row, gauss_col, gauss_cell, gauss_expo, gauss_pref)]
    payload, h_parts = prepare(p_slabs[0], p_mask[0], h_slabs[0], h_mask[0], *flat)
    mine = [h_parts[0]]
    for step in range(1, num_layer):
        mine.append(shifted(h_parts[step], "layer", num_layer, step))
    mine = jnp.stack(mine)
    gathered = lax.all_gather(payload, ("layer", "col"), axis=0)
    parts = [mine] + [shifted(mine, "row", num_row, step) for step in range(1, num_row)]
    core, low, high = collocate(gathered, num_col, num_layer)
    below = shifted(high, "row", num_row, 1)
    above = shifted(low, "row", num_row, num_row - 1)
    product = multiply(gathered, parts, num_row, num_col, num_layer)
    density = fold(core, below, above).reshape(GX, GY, GZ)
    return (product, density)


def solution(mesh):
    placed = (P("layer", "row", "col"),) * 4 + (P(("row", "col", "layer")),) * 5
    return jax.shard_map(
        on_device,
        mesh=mesh,
        in_specs=placed,
        out_specs=(P("row", ("col", "layer")), P("row", "col", "layer")),
        check_vma=False,
    )
```

```python
import functools

import jax
import jax.numpy as jnp
from jax import lax
from jax.experimental import pallas as pl
from jax.experimental.pallas import tpu as pltpu
from jax.sharding import PartitionSpec as P

BS = 32
GX = 16
GY = 16
GZ = 128
R = 4
LANES = 128
F32 = jnp.float32
BF16 = jnp.bfloat16
HALO = R * GY
CORE = GX * GY
FULL = CORE + 2 * HALO
UNIT = 2 * LANES
PAIRS = 4
META = (PAIRS + 1) * 16
BASE = LANES + META
FLAG = 12
VMEM = pl.BlockSpec(memory_space=pltpu.VMEM)
SMEM = pl.BlockSpec(memory_space=pltpu.SMEM)
PARAMS = pltpu.CompilerParams(vmem_limit_bytes=40 * 1024 * 1024)
NT = (((1,), (1,)), ((), ()))
TN = (((0,), (0,)), ((), ()))


def iota(shape, axis):
    return lax.broadcasted_iota(jnp.int32, shape, axis).astype(F32)


def split3(value):
    first = value.astype(BF16).astype(F32)
    rest = value - first
    second = rest.astype(BF16).astype(F32)
    return first, second, rest - second


def masked(values, bits):
    lane = lax.broadcasted_iota(jnp.int32, values.shape, 1) // BS
    keep = jnp.zeros(values.shape, jnp.int32)
    for piece, bit in enumerate(bits):
        keep = jnp.where(lane == piece, bit, keep)
    return jnp.where(keep > 0, values.astype(F32), 0.0)


def ranks(flags):
    up = (iota((LANES, LANES), 0) <= iota((LANES, LANES), 1)).astype(F32).astype(BF16)
    ones = jnp.ones((LANES, LANES), BF16)
    within = jnp.dot(flags.astype(BF16), up, preferred_element_type=F32)
    totals = jnp.dot(flags.astype(BF16), ones, preferred_element_type=F32)
    row, other = iota((16, 16), 0), iota((16, 16), 1)
    same = (row < 8) == (other < 8)
    before = jnp.where(same & (other < row), 1.0, 0.0).astype(BF16)
    every = jnp.where(same, 1.0, 0.0).astype(BF16)
    earlier = jnp.dot(before, totals.astype(BF16), preferred_element_type=F32)
    count = jnp.dot(every, totals.astype(BF16), preferred_element_type=F32)
    return jnp.where(flags > 0, within + earlier - 1.0, -1.0), count


def prepare_kernel(paired, p_ref, pm_ref, h_ref, hm_ref, row_ref, col_ref, cell_ref, expo_ref, pref_ref, *refs):
    outs, (tmp, fields, matrix, onehot) = refs[:-4], refs[-4:]
    layer = lax.axis_index("layer")
    count = lax.axis_size("layer")
    band = p_ref.shape[0]
    for block in range(band // BS):
        rows = pl.ds(block * BS, BS)
        tmp[rows, :] = masked(p_ref[rows, :], [pm_ref[piece, block] for piece in range(LANES // BS)])
    turned = tmp[...].T.astype(BF16)
    col = col_ref[...]
    cell = cell_ref[...]
    cell_z = (cell % GZ).astype(F32)
    values = [
        row_ref[...].astype(F32),
        (col // LANES).astype(F32),
        (col % LANES).astype(F32),
        (cell // (GY * GZ)).astype(F32),
        (cell // GZ % GY).astype(F32),
        cell_z,
        *split3(expo_ref[...]),
        *split3(pref_ref[...]),
    ]
    for index in range(16):
        fields[8 * index : 8 * index + 8, :] = values[index] if index < len(values) else jnp.zeros((8, LANES), F32)
    tiles = [fields[pl.ds(part, 16, stride=8), :].astype(BF16) for part in range(2 * PAIRS)]
    for part in range(2 * PAIRS):
        matrix[:, part * LANES : part * LANES + LANES] = tiles[part]
    faces = jnp.concatenate([jnp.where(cell_z < R, 1.0, 0.0), jnp.where(cell_z >= GZ - R, 1.0, 0.0)], axis=0)
    place, many = ranks(faces)
    slot = iota((LANES, LANES), 0)
    for part in range(2 * PAIRS):
        lanes = pl.ds(part * LANES, LANES)
        for face in range(2):
            hit = slot == place[face * 8 + part : face * 8 + part + 1, :]
            onehot[face * LANES : face * LANES + LANES, lanes] = jnp.where(hit, 1.0, 0.0).astype(BF16)
    listed = lax.dot_general(matrix[...], onehot[...], NT, preferred_element_type=F32)
    over = jnp.where(jnp.max(many, axis=0, keepdims=True) > LANES, 1.0, 0.0)
    over = jnp.concatenate([over, over], axis=1)
    listed = jnp.where(iota(listed.shape, 0) == FLAG, over, listed).astype(BF16)
    copies = outs[:3] if paired else outs[:1]
    for out in copies:
        out[0:LANES, :] = turned
        for pair in range(PAIRS):
            out[LANES + 16 * pair : LANES + 16 * pair + 16, :] = matrix[:, pair * UNIT : pair * UNIT + UNIT]
        out[LANES + 16 * PAIRS : BASE, :] = listed

    def piece(chunk):
        pieces = LANES // BS
        out = []
        for block in range(h_ref.shape[0] // BS):
            rows = pl.ds(block * BS, BS)
            bits = [hm_ref[block, chunk * pieces + at] for at in range(pieces)]
            value = h_ref[rows, pl.ds(pl.multiple_of(chunk * LANES, LANES), LANES)]
            out.append(masked(value, bits).astype(BF16))
        return jnp.concatenate(out, axis=0)

    if paired:
        outs[1][BASE:, 0:LANES] = piece(layer ^ 2)
        outs[1][BASE:, LANES:UNIT] = piece(layer ^ 3)
        outs[2][BASE:, 0:LANES] = piece(layer ^ 1)
        outs[2][BASE:, LANES:UNIT] = jnp.zeros((h_ref.shape[0], LANES), BF16)
        outs[3][...] = piece(layer)
    else:
        for back in range(h_ref.shape[1] // LANES):
            outs[1][back] = piece(lax.rem(layer + back, count))


def prepare(paired, p, p_mask, h, h_mask, *gauss):
    band = p.shape[0]
    base = jax.ShapeDtypeStruct((BASE, band), BF16)
    tall = jax.ShapeDtypeStruct((BASE + h.shape[0], band), BF16)
    if paired:
        outs = (base, tall, tall, jax.ShapeDtypeStruct((h.shape[0], LANES), BF16))
    else:
        outs = (base, jax.ShapeDtypeStruct((h.shape[1] // LANES, h.shape[0], LANES), BF16))
    return pl.pallas_call(
        functools.partial(prepare_kernel, paired),
        out_shape=outs,
        in_specs=[VMEM, SMEM, VMEM, SMEM] + [VMEM] * 5,
        out_specs=(VMEM,) * len(outs),
        scratch_shapes=[
            pltpu.VMEM(p.shape, F32),
            pltpu.VMEM((16 * 8, LANES), F32),
            pltpu.VMEM((16, 2 * PAIRS * LANES), BF16),
            pltpu.VMEM((UNIT, 2 * PAIRS * LANES), BF16),
        ],
        compiler_params=PARAMS,
        name="prepare",
    )(p, p_mask, h, h_mask, *gauss)


class Blocks:
    def __init__(self, refs, num_col, num_layer):
        self.refs = refs
        self.num_col, self.num_layer = num_col, num_layer
        self.paired = len(refs) > 1
        self.col, self.layer = lax.axis_index("col"), lax.axis_index("layer")
        self.total = num_col * num_layer
        self.col_shifts = [0, 1] if num_col == 2 else [0, -1, 1]

    def ident(self, index):
        if not self.paired:
            return index
        return (self.layer ^ (index % 4)) * 2 + (self.col ^ (index // 4))

    def matrix(self, index):
        return self.refs[index][0:LANES, :] if self.paired else self.refs[0][index, 0:LANES, :]

    def slab(self, layer, piece):
        index = layer * self.num_col + piece
        return self.refs[0][index, 0:LANES, :]

    def tile(self, which, side, pair):
        rows = pl.ds(LANES + 16 * pair, 16)
        if self.paired:
            return self.refs[which * 4 + side][rows, :].astype(F32)
        shift_l = 0 if side == 0 else (1 if side == 1 else -1)
        index = lax.rem(self.layer + shift_l + self.num_layer, self.num_layer) * self.num_col
        index += lax.rem(self.col + self.col_shifts[which] + self.num_col, self.num_col)
        return self.refs[0][index, rows, :].astype(F32)

    def side_shift(self, side):
        if self.paired:
            even = (self.layer % 2) == 0
            return jnp.where(even, 1.0, -1.0) if side == 1 else jnp.where(even, -1.0, 1.0)
        return 1.0 if side == 1 else -1.0

    def sides(self):
        return (1, 3) if self.paired else (1, 2)

    def units(self):
        return [(which, pair) for which in range(len(self.col_shifts)) for pair in range(PAIRS + 1)]

    def listed(self, which):
        halves = []
        for side in self.sides():
            both = self.tile(which, side, PAIRS)
            upward = self.side_shift(side) > 0
            halves.append(jnp.where(upward, both[:, 0:LANES], both[:, LANES:UNIT]))
        return jnp.concatenate(halves, axis=1)

    def unit(self, which, pair):
        return self.tile(which, 0, pair) if pair < PAIRS else self.listed(which)

    def lifts(self, pair):
        if pair < PAIRS:
            return 0.0
        lane = iota((1, UNIT), 1)
        first, second = self.sides()
        return jnp.where(lane < LANES, self.side_shift(first), self.side_shift(second)) * float(GZ)

    def over(self):
        flags = [
            self.tile(which, side, PAIRS)[FLAG : FLAG + 1, :]
            for which in range(len(self.col_shifts))
            for side in self.sides()
        ]
        return functools.reduce(jnp.maximum, flags)

    def long_steps(self):
        return [(which, side) for which in range(len(self.col_shifts)) for side in self.sides()]


def weigh(blocks, whole, tile):
    band = whole.shape[1]
    onehot = jnp.where(iota((band, UNIT), 0) == tile[0:1, :], 1.0, 0.0).astype(BF16)
    found = jnp.dot(whole[...], onehot, preferred_element_type=F32)
    picked = jnp.zeros((LANES, UNIT), F32)
    for index in range(blocks.total):
        mine = tile[1:2, :] == jnp.asarray(blocks.ident(index)).astype(F32)
        picked = jnp.where(mine, found[index * LANES : index * LANES + LANES, :], picked)
    value = jnp.sum(jnp.where(iota((LANES, UNIT), 0) == tile[2:3, :], picked, 0.0), axis=0, keepdims=True)
    return (tile[9:10, :] + tile[10:11, :] + tile[11:12, :]) * value


def weigh_kernel(num_col, num_layer, refs_in, *refs):
    blocks = Blocks(refs[:refs_in], num_col, num_layer)
    coef_ref, long_ref, whole = refs[refs_in:]
    for index in range(blocks.total):
        whole[index * LANES : index * LANES + LANES, :] = blocks.matrix(index)
    over = blocks.over()
    for at, (which, pair) in enumerate(blocks.units()):
        coef = weigh(blocks, whole, blocks.unit(which, pair))
        if pair == PAIRS:
            coef = jnp.where(over > 0, 0.0, coef)
        coef_ref[at : at + 1, :] = coef

    @pl.when(jnp.max(over) > 0)
    def _():
        for at, (which, side) in enumerate(blocks.long_steps()):

            def step(pair, carry):
                long_ref[at, pl.ds(pair, 1), :] = weigh(blocks, whole, blocks.tile(which, side, pair))
                return carry

            lax.fori_loop(0, PAIRS, step, 0)


def weigh_all(arrays, num_col, num_layer):
    ways = 2 if num_col == 2 else 3
    band = arrays[0].shape[-1]
    return pl.pallas_call(
        functools.partial(weigh_kernel, num_col, num_layer, len(arrays)),
        out_shape=(
            jax.ShapeDtypeStruct((ways * (PAIRS + 1), UNIT), F32),
            jax.ShapeDtypeStruct((ways * 2, PAIRS, UNIT), F32),
        ),
        in_specs=[VMEM] * len(arrays),
        out_specs=(VMEM, VMEM),
        scratch_shapes=[pltpu.VMEM((num_col * num_layer * LANES, band), BF16)],
        compiler_params=PARAMS,
        cost_estimate=pl.CostEstimate(flops=2_000_000_000, bytes_accessed=1_000_000, transcendentals=0),
        name="weigh",
    )(*arrays)


def bell(dist, expo):
    square = dist * dist
    return jnp.where(square < (R + 0.5) ** 2, jnp.exp(-expo * square), 0.0)


def spread(blocks, tile, which, lift, coef, at, planeh, planel, depth):
    expo = tile[6:7, :] + tile[7:8, :] + tile[8:9, :]
    ex = bell(iota((GX + 2 * R, UNIT), 0) - float(R) - tile[3:4, :], expo)
    dy = iota((GY, UNIT), 0) - tile[4:5, :] - float(blocks.col_shifts[which] * GY)
    if blocks.num_col == 2 and which == 1:
        dy = jnp.where(dy < -float(GY), dy + 2.0 * GY, dy)
    ey = bell(dy, expo)
    ez = bell(iota((GZ, UNIT), 0) - tile[5:6, :] - lift, expo) * coef
    lanes = pl.ds(at * UNIT, UNIT)
    ez_hi = ez.astype(BF16)
    depth[0:GZ, lanes] = ez_hi
    depth[GZ : 2 * GZ, lanes] = (ez - ez_hi.astype(F32)).astype(BF16)
    for x in range(GX + 2 * R):
        plane = ex[x : x + 1, :] * ey
        plane_hi = plane.astype(BF16)
        planeh[x * GY : x * GY + GY, lanes] = plane_hi
        planel[x * GY : x * GY + GY, lanes] = (plane - plane_hi.astype(F32)).astype(BF16)


def summed(planeh, planel, depth):
    first = lax.dot_general(planeh, depth, NT, preferred_element_type=F32)
    second = lax.dot_general(planel, depth[0:GZ, :], NT, preferred_element_type=F32)
    return first[:, 0:GZ] + first[:, GZ : 2 * GZ] + second


def collocate_kernel(num_col, num_layer, refs_in, *refs):
    blocks = Blocks(refs[:refs_in], num_col, num_layer)
    coef_ref, long_ref, core_ref, low_ref, high_ref, planeh, planel, depth, acc = refs[refs_in:]
    for at, (which, pair) in enumerate(blocks.units()):
        spread(
            blocks, blocks.unit(which, pair), which, blocks.lifts(pair), coef_ref[at : at + 1, :], at,
            planeh, planel, depth,
        )
    total = summed(planeh[...], planel[...], depth[...])
    low_ref[...] = total[0:HALO, :]
    core_ref[...] = total[HALO : HALO + CORE, :]
    high_ref[...] = total[HALO + CORE : FULL, :]

    @pl.when(jnp.max(blocks.over()) > 0)
    def _():
        acc[...] = jnp.zeros_like(acc)
        for at, (which, side) in enumerate(blocks.long_steps()):

            def step(pair, carry):
                lift = blocks.side_shift(side) * float(GZ)
                coef = long_ref[at, pl.ds(pair, 1), :]
                spread(blocks, blocks.tile(which, side, pair), which, lift, coef, 0, planeh, planel, depth)
                acc[...] += summed(planeh[:, 0:UNIT], planel[:, 0:UNIT], depth[:, 0:UNIT])
                return carry

            lax.fori_loop(0, PAIRS, step, 0)
        low_ref[...] += acc[0:HALO, :]
        core_ref[...] += acc[HALO : HALO + CORE, :]
        high_ref[...] += acc[HALO + CORE : FULL, :]


def collocate(arrays, coef, long, num_col, num_layer):
    gaussians = coef.shape[0] * UNIT
    return pl.pallas_call(
        functools.partial(collocate_kernel, num_col, num_layer, len(arrays)),
        out_shape=(
            jax.ShapeDtypeStruct((CORE, GZ), F32),
            jax.ShapeDtypeStruct((HALO, GZ), F32),
            jax.ShapeDtypeStruct((HALO, GZ), F32),
        ),
        in_specs=[VMEM] * (len(arrays) + 2),
        out_specs=(VMEM, VMEM, VMEM),
        scratch_shapes=[
            pltpu.VMEM((FULL, gaussians), BF16),
            pltpu.VMEM((FULL, gaussians), BF16),
            pltpu.VMEM((2 * GZ, gaussians), BF16),
            pltpu.VMEM((FULL, GZ), F32),
        ],
        compiler_params=PARAMS,
        cost_estimate=pl.CostEstimate(flops=3_000_000_000, bytes_accessed=1_000_000, transcendentals=0),
        name="collocate",
    )(*arrays, coef, long)


def product_kernel(num_row, num_col, num_layer, refs_in, *refs):
    blocks = Blocks(refs[:refs_in], num_col, num_layer)
    h_refs = refs[refs_in : refs_in + num_row]
    out_ref, slab = refs[refs_in + num_row :]
    row = lax.axis_index("row")
    rows = h_refs[0].shape[1]
    for back in range(num_layer):
        for step in range(num_row):
            start = pl.multiple_of(lax.rem(row - step + num_row, num_row) * rows, rows)
            slab[back, pl.ds(start, rows), :] = h_refs[step][back]
    total = jnp.zeros(out_ref.shape, F32)
    for back in range(num_layer):
        for piece in range(num_col):
            if blocks.paired:
                left = blocks.matrix(piece * 4 + back)
                start = pl.multiple_of((blocks.col ^ piece) * LANES, LANES)
            else:
                source = lax.rem(blocks.layer - back + num_layer, num_layer)
                left = blocks.slab(source, piece)
                start = piece * LANES
            right = slab[back, pl.ds(start, LANES), :]
            total += lax.dot_general(left, right, TN, preferred_element_type=F32)
    out_ref[...] = total.astype(BF16)


def multiply(arrays, parts, num_row, num_col, num_layer):
    return pl.pallas_call(
        functools.partial(product_kernel, num_row, num_col, num_layer, len(arrays)),
        out_shape=jax.ShapeDtypeStruct((arrays[0].shape[-1], LANES), BF16),
        in_specs=[VMEM] * (num_row + len(arrays)),
        out_specs=VMEM,
        scratch_shapes=[pltpu.VMEM((num_layer, num_col * LANES, LANES), BF16)],
        compiler_params=PARAMS,
        cost_estimate=pl.CostEstimate(flops=500_000_000, bytes_accessed=1_000_000, transcendentals=0),
        name="multiply",
    )(*arrays, *parts)


def stack_kernel(rows, own_ref, near_ref, far_ref, both_ref, out_ref):
    out_ref[0] = own_ref[...]
    out_ref[1] = near_ref[BASE:, 0:LANES]
    out_ref[2] = far_ref[BASE:, 0:LANES]
    out_ref[3] = both_ref[BASE:, LANES:UNIT]


def stack(own, near, far, both):
    rows = own.shape[0]
    return pl.pallas_call(
        functools.partial(stack_kernel, rows),
        out_shape=jax.ShapeDtypeStruct((4, rows, LANES), BF16),
        in_specs=[VMEM] * 4,
        out_specs=VMEM,
        compiler_params=PARAMS,
        name="stack",
    )(own, near, far, both)


def fold_kernel(core_ref, below_ref, above_ref, out_ref):
    out_ref[0:HALO, :] = core_ref[0:HALO, :] + below_ref[...]
    out_ref[HALO : CORE - HALO, :] = core_ref[HALO : CORE - HALO, :]
    out_ref[CORE - HALO : CORE, :] = core_ref[CORE - HALO : CORE, :] + above_ref[...]


def fold(core, below, above):
    return pl.pallas_call(
        fold_kernel,
        out_shape=jax.ShapeDtypeStruct((CORE, GZ), F32),
        in_specs=[VMEM, VMEM, VMEM],
        out_specs=VMEM,
        name="fold",
    )(core, below, above)


def shifted(value, axis, count, step):
    return lax.ppermute(value, axis, [(i, (i + step) % count) for i in range(count)])


def crossed(value, col_bit, layer_bits):
    pairs = [(c * 4 + l, (c ^ col_bit) * 4 + (l ^ layer_bits)) for c in range(2) for l in range(4)]
    return lax.ppermute(value, ("col", "layer"), pairs)


def gather_paired(base, tall_y, tall_core):
    got_x = crossed(base, 1, 0)
    got_y = crossed(tall_y, 0, 2)
    got_xy = crossed(base, 1, 2)
    near = crossed(tall_core, 0, 1)
    near_x = crossed(got_x, 0, 1)
    near_y = crossed(got_y, 0, 1)
    near_xy = crossed(got_xy, 0, 1)
    return [base, near, got_y, near_y, got_x, near_x, got_xy, near_xy]


def on_device(p_slabs, p_mask, h_slabs, h_mask, gauss_row, gauss_col, gauss_cell, gauss_expo, gauss_pref):
    num_row, num_col, num_layer = (lax.axis_size(axis) for axis in ("row", "col", "layer"))
    paired = num_col == 2 and num_layer == 4
    flat = [x.reshape(8, LANES) for x in (gauss_row, gauss_col, gauss_cell, gauss_expo, gauss_pref)]
    made = prepare(paired, p_slabs[0], p_mask[0].T, h_slabs[0], h_mask[0], *flat)
    if paired:
        base, tall_y, tall_core, own = made
        arrays = gather_paired(base, tall_y, tall_core)
        mine = stack(own, arrays[1], arrays[2], arrays[3])
    else:
        base, pieces = made
        arrays = [lax.all_gather(base, ("layer", "col"), axis=0)]
        mine = [pieces[0]] + [shifted(pieces[step], "layer", num_layer, step) for step in range(1, num_layer)]
        mine = jnp.stack(mine)
    parts = [mine] + [shifted(mine, "row", num_row, step) for step in range(1, num_row)]
    coef, long = weigh_all(arrays, num_col, num_layer)
    core, low, high = collocate(arrays, coef, long, num_col, num_layer)
    below = shifted(high, "row", num_row, 1)
    above = shifted(low, "row", num_row, num_row - 1)
    product = multiply(arrays, parts, num_row, num_col, num_layer)
    density = fold(core, below, above).reshape(GX, GY, GZ)
    return (product, density)


def solution(mesh):
    placed = (P("layer", "row", "col"),) * 4 + (P(("row", "col", "layer")),) * 5
    return jax.shard_map(
        on_device,
        mesh=mesh,
        in_specs=placed,
        out_specs=(P("row", ("col", "layer")), P("row", "col", "layer")),
        check_vma=False,
    )
```

```python
import functools

import jax
import jax.numpy as jnp
from jax import lax
from jax.experimental import pallas as pl
from jax.experimental.pallas import tpu as pltpu
from jax.sharding import PartitionSpec as P

BS = 32
GX = 16
GY = 16
GZ = 128
R = 4
LANES = 128
F32 = jnp.float32
BF16 = jnp.bfloat16
HALO = R * GY
CORE = GX * GY
FULL = CORE + 2 * HALO
UNIT = 2 * LANES
PAIRS = 4
META = (PAIRS + 1) * 16
BASE = LANES + META
FLAG = 12
VMEM = pl.BlockSpec(memory_space=pltpu.VMEM)
HBM = pl.BlockSpec(memory_space=pltpu.HBM)
PARAMS = pltpu.CompilerParams(vmem_limit_bytes=40 * 1024 * 1024)
NT = (((1,), (1,)), ((), ()))
TN = (((0,), (0,)), ((), ()))


def iota(shape, axis):
    return lax.broadcasted_iota(jnp.int32, shape, axis).astype(F32)


def split3(value):
    first = value.astype(BF16).astype(F32)
    rest = value - first
    second = rest.astype(BF16).astype(F32)
    return first, second, rest - second


def masked(values, bits):
    lane = lax.broadcasted_iota(jnp.int32, values.shape, 1) // BS
    keep = jnp.zeros(values.shape, jnp.int32)
    for piece, bit in enumerate(bits):
        keep = jnp.where(lane == piece, bit, keep)
    return jnp.where(keep > 0, values.astype(F32), 0.0)


def ranks(flags):
    up = (iota((LANES, LANES), 0) <= iota((LANES, LANES), 1)).astype(F32).astype(BF16)
    ones = jnp.ones((LANES, LANES), BF16)
    within = jnp.dot(flags.astype(BF16), up, preferred_element_type=F32)
    totals = jnp.dot(flags.astype(BF16), ones, preferred_element_type=F32)
    row, other = iota((16, 16), 0), iota((16, 16), 1)
    same = (row < 8) == (other < 8)
    before = jnp.where(same & (other < row), 1.0, 0.0).astype(BF16)
    every = jnp.where(same, 1.0, 0.0).astype(BF16)
    earlier = jnp.dot(before, totals.astype(BF16), preferred_element_type=F32)
    count = jnp.dot(every, totals.astype(BF16), preferred_element_type=F32)
    return jnp.where(flags > 0, within + earlier - 1.0, -1.0), count


def prepare_kernel(paired, *refs):
    sources, outs, refs = refs[:9], refs[9:-14], refs[-14:]
    landed, (tmp, fields, matrix, onehot, sems) = refs[:9], refs[9:]
    copies = [pltpu.make_async_copy(src, dst, sems.at[at]) for at, (src, dst) in enumerate(zip(sources, landed))]
    for copy in copies:
        copy.start()
    for copy in copies:
        copy.wait()
    p_ref, pm_ref, h_ref, hm_ref, row_ref, col_ref, cell_ref, expo_ref, pref_ref = landed
    layer = lax.axis_index("layer")
    count = lax.axis_size("layer")
    band = p_ref.shape[0]
    for block in range(band // BS):
        rows = pl.ds(block * BS, BS)
        tmp[rows, :] = masked(p_ref[rows, :], [pm_ref[piece, block] for piece in range(LANES // BS)])
    turned = tmp[...].T.astype(BF16)
    col = col_ref[...]
    cell = cell_ref[...]
    cell_z = (cell % GZ).astype(F32)
    values = [
        row_ref[...].astype(F32),
        (col // LANES).astype(F32),
        (col % LANES).astype(F32),
        (cell // (GY * GZ)).astype(F32),
        (cell // GZ % GY).astype(F32),
        cell_z,
        *split3(expo_ref[...]),
        *split3(pref_ref[...]),
    ]
    for index in range(16):
        fields[8 * index : 8 * index + 8, :] = values[index] if index < len(values) else jnp.zeros((8, LANES), F32)
    tiles = [fields[pl.ds(part, 16, stride=8), :].astype(BF16) for part in range(2 * PAIRS)]
    for part in range(2 * PAIRS):
        matrix[:, part * LANES : part * LANES + LANES] = tiles[part]
    faces = jnp.concatenate([jnp.where(cell_z < R, 1.0, 0.0), jnp.where(cell_z >= GZ - R, 1.0, 0.0)], axis=0)
    place, many = ranks(faces)
    slot = iota((LANES, LANES), 0)
    for part in range(2 * PAIRS):
        lanes = pl.ds(part * LANES, LANES)
        for face in range(2):
            hit = slot == place[face * 8 + part : face * 8 + part + 1, :]
            onehot[face * LANES : face * LANES + LANES, lanes] = jnp.where(hit, 1.0, 0.0).astype(BF16)
    listed = lax.dot_general(matrix[...], onehot[...], NT, preferred_element_type=F32)
    over = jnp.where(jnp.max(many, axis=0, keepdims=True) > LANES, 1.0, 0.0)
    over = jnp.concatenate([over, over], axis=1)
    listed = jnp.where(iota(listed.shape, 0) == FLAG, over, listed).astype(BF16)
    copies = outs[:3] if paired else outs[:1]
    for out in copies:
        out[0:LANES, :] = turned
        for pair in range(PAIRS):
            out[LANES + 16 * pair : LANES + 16 * pair + 16, :] = matrix[:, pair * UNIT : pair * UNIT + UNIT]
        out[LANES + 16 * PAIRS : BASE, :] = listed

    def piece(chunk):
        pieces = LANES // BS
        out = []
        for block in range(h_ref.shape[0] // BS):
            rows = pl.ds(block * BS, BS)
            bits = [hm_ref[block, chunk * pieces + at] for at in range(pieces)]
            value = h_ref[rows, pl.ds(pl.multiple_of(chunk * LANES, LANES), LANES)]
            out.append(masked(value, bits).astype(BF16))
        return jnp.concatenate(out, axis=0)

    if paired:
        outs[1][BASE:, 0:LANES] = piece(layer ^ 2)
        outs[1][BASE:, LANES:UNIT] = piece(layer ^ 3)
        outs[2][BASE:, 0:LANES] = piece(layer ^ 1)
        outs[2][BASE:, LANES:UNIT] = jnp.zeros((h_ref.shape[0], LANES), BF16)
        outs[3][...] = piece(layer)
    else:
        for back in range(h_ref.shape[1] // LANES):
            outs[1][back] = piece(lax.rem(layer + back, count))


def prepare(paired, p, p_mask, h, h_mask, *gauss):
    band = p.shape[0]
    base = jax.ShapeDtypeStruct((BASE, band), BF16)
    tall = jax.ShapeDtypeStruct((BASE + h.shape[0], band), BF16)
    if paired:
        outs = (base, tall, tall, jax.ShapeDtypeStruct((h.shape[0], LANES), BF16))
    else:
        outs = (base, jax.ShapeDtypeStruct((h.shape[1] // LANES, h.shape[0], LANES), BF16))
    return pl.pallas_call(
        functools.partial(prepare_kernel, paired),
        out_shape=outs,
        in_specs=[HBM] * 9,
        out_specs=(VMEM,) * len(outs),
        scratch_shapes=[
            pltpu.VMEM(p.shape, p.dtype),
            pltpu.SMEM(p_mask.shape, p_mask.dtype),
            pltpu.VMEM(h.shape, h.dtype),
            pltpu.SMEM(h_mask.shape, h_mask.dtype),
            *[pltpu.VMEM(x.shape, x.dtype) for x in gauss],
            pltpu.VMEM(p.shape, F32),
            pltpu.VMEM((16 * 8, LANES), F32),
            pltpu.VMEM((16, 2 * PAIRS * LANES), BF16),
            pltpu.VMEM((UNIT, 2 * PAIRS * LANES), BF16),
            pltpu.SemaphoreType.DMA((9,)),
        ],
        compiler_params=pltpu.CompilerParams(vmem_limit_bytes=62 * 1024 * 1024),
        name="prepare",
    )(p, p_mask, h, h_mask, *gauss)


class Blocks:
    def __init__(self, refs, num_col, num_layer):
        self.refs = refs
        self.num_col, self.num_layer = num_col, num_layer
        self.paired = len(refs) > 1
        self.col, self.layer = lax.axis_index("col"), lax.axis_index("layer")
        self.total = num_col * num_layer
        self.col_shifts = [0, 1] if num_col == 2 else [0, -1, 1]

    def ident(self, index):
        if not self.paired:
            return index
        return (self.layer ^ (index % 4)) * 2 + (self.col ^ (index // 4))

    def matrix(self, index):
        return self.refs[index][0:LANES, :] if self.paired else self.refs[0][index, 0:LANES, :]

    def slab(self, layer, piece):
        index = layer * self.num_col + piece
        return self.refs[0][index, 0:LANES, :]

    def tile(self, which, side, pair):
        rows = pl.ds(LANES + 16 * pair, 16)
        if self.paired:
            return self.refs[which * 4 + side][rows, :].astype(F32)
        shift_l = 0 if side == 0 else (1 if side == 1 else -1)
        index = lax.rem(self.layer + shift_l + self.num_layer, self.num_layer) * self.num_col
        index += lax.rem(self.col + self.col_shifts[which] + self.num_col, self.num_col)
        return self.refs[0][index, rows, :].astype(F32)

    def side_shift(self, side):
        if self.paired:
            even = (self.layer % 2) == 0
            return jnp.where(even, 1.0, -1.0) if side == 1 else jnp.where(even, -1.0, 1.0)
        return 1.0 if side == 1 else -1.0

    def sides(self):
        return (1, 3) if self.paired else (1, 2)

    def units(self):
        return [(which, pair) for which in range(len(self.col_shifts)) for pair in range(PAIRS + 1)]

    def listed(self, which):
        halves = []
        for side in self.sides():
            both = self.tile(which, side, PAIRS)
            upward = self.side_shift(side) > 0
            halves.append(jnp.where(upward, both[:, 0:LANES], both[:, LANES:UNIT]))
        return jnp.concatenate(halves, axis=1)

    def unit(self, which, pair):
        return self.tile(which, 0, pair) if pair < PAIRS else self.listed(which)

    def lifts(self, pair):
        if pair < PAIRS:
            return 0.0
        lane = iota((1, UNIT), 1)
        first, second = self.sides()
        return jnp.where(lane < LANES, self.side_shift(first), self.side_shift(second)) * float(GZ)

    def over(self):
        flags = [
            self.tile(which, side, PAIRS)[FLAG : FLAG + 1, :]
            for which in range(len(self.col_shifts))
            for side in self.sides()
        ]
        return functools.reduce(jnp.maximum, flags)

    def long_steps(self):
        return [(which, side) for which in range(len(self.col_shifts)) for side in self.sides()]


def weigh(blocks, whole, tile):
    band = whole.shape[1]
    onehot = jnp.where(iota((band, UNIT), 0) == tile[0:1, :], 1.0, 0.0).astype(BF16)
    found = jnp.dot(whole[...], onehot, preferred_element_type=F32)
    picked = jnp.zeros((LANES, UNIT), F32)
    for index in range(blocks.total):
        mine = tile[1:2, :] == jnp.asarray(blocks.ident(index)).astype(F32)
        picked = jnp.where(mine, found[index * LANES : index * LANES + LANES, :], picked)
    value = jnp.sum(jnp.where(iota((LANES, UNIT), 0) == tile[2:3, :], picked, 0.0), axis=0, keepdims=True)
    return (tile[9:10, :] + tile[10:11, :] + tile[11:12, :]) * value


def weigh_kernel(num_col, num_layer, refs_in, *refs):
    blocks = Blocks(refs[:refs_in], num_col, num_layer)
    coef_ref, long_ref, whole = refs[refs_in:]
    for index in range(blocks.total):
        whole[index * LANES : index * LANES + LANES, :] = blocks.matrix(index)
    over = blocks.over()
    for at, (which, pair) in enumerate(blocks.units()):
        coef = weigh(blocks, whole, blocks.unit(which, pair))
        if pair == PAIRS:
            coef = jnp.where(over > 0, 0.0, coef)
        coef_ref[at : at + 1, :] = coef

    @pl.when(jnp.max(over) > 0)
    def _():
        for at, (which, side) in enumerate(blocks.long_steps()):

            def step(pair, carry):
                long_ref[at, pl.ds(pair, 1), :] = weigh(blocks, whole, blocks.tile(which, side, pair))
                return carry

            lax.fori_loop(0, PAIRS, step, 0)


def weigh_all(arrays, num_col, num_layer):
    ways = 2 if num_col == 2 else 3
    band = arrays[0].shape[-1]
    return pl.pallas_call(
        functools.partial(weigh_kernel, num_col, num_layer, len(arrays)),
        out_shape=(
            jax.ShapeDtypeStruct((ways * (PAIRS + 1), UNIT), F32),
            jax.ShapeDtypeStruct((ways * 2, PAIRS, UNIT), F32),
        ),
        in_specs=[VMEM] * len(arrays),
        out_specs=(VMEM, VMEM),
        scratch_shapes=[pltpu.VMEM((num_col * num_layer * LANES, band), BF16)],
        compiler_params=PARAMS,
        cost_estimate=pl.CostEstimate(flops=2_000_000_000, bytes_accessed=1_000_000, transcendentals=0),
        name="weigh",
    )(*arrays)


def bell(dist, expo):
    square = dist * dist
    return jnp.where(square < (R + 0.5) ** 2, jnp.exp(-expo * square), 0.0)


def spread(blocks, tile, which, lift, coef, at, planeh, planel, depth):
    expo = tile[6:7, :] + tile[7:8, :] + tile[8:9, :]
    ex = bell(iota((GX + 2 * R, UNIT), 0) - float(R) - tile[3:4, :], expo)
    dy = iota((GY, UNIT), 0) - tile[4:5, :] - float(blocks.col_shifts[which] * GY)
    if blocks.num_col == 2 and which == 1:
        dy = jnp.where(dy < -float(GY), dy + 2.0 * GY, dy)
    ey = bell(dy, expo)
    ez = bell(iota((GZ, UNIT), 0) - tile[5:6, :] - lift, expo) * coef
    lanes = pl.ds(at * UNIT, UNIT)
    ez_hi = ez.astype(BF16)
    depth[0:GZ, lanes] = ez_hi
    depth[GZ : 2 * GZ, lanes] = (ez - ez_hi.astype(F32)).astype(BF16)
    for x in range(GX + 2 * R):
        plane = ex[x : x + 1, :] * ey
        plane_hi = plane.astype(BF16)
        planeh[x * GY : x * GY + GY, lanes] = plane_hi
        planel[x * GY : x * GY + GY, lanes] = (plane - plane_hi.astype(F32)).astype(BF16)


def summed(planeh, planel, depth):
    first = lax.dot_general(planeh, depth, NT, preferred_element_type=F32)
    second = lax.dot_general(planel, depth[0:GZ, :], NT, preferred_element_type=F32)
    return first[:, 0:GZ] + first[:, GZ : 2 * GZ] + second


def collocate_kernel(num_col, num_layer, refs_in, *refs):
    blocks = Blocks(refs[:refs_in], num_col, num_layer)
    coef_ref, long_ref, core_ref, low_ref, high_ref, planeh, planel, depth, acc = refs[refs_in:]
    for at, (which, pair) in enumerate(blocks.units()):
        spread(
            blocks, blocks.unit(which, pair), which, blocks.lifts(pair), coef_ref[at : at + 1, :], at,
            planeh, planel, depth,
        )
    total = summed(planeh[...], planel[...], depth[...])
    low_ref[...] = total[0:HALO, :]
    core_ref[...] = total[HALO : HALO + CORE, :]
    high_ref[...] = total[HALO + CORE : FULL, :]

    @pl.when(jnp.max(blocks.over()) > 0)
    def _():
        acc[...] = jnp.zeros_like(acc)
        for at, (which, side) in enumerate(blocks.long_steps()):

            def step(pair, carry):
                lift = blocks.side_shift(side) * float(GZ)
                coef = long_ref[at, pl.ds(pair, 1), :]
                spread(blocks, blocks.tile(which, side, pair), which, lift, coef, 0, planeh, planel, depth)
                acc[...] += summed(planeh[:, 0:UNIT], planel[:, 0:UNIT], depth[:, 0:UNIT])
                return carry

            lax.fori_loop(0, PAIRS, step, 0)
        low_ref[...] += acc[0:HALO, :]
        core_ref[...] += acc[HALO : HALO + CORE, :]
        high_ref[...] += acc[HALO + CORE : FULL, :]


def collocate(arrays, coef, long, num_col, num_layer):
    gaussians = coef.shape[0] * UNIT
    return pl.pallas_call(
        functools.partial(collocate_kernel, num_col, num_layer, len(arrays)),
        out_shape=(
            jax.ShapeDtypeStruct((CORE, GZ), F32),
            jax.ShapeDtypeStruct((HALO, GZ), F32),
            jax.ShapeDtypeStruct((HALO, GZ), F32),
        ),
        in_specs=[VMEM] * (len(arrays) + 2),
        out_specs=(VMEM, VMEM, VMEM),
        scratch_shapes=[
            pltpu.VMEM((FULL, gaussians), BF16),
            pltpu.VMEM((FULL, gaussians), BF16),
            pltpu.VMEM((2 * GZ, gaussians), BF16),
            pltpu.VMEM((FULL, GZ), F32),
        ],
        compiler_params=PARAMS,
        cost_estimate=pl.CostEstimate(flops=3_000_000_000, bytes_accessed=1_000_000, transcendentals=0),
        name="collocate",
    )(*arrays, coef, long)


def product_kernel(num_row, num_col, num_layer, refs_in, *refs):
    blocks = Blocks(refs[:refs_in], num_col, num_layer)
    h_refs = refs[refs_in : refs_in + num_row]
    out_ref, token_ref, slab = refs[refs_in + num_row :]
    token_ref[...] = jnp.zeros_like(token_ref)
    row = lax.axis_index("row")
    rows = h_refs[0].shape[1]
    for back in range(num_layer):
        for step in range(num_row):
            start = pl.multiple_of((row ^ step) * rows, rows)
            slab[back, pl.ds(start, rows), :] = h_refs[step][back]
    total = jnp.zeros(out_ref.shape, F32)
    for back in range(num_layer):
        for piece in range(num_col):
            if blocks.paired:
                left = blocks.matrix(piece * 4 + back)
                start = pl.multiple_of((blocks.col ^ piece) * LANES, LANES)
            else:
                source = lax.rem(blocks.layer - back + num_layer, num_layer)
                left = blocks.slab(source, piece)
                start = piece * LANES
            right = slab[back, pl.ds(start, LANES), :]
            total += lax.dot_general(left, right, TN, preferred_element_type=F32)
    out_ref[...] = total.astype(BF16)


def multiply(arrays, parts, num_row, num_col, num_layer):
    return pl.pallas_call(
        functools.partial(product_kernel, num_row, num_col, num_layer, len(arrays)),
        out_shape=(
            jax.ShapeDtypeStruct((arrays[0].shape[-1], LANES), BF16),
            jax.ShapeDtypeStruct((8, LANES), F32),
        ),
        in_specs=[VMEM] * (num_row + len(arrays)),
        out_specs=(VMEM, VMEM),
        scratch_shapes=[pltpu.VMEM((num_layer, num_col * LANES, LANES), BF16)],
        compiler_params=PARAMS,
        cost_estimate=pl.CostEstimate(flops=500_000_000, bytes_accessed=1_000_000, transcendentals=0),
        name="multiply",
    )(*arrays, *parts)


def stack_kernel(rows, own_ref, near_ref, far_ref, both_ref, out_ref):
    out_ref[0] = own_ref[...]
    out_ref[1] = near_ref[BASE:, 0:LANES]
    out_ref[2] = far_ref[BASE:, 0:LANES]
    out_ref[3] = both_ref[BASE:, LANES:UNIT]


def stack(own, near, far, both):
    rows = own.shape[0]
    return pl.pallas_call(
        functools.partial(stack_kernel, rows),
        out_shape=jax.ShapeDtypeStruct((4, rows, LANES), BF16),
        in_specs=[VMEM] * 4,
        out_specs=VMEM,
        compiler_params=PARAMS,
        name="stack",
    )(own, near, far, both)


def fold_kernel(core_ref, below_ref, above_ref, after_ref, out_ref):
    out_ref[0:HALO, :] = core_ref[0:HALO, :] + below_ref[...]
    out_ref[HALO : CORE - HALO, :] = core_ref[HALO : CORE - HALO, :]
    out_ref[CORE - HALO : CORE, :] = core_ref[CORE - HALO : CORE, :] + above_ref[...]


def fold(core, below, above, after):
    return pl.pallas_call(
        fold_kernel,
        out_shape=jax.ShapeDtypeStruct((CORE, GZ), F32),
        in_specs=[VMEM] * 4,
        out_specs=VMEM,
        compiler_params=PARAMS,
        cost_estimate=pl.CostEstimate(flops=1_000_000, bytes_accessed=400_000, transcendentals=0),
        name="fold",
    )(core, below, above, after)


def shifted(value, axis, count, step):
    return lax.ppermute(value, axis, [(i, (i + step) % count) for i in range(count)])


def crossed(value, col_bit, layer_bits):
    pairs = [(c * 4 + l, (c ^ col_bit) * 4 + (l ^ layer_bits)) for c in range(2) for l in range(4)]
    return lax.ppermute(value, ("col", "layer"), pairs)


def gather_paired(base, tall_y, tall_core):
    got_x = crossed(base, 1, 0)
    got_y = crossed(tall_y, 0, 2)
    got_xy = crossed(base, 1, 2)
    near = crossed(tall_core, 0, 1)
    near_x = crossed(got_x, 0, 1)
    near_y = crossed(got_y, 0, 1)
    near_xy = crossed(got_xy, 0, 1)
    return [base, near, got_y, near_y, got_x, near_x, got_xy, near_xy]


def on_device(p_slabs, p_mask, h_slabs, h_mask, gauss_row, gauss_col, gauss_cell, gauss_expo, gauss_pref):
    num_row, num_col, num_layer = (lax.axis_size(axis) for axis in ("row", "col", "layer"))
    paired = num_col == 2 and num_layer == 4
    flat = [x.reshape(8, LANES) for x in (gauss_row, gauss_col, gauss_cell, gauss_expo, gauss_pref)]
    made = prepare(paired, p_slabs[0], p_mask[0].T, h_slabs[0], h_mask[0], *flat)
    if paired:
        base, tall_y, tall_core, own = made
        arrays = gather_paired(base, tall_y, tall_core)
        mine = stack(own, arrays[1], arrays[2], arrays[3])
    else:
        base, pieces = made
        arrays = [lax.all_gather(base, ("layer", "col"), axis=0)]
        mine = [pieces[0]] + [shifted(pieces[step], "layer", num_layer, step) for step in range(1, num_layer)]
        mine = jnp.stack(mine)
    parts = [mine] + [
        lax.ppermute(mine, "row", [(i, i ^ step) for i in range(num_row)]) for step in range(1, num_row)
    ]
    coef, long = weigh_all(arrays, num_col, num_layer)
    core, low, high = collocate(arrays, coef, long, num_col, num_layer)
    below = shifted(high, "row", num_row, 1)
    above = shifted(low, "row", num_row, num_row - 1)
    product, token = multiply(arrays, parts, num_row, num_col, num_layer)
    density = fold(core, below, above, token).reshape(GX, GY, GZ)
    return (product, density)


def solution(mesh):
    placed = (P("layer", "row", "col"),) * 4 + (P(("row", "col", "layer")),) * 5
    return jax.shard_map(
        on_device,
        mesh=mesh,
        in_specs=placed,
        out_specs=(P("row", ("col", "layer")), P("row", "col", "layer")),
        check_vma=False,
    )
```

```python
import functools

import jax
import jax.numpy as jnp
from jax import lax
from jax.experimental import pallas as pl
from jax.experimental.pallas import tpu as pltpu
from jax.sharding import PartitionSpec as P

BS = 32
GX = 16
GY = 16
GZ = 128
R = 4
LANES = 128
F32 = jnp.float32
BF16 = jnp.bfloat16
HALO = R * GY
CORE = GX * GY
FULL = CORE + 2 * HALO
UNIT = 2 * LANES
PAIRS = 4
META = (PAIRS + 1) * 16
BASE = LANES + META
FLAG = 12
VMEM = pl.BlockSpec(memory_space=pltpu.VMEM)
HBM = pl.BlockSpec(memory_space=pltpu.HBM)
PARAMS = pltpu.CompilerParams(vmem_limit_bytes=40 * 1024 * 1024)
NT = (((1,), (1,)), ((), ()))
TN = (((0,), (0,)), ((), ()))


def iota(shape, axis):
    return lax.broadcasted_iota(jnp.int32, shape, axis).astype(F32)


def split3(value):
    first = value.astype(BF16).astype(F32)
    rest = value - first
    second = rest.astype(BF16).astype(F32)
    return first, second, rest - second


def masked(values, bits):
    lane = lax.broadcasted_iota(jnp.int32, values.shape, 1) // BS
    keep = jnp.zeros(values.shape, jnp.int32)
    for piece, bit in enumerate(bits):
        keep = jnp.where(lane == piece, bit, keep)
    return jnp.where(keep > 0, values.astype(F32), 0.0)


def ranks(flags):
    up = (iota((LANES, LANES), 0) <= iota((LANES, LANES), 1)).astype(F32).astype(BF16)
    ones = jnp.ones((LANES, LANES), BF16)
    within = jnp.dot(flags.astype(BF16), up, preferred_element_type=F32)
    totals = jnp.dot(flags.astype(BF16), ones, preferred_element_type=F32)
    row, other = iota((16, 16), 0), iota((16, 16), 1)
    same = (row < 8) == (other < 8)
    before = jnp.where(same & (other < row), 1.0, 0.0).astype(BF16)
    every = jnp.where(same, 1.0, 0.0).astype(BF16)
    earlier = jnp.dot(before, totals.astype(BF16), preferred_element_type=F32)
    count = jnp.dot(every, totals.astype(BF16), preferred_element_type=F32)
    return jnp.where(flags > 0, within + earlier - 1.0, -1.0), count


def prepare_kernel(*refs):
    sources, outs, refs = refs[:9], refs[9:-14], refs[-14:]
    landed, (tmp, fields, matrix, onehot, sems) = refs[:9], refs[9:]
    copies = [pltpu.make_async_copy(src, dst, sems.at[at]) for at, (src, dst) in enumerate(zip(sources, landed))]
    for copy in copies:
        copy.start()
    for copy in copies:
        copy.wait()
    p_ref, pm_ref, h_ref, hm_ref, row_ref, col_ref, cell_ref, expo_ref, pref_ref = landed
    band = p_ref.shape[0]
    for block in range(band // BS):
        rows = pl.ds(block * BS, BS)
        tmp[rows, :] = masked(p_ref[rows, :], [pm_ref[piece, block] for piece in range(LANES // BS)])
    turned = tmp[...].T.astype(BF16)
    col = col_ref[...]
    cell = cell_ref[...]
    cell_z = (cell % GZ).astype(F32)
    values = [
        row_ref[...].astype(F32),
        (col // LANES).astype(F32),
        (col % LANES).astype(F32),
        (cell // (GY * GZ)).astype(F32),
        (cell // GZ % GY).astype(F32),
        cell_z,
        *split3(expo_ref[...]),
        *split3(pref_ref[...]),
    ]
    for index in range(16):
        fields[8 * index : 8 * index + 8, :] = values[index] if index < len(values) else jnp.zeros((8, LANES), F32)
    tiles = [fields[pl.ds(part, 16, stride=8), :].astype(BF16) for part in range(2 * PAIRS)]
    for part in range(2 * PAIRS):
        matrix[:, part * LANES : part * LANES + LANES] = tiles[part]
    faces = jnp.concatenate([jnp.where(cell_z < R, 1.0, 0.0), jnp.where(cell_z >= GZ - R, 1.0, 0.0)], axis=0)
    place, many = ranks(faces)
    slot = iota((LANES, LANES), 0)
    for part in range(2 * PAIRS):
        lanes = pl.ds(part * LANES, LANES)
        for face in range(2):
            hit = slot == place[face * 8 + part : face * 8 + part + 1, :]
            onehot[face * LANES : face * LANES + LANES, lanes] = jnp.where(hit, 1.0, 0.0).astype(BF16)
    listed = lax.dot_general(matrix[...], onehot[...], NT, preferred_element_type=F32)
    over = jnp.where(jnp.max(many, axis=0, keepdims=True) > LANES, 1.0, 0.0)
    over = jnp.concatenate([over, over], axis=1)
    listed = jnp.where(iota(listed.shape, 0) == FLAG, over, listed).astype(BF16)
    out, tile_ref = outs
    out[0:LANES, :] = turned
    for pair in range(PAIRS):
        out[LANES + 16 * pair : LANES + 16 * pair + 16, :] = matrix[:, pair * UNIT : pair * UNIT + UNIT]
    out[LANES + 16 * PAIRS : BASE, :] = listed
    pieces = LANES // BS
    for chunk in range(h_ref.shape[1] // LANES):
        cols = pl.ds(chunk * LANES, LANES)
        for block in range(h_ref.shape[0] // BS):
            rows = pl.ds(block * BS, BS)
            bits = [hm_ref[block, chunk * pieces + at] for at in range(pieces)]
            tile_ref[rows, cols] = masked(h_ref[rows, cols], bits).astype(BF16)


def prepare(p, p_mask, h, h_mask, *gauss):
    outs = (jax.ShapeDtypeStruct((BASE, p.shape[0]), BF16), jax.ShapeDtypeStruct(h.shape, BF16))
    return pl.pallas_call(
        prepare_kernel,
        out_shape=outs,
        in_specs=[HBM] * 9,
        out_specs=(VMEM,) * len(outs),
        scratch_shapes=[
            pltpu.VMEM(p.shape, p.dtype),
            pltpu.SMEM(p_mask.shape, p_mask.dtype),
            pltpu.VMEM(h.shape, h.dtype),
            pltpu.SMEM(h_mask.shape, h_mask.dtype),
            *[pltpu.VMEM(x.shape, x.dtype) for x in gauss],
            pltpu.VMEM(p.shape, F32),
            pltpu.VMEM((16 * 8, LANES), F32),
            pltpu.VMEM((16, 2 * PAIRS * LANES), BF16),
            pltpu.VMEM((UNIT, 2 * PAIRS * LANES), BF16),
            pltpu.SemaphoreType.DMA((9,)),
        ],
        compiler_params=pltpu.CompilerParams(vmem_limit_bytes=62 * 1024 * 1024),
        name="prepare",
    )(p, p_mask, h, h_mask, *gauss)


class Blocks:
    def __init__(self, refs, num_col, num_layer):
        self.refs = refs
        self.num_col, self.num_layer = num_col, num_layer
        self.paired = len(refs) > 1
        self.col, self.layer = lax.axis_index("col"), lax.axis_index("layer")
        self.total = num_col * num_layer
        self.col_shifts = [0, 1] if num_col == 2 else [0, -1, 1]

    def ident(self, index):
        if not self.paired:
            return index
        return (self.layer ^ (index % 4)) * 2 + (self.col ^ (index // 4))

    def matrix(self, index):
        return self.refs[index][0:LANES, :] if self.paired else self.refs[0][index, 0:LANES, :]

    def slab(self, layer, piece):
        index = layer * self.num_col + piece
        return self.refs[0][index, 0:LANES, :]

    def tile(self, which, side, pair):
        rows = pl.ds(LANES + 16 * pair, 16)
        if self.paired:
            return self.refs[which * 4 + side][rows, :].astype(F32)
        shift_l = 0 if side == 0 else (1 if side == 1 else -1)
        index = lax.rem(self.layer + shift_l + self.num_layer, self.num_layer) * self.num_col
        index += lax.rem(self.col + self.col_shifts[which] + self.num_col, self.num_col)
        return self.refs[0][index, rows, :].astype(F32)

    def side_shift(self, side):
        if self.paired:
            even = (self.layer % 2) == 0
            return jnp.where(even, 1.0, -1.0) if side == 1 else jnp.where(even, -1.0, 1.0)
        return 1.0 if side == 1 else -1.0

    def sides(self):
        return (1, 3) if self.paired else (1, 2)

    def units(self):
        return [(which, pair) for which in range(len(self.col_shifts)) for pair in range(PAIRS + 1)]

    def listed(self, which):
        halves = []
        for side in self.sides():
            both = self.tile(which, side, PAIRS)
            upward = self.side_shift(side) > 0
            halves.append(jnp.where(upward, both[:, 0:LANES], both[:, LANES:UNIT]))
        return jnp.concatenate(halves, axis=1)

    def unit(self, which, pair):
        return self.tile(which, 0, pair) if pair < PAIRS else self.listed(which)

    def lifts(self, pair):
        if pair < PAIRS:
            return 0.0
        lane = iota((1, UNIT), 1)
        first, second = self.sides()
        return jnp.where(lane < LANES, self.side_shift(first), self.side_shift(second)) * float(GZ)

    def over(self):
        flags = [
            self.tile(which, side, PAIRS)[FLAG : FLAG + 1, :]
            for which in range(len(self.col_shifts))
            for side in self.sides()
        ]
        return functools.reduce(jnp.maximum, flags)

    def long_steps(self):
        return [(which, side) for which in range(len(self.col_shifts)) for side in self.sides()]


def weigh(blocks, whole, tile):
    band = whole.shape[1]
    onehot = jnp.where(iota((band, UNIT), 0) == tile[0:1, :], 1.0, 0.0).astype(BF16)
    found = jnp.dot(whole[...], onehot, preferred_element_type=F32)
    picked = jnp.zeros((LANES, UNIT), F32)
    for index in range(blocks.total):
        mine = tile[1:2, :] == jnp.asarray(blocks.ident(index)).astype(F32)
        picked = jnp.where(mine, found[index * LANES : index * LANES + LANES, :], picked)
    value = jnp.sum(jnp.where(iota((LANES, UNIT), 0) == tile[2:3, :], picked, 0.0), axis=0, keepdims=True)
    return (tile[9:10, :] + tile[10:11, :] + tile[11:12, :]) * value


def bell(dist, expo):
    square = dist * dist
    return jnp.where(square < (R + 0.5) ** 2, jnp.exp(-expo * square), 0.0)


RIM_X = tuple(range(R)) + tuple(range(GX + R, GX + 2 * R))
CORE_X = tuple(range(R, GX + R))
ALL_X = tuple(range(GX + 2 * R))


def decay(tile):
    return tile[6:7, :] + tile[7:8, :] + tile[8:9, :]


def set_planes(blocks, tile, which, places, at, planeh, planel):
    expo = decay(tile)
    ex = bell(iota((GX + 2 * R, UNIT), 0) - float(R) - tile[3:4, :], expo)
    dy = iota((GY, UNIT), 0) - tile[4:5, :] - float(blocks.col_shifts[which] * GY)
    if blocks.num_col == 2 and which == 1:
        dy = jnp.where(dy < -float(GY), dy + 2.0 * GY, dy)
    ey = bell(dy, expo)
    lanes = pl.ds(at * UNIT, UNIT)
    for spot, x in enumerate(places):
        plane = ex[x : x + 1, :] * ey
        plane_hi = plane.astype(BF16)
        planeh[spot * GY : spot * GY + GY, lanes] = plane_hi
        planel[spot * GY : spot * GY + GY, lanes] = (plane - plane_hi.astype(F32)).astype(BF16)


def set_depth(tile, lift, coef, at, depth):
    ez = bell(iota((GZ, UNIT), 0) - tile[5:6, :] - lift, decay(tile)) * coef
    lanes = pl.ds(at * UNIT, UNIT)
    ez_hi = ez.astype(BF16)
    depth[0:GZ, lanes] = ez_hi
    depth[GZ : 2 * GZ, lanes] = (ez - ez_hi.astype(F32)).astype(BF16)


def summed(planeh, planel, depth):
    first = lax.dot_general(planeh, depth, NT, preferred_element_type=F32)
    second = lax.dot_general(planel, depth[0:GZ, :], NT, preferred_element_type=F32)
    return first[:, 0:GZ] + first[:, GZ : 2 * GZ] + second


def rims_kernel(num_col, num_layer, refs_in, *refs):
    blocks = Blocks(refs[:refs_in], num_col, num_layer)
    low_ref, high_ref, depth, extra, whole, planeh, planel, longh, longl, long_depth, acc = refs[refs_in:]
    for index in range(blocks.total):
        whole[index * LANES : index * LANES + LANES, :] = blocks.matrix(index)
    over = blocks.over()
    for at, (which, pair) in enumerate(blocks.units()):
        tile = blocks.unit(which, pair)
        set_planes(blocks, tile, which, RIM_X, at, planeh, planel)
        coef = weigh(blocks, whole, tile)
        if pair == PAIRS:
            coef = jnp.where(over > 0, 0.0, coef)
        set_depth(tile, blocks.lifts(pair), coef, at, depth)
    total = summed(planeh[...], planel[...], depth[...])
    low_ref[...] = total[0:HALO, :]
    high_ref[...] = total[HALO:, :]

    @pl.when(jnp.max(over) > 0)
    def _():
        acc[...] = jnp.zeros_like(acc)
        for which, side in blocks.long_steps():

            def step(pair, carry):
                tile = blocks.tile(which, side, pair)
                lift = blocks.side_shift(side) * float(GZ)
                set_planes(blocks, tile, which, ALL_X, 0, longh, longl)
                set_depth(tile, lift, weigh(blocks, whole, tile), 0, long_depth)
                acc[...] += summed(longh[...], longl[...], long_depth[...])
                return carry

            lax.fori_loop(0, PAIRS, step, 0)
        low_ref[...] += acc[0:HALO, :]
        extra[...] = acc[HALO : HALO + CORE, :]
        high_ref[...] += acc[HALO + CORE : FULL, :]


def rims(arrays, num_col, num_layer):
    gaussians = (2 if num_col == 2 else 3) * (PAIRS + 1) * UNIT
    return pl.pallas_call(
        functools.partial(rims_kernel, num_col, num_layer, len(arrays)),
        out_shape=(
            jax.ShapeDtypeStruct((HALO, GZ), F32),
            jax.ShapeDtypeStruct((HALO, GZ), F32),
            jax.ShapeDtypeStruct((2 * GZ, gaussians), BF16),
            jax.ShapeDtypeStruct((CORE, GZ), F32),
        ),
        in_specs=[VMEM] * len(arrays),
        out_specs=(VMEM,) * 4,
        scratch_shapes=[
            pltpu.VMEM((num_col * num_layer * LANES, arrays[0].shape[-1]), BF16),
            pltpu.VMEM((2 * HALO, gaussians), BF16),
            pltpu.VMEM((2 * HALO, gaussians), BF16),
            pltpu.VMEM((FULL, UNIT), BF16),
            pltpu.VMEM((FULL, UNIT), BF16),
            pltpu.VMEM((2 * GZ, UNIT), BF16),
            pltpu.VMEM((FULL, GZ), F32),
        ],
        compiler_params=PARAMS,
        cost_estimate=pl.CostEstimate(flops=3_000_000_000, bytes_accessed=1_000_000, transcendentals=0),
        name="rims",
    )(*arrays)


def core_kernel(num_col, num_layer, refs_in, *refs):
    blocks = Blocks(refs[:refs_in], num_col, num_layer)
    depth, extra, core_ref, planeh, planel = refs[refs_in:]
    for at, (which, pair) in enumerate(blocks.units()):
        set_planes(blocks, blocks.unit(which, pair), which, CORE_X, at, planeh, planel)
    core_ref[...] = summed(planeh[...], planel[...], depth[...])

    @pl.when(jnp.max(blocks.over()) > 0)
    def _():
        core_ref[...] += extra[...]


def core_part(arrays, depth, extra, num_col, num_layer):
    gaussians = depth.shape[1]
    return pl.pallas_call(
        functools.partial(core_kernel, num_col, num_layer, len(arrays)),
        out_shape=jax.ShapeDtypeStruct((CORE, GZ), F32),
        in_specs=[VMEM] * (len(arrays) + 2),
        out_specs=VMEM,
        scratch_shapes=[pltpu.VMEM((CORE, gaussians), BF16), pltpu.VMEM((CORE, gaussians), BF16)],
        compiler_params=PARAMS,
        cost_estimate=pl.CostEstimate(flops=1_500_000_000, bytes_accessed=1_000_000, transcendentals=0),
        name="core",
    )(*arrays, depth, extra)


def cut_kernel(paired, num_row, own_hbm, *refs):
    tiles, outs, (own, sem) = refs[: num_row - 1], refs[num_row:-2], refs[-2:]
    copy = pltpu.make_async_copy(own_hbm, own, sem)
    copy.start()
    row, layer = lax.axis_index("row"), lax.axis_index("layer")
    count = lax.axis_size("layer")
    rows = own.shape[0]

    def place(tile, step):
        start = pl.multiple_of((row ^ step) * rows, rows)
        for back in range(count):
            chunk = (layer ^ back) if paired else lax.rem(layer + back, count)
            value = tile[:, pl.ds(pl.multiple_of(chunk * LANES, LANES), LANES)]
            if paired and back >= 2:
                outs[2][back - 2, pl.ds(start, rows), :] = value
            else:
                outs[back][pl.ds(start, rows), :] = value

    for step in range(1, num_row):
        place(tiles[step - 1], step)
    copy.wait()
    place(own, 0)


def cut(paired, own, tiles, after, num_layer):
    num_row = len(tiles) + 1
    piece = jax.ShapeDtypeStruct((num_row * own.shape[0], LANES), BF16)
    both = jax.ShapeDtypeStruct((2, num_row * own.shape[0], LANES), BF16)
    outs = (piece, piece, both) if paired else (piece,) * num_layer
    return pl.pallas_call(
        functools.partial(cut_kernel, paired, num_row),
        out_shape=outs,
        in_specs=[HBM] + [VMEM] * num_row,
        out_specs=(VMEM,) * len(outs),
        scratch_shapes=[pltpu.VMEM(own.shape, BF16), pltpu.SemaphoreType.DMA(())],
        compiler_params=PARAMS,
        cost_estimate=pl.CostEstimate(flops=100_000_000, bytes_accessed=500_000, transcendentals=0),
        name="cut",
    )(own, *tiles, after)


def product_kernel(num_col, num_layer, refs_in, *refs):
    blocks = Blocks(refs[:refs_in], num_col, num_layer)
    slabs = refs[refs_in:-2]
    out_ref, token_ref = refs[-2:]
    token_ref[...] = jnp.zeros_like(token_ref)
    total = jnp.zeros(out_ref.shape, F32)
    for back in range(num_layer):
        for piece in range(num_col):
            if blocks.paired:
                left = blocks.matrix(piece * 4 + back)
                start = pl.multiple_of((blocks.col ^ piece) * LANES, LANES)
                right = slabs[back][pl.ds(start, LANES), :] if back < 2 else slabs[back][back - 2, pl.ds(start, LANES), :]
            else:
                source = lax.rem(blocks.layer - back + num_layer, num_layer)
                left = blocks.slab(source, piece)
                right = slabs[back][piece * LANES : piece * LANES + LANES, :]
            total += lax.dot_general(left, right, TN, preferred_element_type=F32)
    out_ref[...] = total.astype(BF16)


def multiply(arrays, slabs, num_col, num_layer):
    return pl.pallas_call(
        functools.partial(product_kernel, num_col, num_layer, len(arrays)),
        out_shape=(
            jax.ShapeDtypeStruct((arrays[0].shape[-1], LANES), BF16),
            jax.ShapeDtypeStruct((8, LANES), F32),
        ),
        in_specs=[VMEM] * (num_layer + len(arrays)),
        out_specs=(VMEM, VMEM),
        compiler_params=PARAMS,
        cost_estimate=pl.CostEstimate(flops=500_000_000, bytes_accessed=1_000_000, transcendentals=0),
        name="multiply",
    )(*arrays, *slabs)


def fold_kernel(core_ref, below_ref, above_ref, after_ref, out_ref):
    out_ref[0:HALO, :] = core_ref[0:HALO, :] + below_ref[...]
    out_ref[HALO : CORE - HALO, :] = core_ref[HALO : CORE - HALO, :]
    out_ref[CORE - HALO : CORE, :] = core_ref[CORE - HALO : CORE, :] + above_ref[...]


def fold(core, below, above, after):
    return pl.pallas_call(
        fold_kernel,
        out_shape=jax.ShapeDtypeStruct((CORE, GZ), F32),
        in_specs=[VMEM] * 4,
        out_specs=VMEM,
        compiler_params=PARAMS,
        cost_estimate=pl.CostEstimate(flops=1_000_000, bytes_accessed=400_000, transcendentals=0),
        name="fold",
    )(core, below, above, after)


def shifted(value, axis, count, step):
    return lax.ppermute(value, axis, [(i, (i + step) % count) for i in range(count)])


def crossed(value, col_bit, layer_bits):
    pairs = [(c * 4 + l, (c ^ col_bit) * 4 + (l ^ layer_bits)) for c in range(2) for l in range(4)]
    return lax.ppermute(value, ("col", "layer"), pairs)


def gather_paired(base):
    got_x = crossed(base, 1, 0)
    got_y = crossed(base, 0, 2)
    got_xy = crossed(base, 1, 2)
    near = crossed(base, 0, 1)
    near_x = crossed(got_x, 0, 1)
    near_y = crossed(got_y, 0, 1)
    near_xy = crossed(got_xy, 0, 1)
    return [base, near, got_y, near_y, got_x, near_x, got_xy, near_xy]


def on_device(p_slabs, p_mask, h_slabs, h_mask, gauss_row, gauss_col, gauss_cell, gauss_expo, gauss_pref):
    num_row, num_col, num_layer = (lax.axis_size(axis) for axis in ("row", "col", "layer"))
    paired = num_col == 2 and num_layer == 4
    flat = [x.reshape(8, LANES) for x in (gauss_row, gauss_col, gauss_cell, gauss_expo, gauss_pref)]
    base, tile = prepare(p_slabs[0], p_mask[0].T, h_slabs[0], h_mask[0], *flat)
    arrays = gather_paired(base) if paired else [lax.all_gather(base, ("layer", "col"), axis=0)]
    tiles = [lax.ppermute(tile, "row", [(i, i ^ step) for i in range(num_row)]) for step in range(1, num_row)]
    low, high, depth, extra = rims(arrays, num_col, num_layer)
    parts = cut(paired, tile, tiles, low, num_layer)
    if paired:
        far = crossed(parts[2], 0, 2)
        slabs = [parts[0], crossed(parts[1], 0, 1), far, crossed(far, 0, 1)]
    else:
        slabs = [parts[0]] + [shifted(parts[step], "layer", num_layer, step) for step in range(1, num_layer)]
    below = shifted(high, "row", num_row, 1)
    above = shifted(low, "row", num_row, num_row - 1)
    core = core_part(arrays, depth, extra, num_col, num_layer)
    product, token = multiply(arrays, slabs, num_col, num_layer)
    density = fold(core, below, above, token).reshape(GX, GY, GZ)
    return (product, density)


def solution(mesh):
    placed = (P("layer", "row", "col"),) * 4 + (P(("row", "col", "layer")),) * 5
    return jax.shard_map(
        on_device,
        mesh=mesh,
        in_specs=placed,
        out_specs=(P("row", ("col", "layer")), P("row", "col", "layer")),
        check_vma=False,
    )
```

```python
import functools

import jax
import jax.numpy as jnp
from jax import lax
from jax.experimental import pallas as pl
from jax.experimental.pallas import tpu as pltpu
from jax.sharding import PartitionSpec as P

BS = 32
GX = 16
GY = 16
GZ = 128
R = 4
LANES = 128
F32 = jnp.float32
BF16 = jnp.bfloat16
HALO = R * GY
CORE = GX * GY
FULL = CORE + 2 * HALO
UNIT = 2 * LANES
PAIRS = 4
META = (PAIRS + 1) * 16
BASE = LANES + META
FLAG = 12
VMEM = pl.BlockSpec(memory_space=pltpu.VMEM)
HBM = pl.BlockSpec(memory_space=pltpu.HBM)
PARAMS = pltpu.CompilerParams(vmem_limit_bytes=40 * 1024 * 1024)
NT = (((1,), (1,)), ((), ()))
TN = (((0,), (0,)), ((), ()))


def iota(shape, axis):
    return lax.broadcasted_iota(jnp.int32, shape, axis).astype(F32)


def split3(value):
    first = value.astype(BF16).astype(F32)
    rest = value - first
    second = rest.astype(BF16).astype(F32)
    return first, second, rest - second


def masked(values, bits):
    lane = lax.broadcasted_iota(jnp.int32, values.shape, 1) // BS
    keep = jnp.zeros(values.shape, jnp.int32)
    for piece, bit in enumerate(bits):
        keep = jnp.where(lane == piece, bit, keep)
    return jnp.where(keep > 0, values.astype(F32), 0.0)


def ranks(flags):
    up = (iota((LANES, LANES), 0) <= iota((LANES, LANES), 1)).astype(F32).astype(BF16)
    ones = jnp.ones((LANES, LANES), BF16)
    within = jnp.dot(flags.astype(BF16), up, preferred_element_type=F32)
    totals = jnp.dot(flags.astype(BF16), ones, preferred_element_type=F32)
    row, other = iota((16, 16), 0), iota((16, 16), 1)
    same = (row < 8) == (other < 8)
    before = jnp.where(same & (other < row), 1.0, 0.0).astype(BF16)
    every = jnp.where(same, 1.0, 0.0).astype(BF16)
    earlier = jnp.dot(before, totals.astype(BF16), preferred_element_type=F32)
    count = jnp.dot(every, totals.astype(BF16), preferred_element_type=F32)
    return jnp.where(flags > 0, within + earlier - 1.0, -1.0), count


def h_piece(h_ref, hm_ref, chunk):
    pieces = LANES // BS
    out = []
    for block in range(h_ref.shape[0] // BS):
        bits = [hm_ref[block, chunk * pieces + at] for at in range(pieces)]
        value = h_ref[pl.ds(block * BS, BS), pl.ds(pl.multiple_of(chunk * LANES, LANES), LANES)]
        out.append(masked(value, bits).astype(BF16))
    return jnp.concatenate(out, axis=0)


def prepare_kernel(paired, *refs):
    sources, outs, refs = refs[:9], refs[9:-14], refs[-14:]
    landed, (tmp, fields, matrix, onehot, sems) = refs[:9], refs[9:]
    copies = [pltpu.make_async_copy(src, dst, sems.at[at]) for at, (src, dst) in enumerate(zip(sources, landed))]
    for copy in copies:
        copy.start()
    for copy in copies:
        copy.wait()
    p_ref, pm_ref, h_ref, hm_ref, row_ref, col_ref, cell_ref, expo_ref, pref_ref = landed
    layer = lax.axis_index("layer")
    count = lax.axis_size("layer")
    band = p_ref.shape[0]
    for block in range(band // BS):
        rows = pl.ds(block * BS, BS)
        tmp[rows, :] = masked(p_ref[rows, :], [pm_ref[piece, block] for piece in range(LANES // BS)])
    turned = tmp[...].T.astype(BF16)
    col = col_ref[...]
    cell = cell_ref[...]
    cell_z = (cell % GZ).astype(F32)
    values = [
        row_ref[...].astype(F32),
        (col // LANES).astype(F32),
        (col % LANES).astype(F32),
        (cell // (GY * GZ)).astype(F32),
        (cell // GZ % GY).astype(F32),
        cell_z,
        *split3(expo_ref[...]),
        *split3(pref_ref[...]),
    ]
    for index in range(16):
        fields[8 * index : 8 * index + 8, :] = values[index] if index < len(values) else jnp.zeros((8, LANES), F32)
    tiles = [fields[pl.ds(part, 16, stride=8), :].astype(BF16) for part in range(2 * PAIRS)]
    for part in range(2 * PAIRS):
        matrix[:, part * LANES : part * LANES + LANES] = tiles[part]
    faces = jnp.concatenate([jnp.where(cell_z < R, 1.0, 0.0), jnp.where(cell_z >= GZ - R, 1.0, 0.0)], axis=0)
    place, many = ranks(faces)
    slot = iota((LANES, LANES), 0)
    for part in range(2 * PAIRS):
        lanes = pl.ds(part * LANES, LANES)
        for face in range(2):
            hit = slot == place[face * 8 + part : face * 8 + part + 1, :]
            onehot[face * LANES : face * LANES + LANES, lanes] = jnp.where(hit, 1.0, 0.0).astype(BF16)
    listed = lax.dot_general(matrix[...], onehot[...], NT, preferred_element_type=F32)
    over = jnp.where(jnp.max(many, axis=0, keepdims=True) > LANES, 1.0, 0.0)
    over = jnp.concatenate([over, over], axis=1)
    listed = jnp.where(iota(listed.shape, 0) == FLAG, over, listed).astype(BF16)
    copies = outs[:3] if paired else outs[:1]
    for out in copies:
        out[0:LANES, :] = turned
        for pair in range(PAIRS):
            out[LANES + 16 * pair : LANES + 16 * pair + 16, :] = matrix[:, pair * UNIT : pair * UNIT + UNIT]
        out[LANES + 16 * PAIRS : BASE, :] = listed

    def piece(chunk):
        return h_piece(h_ref, hm_ref, chunk)

    if paired:
        outs[1][BASE:, 0:LANES] = piece(layer ^ 2)
        outs[1][BASE:, LANES:UNIT] = piece(layer ^ 3)
        outs[2][BASE:, 0:LANES] = piece(layer ^ 1)
        outs[2][BASE:, LANES:UNIT] = piece(layer)
    else:
        for back in range(h_ref.shape[1] // LANES):
            outs[1][back] = piece(lax.rem(layer + back, count))


def prepare(paired, p, p_mask, h, h_mask, *gauss):
    band = p.shape[0]
    base = jax.ShapeDtypeStruct((BASE, band), BF16)
    tall = jax.ShapeDtypeStruct((BASE + h.shape[0], band), BF16)
    if paired:
        outs = (base, tall, tall)
    else:
        outs = (base, jax.ShapeDtypeStruct((h.shape[1] // LANES, h.shape[0], LANES), BF16))
    return pl.pallas_call(
        functools.partial(prepare_kernel, paired),
        out_shape=outs,
        in_specs=[HBM] * 9,
        out_specs=(VMEM,) * len(outs),
        scratch_shapes=[
            pltpu.VMEM(p.shape, p.dtype),
            pltpu.SMEM(p_mask.shape, p_mask.dtype),
            pltpu.VMEM(h.shape, h.dtype),
            pltpu.SMEM(h_mask.shape, h_mask.dtype),
            *[pltpu.VMEM(x.shape, x.dtype) for x in gauss],
            pltpu.VMEM(p.shape, F32),
            pltpu.VMEM((16 * 8, LANES), F32),
            pltpu.VMEM((16, 2 * PAIRS * LANES), BF16),
            pltpu.VMEM((UNIT, 2 * PAIRS * LANES), BF16),
            pltpu.SemaphoreType.DMA((9,)),
        ],
        compiler_params=pltpu.CompilerParams(vmem_limit_bytes=62 * 1024 * 1024),
        name="prepare",
    )(p, p_mask, h, h_mask, *gauss)


class Blocks:
    def __init__(self, refs, num_col, num_layer):
        self.refs = refs
        self.num_col, self.num_layer = num_col, num_layer
        self.paired = len(refs) > 1
        self.col, self.layer = lax.axis_index("col"), lax.axis_index("layer")
        self.total = num_col * num_layer
        self.col_shifts = [0, 1] if num_col == 2 else [0, -1, 1]

    def ident(self, index):
        if not self.paired:
            return index
        return (self.layer ^ (index % 4)) * 2 + (self.col ^ (index // 4))

    def matrix(self, index):
        return self.refs[index][0:LANES, :] if self.paired else self.refs[0][index, 0:LANES, :]

    def slab(self, layer, piece):
        index = layer * self.num_col + piece
        return self.refs[0][index, 0:LANES, :]

    def tile(self, which, side, pair):
        rows = pl.ds(LANES + 16 * pair, 16)
        if self.paired:
            return self.refs[which * 4 + side][rows, :].astype(F32)
        shift_l = 0 if side == 0 else (1 if side == 1 else -1)
        index = lax.rem(self.layer + shift_l + self.num_layer, self.num_layer) * self.num_col
        index += lax.rem(self.col + self.col_shifts[which] + self.num_col, self.num_col)
        return self.refs[0][index, rows, :].astype(F32)

    def side_shift(self, side):
        if self.paired:
            even = (self.layer % 2) == 0
            return jnp.where(even, 1.0, -1.0) if side == 1 else jnp.where(even, -1.0, 1.0)
        return 1.0 if side == 1 else -1.0

    def sides(self):
        return (1, 3) if self.paired else (1, 2)

    def units(self):
        return [(which, pair) for which in range(len(self.col_shifts)) for pair in range(PAIRS + 1)]

    def listed(self, which):
        halves = []
        for side in self.sides():
            both = self.tile(which, side, PAIRS)
            upward = self.side_shift(side) > 0
            halves.append(jnp.where(upward, both[:, 0:LANES], both[:, LANES:UNIT]))
        return jnp.concatenate(halves, axis=1)

    def unit(self, which, pair):
        return self.tile(which, 0, pair) if pair < PAIRS else self.listed(which)

    def lifts(self, pair):
        if pair < PAIRS:
            return 0.0
        lane = iota((1, UNIT), 1)
        first, second = self.sides()
        return jnp.where(lane < LANES, self.side_shift(first), self.side_shift(second)) * float(GZ)

    def over(self):
        flags = [
            self.tile(which, side, PAIRS)[FLAG : FLAG + 1, :]
            for which in range(len(self.col_shifts))
            for side in self.sides()
        ]
        return functools.reduce(jnp.maximum, flags)

    def long_steps(self):
        return [(which, side) for which in range(len(self.col_shifts)) for side in self.sides()]


def weigh(blocks, whole, tile):
    band = whole.shape[1]
    onehot = jnp.where(iota((band, UNIT), 0) == tile[0:1, :], 1.0, 0.0).astype(BF16)
    found = jnp.dot(whole[...], onehot, preferred_element_type=F32)
    picked = jnp.zeros((LANES, UNIT), F32)
    for index in range(blocks.total):
        mine = tile[1:2, :] == jnp.asarray(blocks.ident(index)).astype(F32)
        picked = jnp.where(mine, found[index * LANES : index * LANES + LANES, :], picked)
    value = jnp.sum(jnp.where(iota((LANES, UNIT), 0) == tile[2:3, :], picked, 0.0), axis=0, keepdims=True)
    return (tile[9:10, :] + tile[10:11, :] + tile[11:12, :]) * value


def bell(dist, expo):
    square = dist * dist
    return jnp.where(square < (R + 0.5) ** 2, jnp.exp(-expo * square), 0.0)


RIM_X = tuple(range(R)) + tuple(range(GX + R, GX + 2 * R))
CORE_X = tuple(range(R, GX + R))
ALL_X = tuple(range(GX + 2 * R))


def decay(tile):
    return tile[6:7, :] + tile[7:8, :] + tile[8:9, :]


def shapes_x(tile):
    return bell(iota((GX + 2 * R, UNIT), 0) - float(R) - tile[3:4, :], decay(tile))


def shapes_y(tile, shift, wraps):
    dy = iota((GY, UNIT), 0) - tile[4:5, :] - float(shift * GY)
    if wraps:
        dy = jnp.where(dy < -float(GY), dy + 2.0 * GY, dy)
    return bell(dy, decay(tile))


def shapes_z(tile, lift):
    return bell(iota((GZ, UNIT), 0) - tile[5:6, :] - lift, decay(tile))


def fill_planes(ex, ey, places, at, planeh, planel):
    lanes = pl.ds(at * UNIT, UNIT)
    for spot, x in enumerate(places):
        plane = ex[x : x + 1, :] * ey
        plane_hi = plane.astype(BF16)
        planeh[spot * GY : spot * GY + GY, lanes] = plane_hi
        planel[spot * GY : spot * GY + GY, lanes] = (plane - plane_hi.astype(F32)).astype(BF16)


def fill_depth(ez, coef, at, depth):
    weighed = ez * coef
    lanes = pl.ds(at * UNIT, UNIT)
    weighed_hi = weighed.astype(BF16)
    depth[0:GZ, lanes] = weighed_hi
    depth[GZ : 2 * GZ, lanes] = (weighed - weighed_hi.astype(F32)).astype(BF16)


def settle_kernel(block_ref, out_ref, planeh, planel, ez_ref):
    out_ref[...] = block_ref[...]
    for pair in range(PAIRS):
        tile = block_ref[LANES + 16 * pair : LANES + 16 * pair + 16, :].astype(F32)
        fill_planes(shapes_x(tile), shapes_y(tile, 0, False), ALL_X, pair, planeh, planel)
        ez_ref[:, pair * UNIT : pair * UNIT + UNIT] = shapes_z(tile, 0.0)


def settle(block):
    plane = jax.ShapeDtypeStruct((FULL, PAIRS * UNIT), BF16)
    return pl.pallas_call(
        settle_kernel,
        out_shape=(
            jax.ShapeDtypeStruct(block.shape, BF16),
            plane,
            plane,
            jax.ShapeDtypeStruct((GZ, PAIRS * UNIT), F32),
        ),
        in_specs=[VMEM],
        out_specs=(VMEM,) * 4,
        compiler_params=PARAMS,
        cost_estimate=pl.CostEstimate(flops=1_500_000_000, bytes_accessed=1_000_000, transcendentals=0),
        name="settle",
    )(block)


def set_planes(blocks, tile, which, places, at, planeh, planel):
    wraps = blocks.num_col == 2 and which == 1
    fill_planes(shapes_x(tile), shapes_y(tile, blocks.col_shifts[which], wraps), places, at, planeh, planel)


def summed(planeh, planel, depth):
    first = lax.dot_general(planeh, depth, NT, preferred_element_type=F32)
    second = lax.dot_general(planel, depth[0:GZ, :], NT, preferred_element_type=F32)
    return first[:, 0:GZ] + first[:, GZ : 2 * GZ] + second


def rims_kernel(num_col, num_layer, refs_in, *refs):
    blocks = Blocks(refs[:refs_in], num_col, num_layer)
    ownh, ownl, own_ez = refs[refs_in : refs_in + 3]
    low_ref, high_ref, depth, extra, whole, planeh, planel, longh, longl, long_depth, acc = refs[refs_in + 3 :]
    for index in range(blocks.total):
        whole[index * LANES : index * LANES + LANES, :] = blocks.matrix(index)
    over = blocks.over()
    mine = pl.ds(0, PAIRS * UNIT)
    for target, source in ((planeh, ownh), (planel, ownl)):
        target[0:HALO, mine] = source[0:HALO, :]
        target[HALO : 2 * HALO, mine] = source[HALO + CORE : FULL, :]
    for at, (which, pair) in enumerate(blocks.units()):
        tile = blocks.unit(which, pair)
        coef = weigh(blocks, whole, tile)
        if pair == PAIRS:
            coef = jnp.where(over > 0, 0.0, coef)
        if at < PAIRS:
            ez = own_ez[:, at * UNIT : at * UNIT + UNIT]
        else:
            set_planes(blocks, tile, which, RIM_X, at, planeh, planel)
            ez = shapes_z(tile, blocks.lifts(pair))
        fill_depth(ez, coef, at, depth)
    total = summed(planeh[...], planel[...], depth[...])
    low_ref[...] = total[0:HALO, :]
    high_ref[...] = total[HALO:, :]

    @pl.when(jnp.max(over) > 0)
    def _():
        acc[...] = jnp.zeros_like(acc)
        for which, side in blocks.long_steps():

            def step(pair, carry):
                tile = blocks.tile(which, side, pair)
                lift = blocks.side_shift(side) * float(GZ)
                set_planes(blocks, tile, which, ALL_X, 0, longh, longl)
                fill_depth(shapes_z(tile, lift), weigh(blocks, whole, tile), 0, long_depth)
                acc[...] += summed(longh[...], longl[...], long_depth[...])
                return carry

            lax.fori_loop(0, PAIRS, step, 0)
        low_ref[...] += acc[0:HALO, :]
        extra[...] = acc[HALO : HALO + CORE, :]
        high_ref[...] += acc[HALO + CORE : FULL, :]


def rims(arrays, shapes, num_col, num_layer):
    gaussians = (2 if num_col == 2 else 3) * (PAIRS + 1) * UNIT
    return pl.pallas_call(
        functools.partial(rims_kernel, num_col, num_layer, len(arrays)),
        out_shape=(
            jax.ShapeDtypeStruct((HALO, GZ), F32),
            jax.ShapeDtypeStruct((HALO, GZ), F32),
            jax.ShapeDtypeStruct((2 * GZ, gaussians), BF16),
            jax.ShapeDtypeStruct((CORE, GZ), F32),
        ),
        in_specs=[VMEM] * (len(arrays) + len(shapes)),
        out_specs=(VMEM,) * 4,
        scratch_shapes=[
            pltpu.VMEM((num_col * num_layer * LANES, arrays[0].shape[-1]), BF16),
            pltpu.VMEM((2 * HALO, gaussians), BF16),
            pltpu.VMEM((2 * HALO, gaussians), BF16),
            pltpu.VMEM((FULL, UNIT), BF16),
            pltpu.VMEM((FULL, UNIT), BF16),
            pltpu.VMEM((2 * GZ, UNIT), BF16),
            pltpu.VMEM((FULL, GZ), F32),
        ],
        compiler_params=PARAMS,
        cost_estimate=pl.CostEstimate(flops=3_000_000_000, bytes_accessed=1_000_000, transcendentals=0),
        name="rims",
    )(*arrays, *shapes)


def core_kernel(num_col, num_layer, refs_in, *refs):
    blocks = Blocks(refs[:refs_in], num_col, num_layer)
    ownh, ownl, depth, extra, core_ref, planeh, planel = refs[refs_in:]
    for at, (which, pair) in enumerate(blocks.units()):
        if at >= PAIRS:
            set_planes(blocks, blocks.unit(which, pair), which, CORE_X, at - PAIRS, planeh, planel)
    inner = pl.ds(HALO, CORE)
    split = PAIRS * UNIT
    core_ref[...] = summed(ownh[inner, :], ownl[inner, :], depth[:, 0:split]) + summed(
        planeh[...], planel[...], depth[:, split:]
    )

    @pl.when(jnp.max(blocks.over()) > 0)
    def _():
        core_ref[...] += extra[...]


def core_part(arrays, shapes, depth, extra, num_col, num_layer):
    gaussians = depth.shape[1] - PAIRS * UNIT
    return pl.pallas_call(
        functools.partial(core_kernel, num_col, num_layer, len(arrays)),
        out_shape=jax.ShapeDtypeStruct((CORE, GZ), F32),
        in_specs=[VMEM] * (len(arrays) + 4),
        out_specs=VMEM,
        scratch_shapes=[pltpu.VMEM((CORE, gaussians), BF16), pltpu.VMEM((CORE, gaussians), BF16)],
        compiler_params=PARAMS,
        cost_estimate=pl.CostEstimate(flops=1_500_000_000, bytes_accessed=1_000_000, transcendentals=0),
        name="core",
    )(*arrays, *shapes, depth, extra)


def product_kernel(num_row, num_col, num_layer, refs_in, *refs):
    blocks = Blocks(refs[:refs_in], num_col, num_layer)
    h_refs = refs[refs_in : refs_in + num_row]
    out_ref, token_ref, slab = refs[refs_in + num_row :]
    token_ref[...] = jnp.zeros_like(token_ref)
    row = lax.axis_index("row")
    rows = h_refs[0].shape[1]
    for back in range(num_layer):
        for step in range(num_row):
            start = pl.multiple_of((row ^ step) * rows, rows)
            slab[back, pl.ds(start, rows), :] = h_refs[step][back]
    total = jnp.zeros(out_ref.shape, F32)
    for back in range(num_layer):
        for piece in range(num_col):
            if blocks.paired:
                left = blocks.matrix(piece * 4 + back)
                start = pl.multiple_of((blocks.col ^ piece) * LANES, LANES)
            else:
                source = lax.rem(blocks.layer - back + num_layer, num_layer)
                left = blocks.slab(source, piece)
                start = piece * LANES
            right = slab[back, pl.ds(start, LANES), :]
            total += lax.dot_general(left, right, TN, preferred_element_type=F32)
    out_ref[...] = total.astype(BF16)


def multiply(arrays, parts, num_row, num_col, num_layer):
    return pl.pallas_call(
        functools.partial(product_kernel, num_row, num_col, num_layer, len(arrays)),
        out_shape=(
            jax.ShapeDtypeStruct((arrays[0].shape[-1], LANES), BF16),
            jax.ShapeDtypeStruct((8, LANES), F32),
        ),
        in_specs=[VMEM] * (num_row + len(arrays)),
        out_specs=(VMEM, VMEM),
        scratch_shapes=[pltpu.VMEM((num_layer, num_col * LANES, LANES), BF16)],
        compiler_params=PARAMS,
        cost_estimate=pl.CostEstimate(flops=500_000_000, bytes_accessed=1_000_000, transcendentals=0),
        name="multiply",
    )(*arrays, *parts)


def stack_kernel(own_ref, near_ref, far_ref, both_ref, out_ref):
    out_ref[0] = own_ref[BASE:, LANES:UNIT]
    out_ref[1] = near_ref[BASE:, 0:LANES]
    out_ref[2] = far_ref[BASE:, 0:LANES]
    out_ref[3] = both_ref[BASE:, LANES:UNIT]


def stack(own, near, far, both):
    return pl.pallas_call(
        stack_kernel,
        out_shape=jax.ShapeDtypeStruct((4, own.shape[0] - BASE, LANES), BF16),
        in_specs=[VMEM] * 4,
        out_specs=VMEM,
        compiler_params=PARAMS,
        name="stack",
    )(own, near, far, both)


def fold_kernel(core_ref, below_ref, above_ref, after_ref, out_ref):
    out_ref[0:HALO, :] = core_ref[0:HALO, :] + below_ref[...]
    out_ref[HALO : CORE - HALO, :] = core_ref[HALO : CORE - HALO, :]
    out_ref[CORE - HALO : CORE, :] = core_ref[CORE - HALO : CORE, :] + above_ref[...]


def fold(core, below, above, after):
    return pl.pallas_call(
        fold_kernel,
        out_shape=jax.ShapeDtypeStruct((CORE, GZ), F32),
        in_specs=[VMEM] * 4,
        out_specs=VMEM,
        compiler_params=PARAMS,
        cost_estimate=pl.CostEstimate(flops=1_000_000, bytes_accessed=400_000, transcendentals=0),
        name="fold",
    )(core, below, above, after)


def shifted(value, axis, count, step):
    return lax.ppermute(value, axis, [(i, (i + step) % count) for i in range(count)])


def crossed(value, col_bit, layer_bits):
    pairs = [(c * 4 + l, (c ^ col_bit) * 4 + (l ^ layer_bits)) for c in range(2) for l in range(4)]
    return lax.ppermute(value, ("col", "layer"), pairs)


def gather_paired(base, tall_y, tall_core):
    got_x = crossed(base, 1, 0)
    got_y = crossed(tall_y, 0, 2)
    got_xy = crossed(base, 1, 2)
    near = crossed(tall_core, 0, 1)
    near_x = crossed(got_x, 0, 1)
    near_y = crossed(got_y, 0, 1)
    near_xy = crossed(got_xy, 0, 1)
    return [tall_core, near, got_y, near_y, got_x, near_x, got_xy, near_xy]


def on_device(p_slabs, p_mask, h_slabs, h_mask, gauss_row, gauss_col, gauss_cell, gauss_expo, gauss_pref):
    num_row, num_col, num_layer = (lax.axis_size(axis) for axis in ("row", "col", "layer"))
    paired = num_col == 2 and num_layer == 4
    flat = [x.reshape(8, LANES) for x in (gauss_row, gauss_col, gauss_cell, gauss_expo, gauss_pref)]
    made = prepare(paired, p_slabs[0], p_mask[0].T, h_slabs[0], h_mask[0], *flat)
    if paired:
        base, tall_y, tall_core = made
        settled, planeh, planel, ez = settle(tall_core)
        arrays = gather_paired(base, tall_y, settled)
        mine = stack(*arrays[:4])
    else:
        base, pieces = made
        arrays = [lax.all_gather(base, ("layer", "col"), axis=0)]
        _, planeh, planel, ez = settle(base)
        mine = [pieces[0]] + [shifted(pieces[step], "layer", num_layer, step) for step in range(1, num_layer)]
        mine = jnp.stack(mine)

    def over_row(value, step):
        return lax.ppermute(value, "row", [(i, i ^ step) for i in range(num_row)])

    parts = [mine] + [over_row(mine, step) for step in range(1, num_row)]
    if num_row == 4:
        parts[3] = over_row(parts[2], 1)
    low, high, depth, extra = rims(arrays, (planeh, planel, ez), num_col, num_layer)
    below = shifted(high, "row", num_row, 1)
    above = shifted(low, "row", num_row, num_row - 1)
    core = core_part(arrays, (planeh, planel), depth, extra, num_col, num_layer)
    product, token = multiply(arrays, parts, num_row, num_col, num_layer)
    density = fold(core, below, above, token).reshape(GX, GY, GZ)
    return (product, density)


def solution(mesh):
    placed = (P("layer", "row", "col"),) * 4 + (P(("row", "col", "layer")),) * 5
    return jax.shard_map(
        on_device,
        mesh=mesh,
        in_specs=placed,
        out_specs=(P("row", ("col", "layer")), P("row", "col", "layer")),
        check_vma=False,
    )
```

```python
import functools

import jax
import jax.numpy as jnp
from jax import lax
from jax.experimental import pallas as pl
from jax.experimental.pallas import tpu as pltpu
from jax.sharding import PartitionSpec as P

BS = 32
GX = 16
GY = 16
GZ = 128
R = 4
LANES = 128
F32 = jnp.float32
BF16 = jnp.bfloat16
HALO = R * GY
CORE = GX * GY
FULL = CORE + 2 * HALO
UNIT = 2 * LANES
PAIRS = 4
META = (PAIRS + 1) * 16
BASE = LANES + META
FLAG = 12
VMEM = pl.BlockSpec(memory_space=pltpu.VMEM)
HBM = pl.BlockSpec(memory_space=pltpu.HBM)
PARAMS = pltpu.CompilerParams(vmem_limit_bytes=40 * 1024 * 1024)
NT = (((1,), (1,)), ((), ()))
TN = (((0,), (0,)), ((), ()))


def iota(shape, axis):
    return lax.broadcasted_iota(jnp.int32, shape, axis).astype(F32)


def split3(value):
    first = value.astype(BF16).astype(F32)
    rest = value - first
    second = rest.astype(BF16).astype(F32)
    return first, second, rest - second


def masked(values, bits):
    lane = lax.broadcasted_iota(jnp.int32, values.shape, 1) // BS
    keep = jnp.zeros(values.shape, jnp.int32)
    for piece, bit in enumerate(bits):
        keep = jnp.where(lane == piece, bit, keep)
    return jnp.where(keep > 0, values.astype(F32), 0.0)


def ranks(flags):
    up = (iota((LANES, LANES), 0) <= iota((LANES, LANES), 1)).astype(F32).astype(BF16)
    ones = jnp.ones((LANES, LANES), BF16)
    within = jnp.dot(flags.astype(BF16), up, preferred_element_type=F32)
    totals = jnp.dot(flags.astype(BF16), ones, preferred_element_type=F32)
    row, other = iota((16, 16), 0), iota((16, 16), 1)
    same = (row < 8) == (other < 8)
    before = jnp.where(same & (other < row), 1.0, 0.0).astype(BF16)
    every = jnp.where(same, 1.0, 0.0).astype(BF16)
    earlier = jnp.dot(before, totals.astype(BF16), preferred_element_type=F32)
    count = jnp.dot(every, totals.astype(BF16), preferred_element_type=F32)
    return jnp.where(flags > 0, within + earlier - 1.0, -1.0), count


def h_piece(h_ref, hm_ref, chunk):
    pieces = LANES // BS
    out = []
    for block in range(h_ref.shape[0] // BS):
        bits = [hm_ref[block, chunk * pieces + at] for at in range(pieces)]
        value = h_ref[pl.ds(block * BS, BS), pl.ds(pl.multiple_of(chunk * LANES, LANES), LANES)]
        out.append(masked(value, bits).astype(BF16))
    return jnp.concatenate(out, axis=0)


def prepare_kernel(paired, *refs):
    sources, outs, refs = refs[:9], refs[9:-14], refs[-14:]
    landed, (tmp, fields, matrix, onehot, sems) = refs[:9], refs[9:]
    copies = [pltpu.make_async_copy(src, dst, sems.at[at]) for at, (src, dst) in enumerate(zip(sources, landed))]
    for copy in copies:
        copy.start()
    for copy in copies:
        copy.wait()
    p_ref, pm_ref, h_ref, hm_ref, row_ref, col_ref, cell_ref, expo_ref, pref_ref = landed
    layer = lax.axis_index("layer")
    count = lax.axis_size("layer")
    band = p_ref.shape[0]
    for block in range(band // BS):
        rows = pl.ds(block * BS, BS)
        tmp[rows, :] = masked(p_ref[rows, :], [pm_ref[piece, block] for piece in range(LANES // BS)])
    turned = tmp[...].T.astype(BF16)
    col = col_ref[...]
    cell = cell_ref[...]
    cell_z = (cell % GZ).astype(F32)
    values = [
        row_ref[...].astype(F32),
        (col // LANES).astype(F32),
        (col % LANES).astype(F32),
        (cell // (GY * GZ)).astype(F32),
        (cell // GZ % GY).astype(F32),
        cell_z,
        *split3(expo_ref[...]),
        *split3(pref_ref[...]),
    ]
    for index in range(16):
        fields[8 * index : 8 * index + 8, :] = values[index] if index < len(values) else jnp.zeros((8, LANES), F32)
    tiles = [fields[pl.ds(part, 16, stride=8), :].astype(BF16) for part in range(2 * PAIRS)]
    for part in range(2 * PAIRS):
        matrix[:, part * LANES : part * LANES + LANES] = tiles[part]
    faces = jnp.concatenate([jnp.where(cell_z < R, 1.0, 0.0), jnp.where(cell_z >= GZ - R, 1.0, 0.0)], axis=0)
    place, many = ranks(faces)
    slot = iota((LANES, LANES), 0)
    for part in range(2 * PAIRS):
        lanes = pl.ds(part * LANES, LANES)
        for face in range(2):
            hit = slot == place[face * 8 + part : face * 8 + part + 1, :]
            onehot[face * LANES : face * LANES + LANES, lanes] = jnp.where(hit, 1.0, 0.0).astype(BF16)
    listed = lax.dot_general(matrix[...], onehot[...], NT, preferred_element_type=F32)
    over = jnp.where(jnp.max(many, axis=0, keepdims=True) > LANES, 1.0, 0.0)
    over = jnp.concatenate([over, over], axis=1)
    listed = jnp.where(iota(listed.shape, 0) == FLAG, over, listed).astype(BF16)
    copies = outs[:3] if paired else outs[:1]
    for out in copies:
        out[0:LANES, :] = turned
        for pair in range(PAIRS):
            out[LANES + 16 * pair : LANES + 16 * pair + 16, :] = matrix[:, pair * UNIT : pair * UNIT + UNIT]
        out[LANES + 16 * PAIRS : BASE, :] = listed

    def piece(chunk):
        return h_piece(h_ref, hm_ref, chunk)

    if paired:
        outs[1][BASE:, 0:LANES] = piece(layer ^ 2)
        outs[1][BASE:, LANES:UNIT] = piece(layer ^ 3)
        outs[2][BASE:, 0:LANES] = piece(layer ^ 1)
        outs[2][BASE:, LANES:UNIT] = piece(layer)
    else:
        for back in range(h_ref.shape[1] // LANES):
            outs[1][back] = piece(lax.rem(layer + back, count))


def prepare(paired, p, p_mask, h, h_mask, *gauss):
    band = p.shape[0]
    base = jax.ShapeDtypeStruct((BASE, band), BF16)
    tall = jax.ShapeDtypeStruct((BASE + h.shape[0], band), BF16)
    if paired:
        outs = (base, tall, tall)
    else:
        outs = (base, jax.ShapeDtypeStruct((h.shape[1] // LANES, h.shape[0], LANES), BF16))
    return pl.pallas_call(
        functools.partial(prepare_kernel, paired),
        out_shape=outs,
        in_specs=[HBM] * 9,
        out_specs=(VMEM,) * len(outs),
        scratch_shapes=[
            pltpu.VMEM(p.shape, p.dtype),
            pltpu.SMEM(p_mask.shape, p_mask.dtype),
            pltpu.VMEM(h.shape, h.dtype),
            pltpu.SMEM(h_mask.shape, h_mask.dtype),
            *[pltpu.VMEM(x.shape, x.dtype) for x in gauss],
            pltpu.VMEM(p.shape, F32),
            pltpu.VMEM((16 * 8, LANES), F32),
            pltpu.VMEM((16, 2 * PAIRS * LANES), BF16),
            pltpu.VMEM((UNIT, 2 * PAIRS * LANES), BF16),
            pltpu.SemaphoreType.DMA((9,)),
        ],
        compiler_params=pltpu.CompilerParams(vmem_limit_bytes=62 * 1024 * 1024),
        name="prepare",
    )(p, p_mask, h, h_mask, *gauss)


class Blocks:
    def __init__(self, refs, num_col, num_layer):
        self.refs = refs
        self.num_col, self.num_layer = num_col, num_layer
        self.paired = len(refs) > 1
        self.col, self.layer = lax.axis_index("col"), lax.axis_index("layer")
        self.total = num_col * num_layer
        self.col_shifts = [0, 1] if num_col == 2 else [0, -1, 1]

    def ident(self, index):
        if not self.paired:
            return index
        return (self.layer ^ (index % 4)) * 2 + (self.col ^ (index // 4))

    def matrix(self, index):
        return self.refs[index][0:LANES, :] if self.paired else self.refs[0][index, 0:LANES, :]

    def slab(self, layer, piece):
        index = layer * self.num_col + piece
        return self.refs[0][index, 0:LANES, :]

    def tile(self, which, side, pair):
        rows = pl.ds(LANES + 16 * pair, 16)
        if self.paired:
            return self.refs[which * 4 + side][rows, :].astype(F32)
        shift_l = 0 if side == 0 else (1 if side == 1 else -1)
        index = lax.rem(self.layer + shift_l + self.num_layer, self.num_layer) * self.num_col
        index += lax.rem(self.col + self.col_shifts[which] + self.num_col, self.num_col)
        return self.refs[0][index, rows, :].astype(F32)

    def side_shift(self, side):
        if self.paired:
            even = (self.layer % 2) == 0
            return jnp.where(even, 1.0, -1.0) if side == 1 else jnp.where(even, -1.0, 1.0)
        return 1.0 if side == 1 else -1.0

    def sides(self):
        return (1, 3) if self.paired else (1, 2)

    def units(self):
        return [(which, pair) for which in range(len(self.col_shifts)) for pair in range(PAIRS + 1)]

    def listed(self, which):
        halves = []
        for side in self.sides():
            both = self.tile(which, side, PAIRS)
            upward = self.side_shift(side) > 0
            halves.append(jnp.where(upward, both[:, 0:LANES], both[:, LANES:UNIT]))
        return jnp.concatenate(halves, axis=1)

    def unit(self, which, pair):
        return self.tile(which, 0, pair) if pair < PAIRS else self.listed(which)

    def lifts(self, pair):
        if pair < PAIRS:
            return 0.0
        lane = iota((1, UNIT), 1)
        first, second = self.sides()
        return jnp.where(lane < LANES, self.side_shift(first), self.side_shift(second)) * float(GZ)

    def over(self):
        flags = [
            self.tile(which, side, PAIRS)[FLAG : FLAG + 1, :]
            for which in range(len(self.col_shifts))
            for side in self.sides()
        ]
        return functools.reduce(jnp.maximum, flags)

    def long_steps(self):
        return [(which, side) for which in range(len(self.col_shifts)) for side in self.sides()]


def weigh(blocks, whole, tile):
    band = whole.shape[1]
    onehot = jnp.where(iota((band, UNIT), 0) == tile[0:1, :], 1.0, 0.0).astype(BF16)
    found = jnp.dot(whole[...], onehot, preferred_element_type=F32)
    picked = jnp.zeros((LANES, UNIT), F32)
    for index in range(blocks.total):
        mine = tile[1:2, :] == jnp.asarray(blocks.ident(index)).astype(F32)
        picked = jnp.where(mine, found[index * LANES : index * LANES + LANES, :], picked)
    value = jnp.sum(jnp.where(iota((LANES, UNIT), 0) == tile[2:3, :], picked, 0.0), axis=0, keepdims=True)
    return (tile[9:10, :] + tile[10:11, :] + tile[11:12, :]) * value


def bell(dist, expo):
    square = dist * dist
    return jnp.where(square < (R + 0.5) ** 2, jnp.exp(-expo * square), 0.0)


RIM_X = tuple(range(R)) + tuple(range(GX + R, GX + 2 * R))
CORE_X = tuple(range(R, GX + R))
ALL_X = tuple(range(GX + 2 * R))


def decay(tile):
    return tile[6:7, :] + tile[7:8, :] + tile[8:9, :]


def shapes_x(tile):
    return bell(iota((GX + 2 * R, UNIT), 0) - float(R) - tile[3:4, :], decay(tile))


def shapes_y(tile, shift, wraps):
    dy = iota((GY, UNIT), 0) - tile[4:5, :] - float(shift * GY)
    if wraps:
        dy = jnp.where(dy < -float(GY), dy + 2.0 * GY, dy)
    return bell(dy, decay(tile))


def shapes_z(tile, lift):
    return bell(iota((GZ, UNIT), 0) - tile[5:6, :] - lift, decay(tile))


def fill_planes(ex, ey, places, at, planeh, planel):
    lanes = pl.ds(at * UNIT, UNIT)
    for spot, x in enumerate(places):
        plane = ex[x : x + 1, :] * ey
        plane_hi = plane.astype(BF16)
        planeh[spot * GY : spot * GY + GY, lanes] = plane_hi
        planel[spot * GY : spot * GY + GY, lanes] = (plane - plane_hi.astype(F32)).astype(BF16)


def fill_depth(ez, coef, at, depth):
    weighed = ez * coef
    lanes = pl.ds(at * UNIT, UNIT)
    weighed_hi = weighed.astype(BF16)
    depth[0:GZ, lanes] = weighed_hi
    depth[GZ : 2 * GZ, lanes] = (weighed - weighed_hi.astype(F32)).astype(BF16)


def set_planes(blocks, tile, which, places, at, planeh, planel):
    wraps = blocks.num_col == 2 and which == 1
    fill_planes(shapes_x(tile), shapes_y(tile, blocks.col_shifts[which], wraps), places, at, planeh, planel)


def summed(planeh, planel, depth):
    first = lax.dot_general(planeh, depth, NT, preferred_element_type=F32)
    second = lax.dot_general(planel, depth[0:GZ, :], NT, preferred_element_type=F32)
    return first[:, 0:GZ] + first[:, GZ : 2 * GZ] + second


def rims_kernel(num_col, num_layer, refs_in, *refs):
    blocks = Blocks(refs[:refs_in], num_col, num_layer)
    low_ref, high_ref, depth, extra, whole, planeh, planel, longh, longl, long_depth, acc = refs[refs_in:]
    for index in range(blocks.total):
        whole[index * LANES : index * LANES + LANES, :] = blocks.matrix(index)
    over = blocks.over()
    for at, (which, pair) in enumerate(blocks.units()):
        tile = blocks.unit(which, pair)
        coef = weigh(blocks, whole, tile)
        if pair == PAIRS:
            coef = jnp.where(over > 0, 0.0, coef)
        set_planes(blocks, tile, which, RIM_X, at, planeh, planel)
        fill_depth(shapes_z(tile, blocks.lifts(pair)), coef, at, depth)
    total = summed(planeh[...], planel[...], depth[...])
    low_ref[...] = total[0:HALO, :]
    high_ref[...] = total[HALO:, :]

    @pl.when(jnp.max(over) > 0)
    def _():
        acc[...] = jnp.zeros_like(acc)
        for which, side in blocks.long_steps():

            def step(pair, carry):
                tile = blocks.tile(which, side, pair)
                lift = blocks.side_shift(side) * float(GZ)
                set_planes(blocks, tile, which, ALL_X, 0, longh, longl)
                fill_depth(shapes_z(tile, lift), weigh(blocks, whole, tile), 0, long_depth)
                acc[...] += summed(longh[...], longl[...], long_depth[...])
                return carry

            lax.fori_loop(0, PAIRS, step, 0)
        low_ref[...] += acc[0:HALO, :]
        extra[...] = acc[HALO : HALO + CORE, :]
        high_ref[...] += acc[HALO + CORE : FULL, :]


def rims(arrays, num_col, num_layer):
    gaussians = (2 if num_col == 2 else 3) * (PAIRS + 1) * UNIT
    return pl.pallas_call(
        functools.partial(rims_kernel, num_col, num_layer, len(arrays)),
        out_shape=(
            jax.ShapeDtypeStruct((HALO, GZ), F32),
            jax.ShapeDtypeStruct((HALO, GZ), F32),
            jax.ShapeDtypeStruct((2 * GZ, gaussians), BF16),
            jax.ShapeDtypeStruct((CORE, GZ), F32),
        ),
        in_specs=[VMEM] * len(arrays),
        out_specs=(VMEM,) * 4,
        scratch_shapes=[
            pltpu.VMEM((num_col * num_layer * LANES, arrays[0].shape[-1]), BF16),
            pltpu.VMEM((2 * HALO, gaussians), BF16),
            pltpu.VMEM((2 * HALO, gaussians), BF16),
            pltpu.VMEM((FULL, UNIT), BF16),
            pltpu.VMEM((FULL, UNIT), BF16),
            pltpu.VMEM((2 * GZ, UNIT), BF16),
            pltpu.VMEM((FULL, GZ), F32),
        ],
        compiler_params=PARAMS,
        cost_estimate=pl.CostEstimate(flops=3_000_000_000, bytes_accessed=1_000_000, transcendentals=0),
        name="rims",
    )(*arrays)


def core_kernel(num_col, num_layer, refs_in, *refs):
    blocks = Blocks(refs[:refs_in], num_col, num_layer)
    depth, extra, core_ref, planeh, planel = refs[refs_in:]
    for at, (which, pair) in enumerate(blocks.units()):
        set_planes(blocks, blocks.unit(which, pair), which, CORE_X, at, planeh, planel)
    core_ref[...] = summed(planeh[...], planel[...], depth[...])

    @pl.when(jnp.max(blocks.over()) > 0)
    def _():
        core_ref[...] += extra[...]


def core_part(arrays, depth, extra, num_col, num_layer):
    gaussians = depth.shape[1]
    return pl.pallas_call(
        functools.partial(core_kernel, num_col, num_layer, len(arrays)),
        out_shape=jax.ShapeDtypeStruct((CORE, GZ), F32),
        in_specs=[VMEM] * (len(arrays) + 2),
        out_specs=VMEM,
        scratch_shapes=[pltpu.VMEM((CORE, gaussians), BF16), pltpu.VMEM((CORE, gaussians), BF16)],
        compiler_params=PARAMS,
        cost_estimate=pl.CostEstimate(flops=1_500_000_000, bytes_accessed=1_000_000, transcendentals=0),
        name="core",
    )(*arrays, depth, extra)


def product_kernel(num_row, num_col, num_layer, refs_in, *refs):
    blocks = Blocks(refs[:refs_in], num_col, num_layer)
    h_refs = refs[refs_in : refs_in + num_row]
    out_ref, token_ref, slab = refs[refs_in + num_row :]
    token_ref[...] = jnp.zeros_like(token_ref)
    row = lax.axis_index("row")
    rows = h_refs[0].shape[1]
    for back in range(num_layer):
        for step in range(num_row):
            start = pl.multiple_of((row ^ step) * rows, rows)
            slab[back, pl.ds(start, rows), :] = h_refs[step][back]
    total = jnp.zeros(out_ref.shape, F32)
    for back in range(num_layer):
        for piece in range(num_col):
            if blocks.paired:
                left = blocks.matrix(piece * 4 + back)
                start = pl.multiple_of((blocks.col ^ piece) * LANES, LANES)
            else:
                source = lax.rem(blocks.layer - back + num_layer, num_layer)
                left = blocks.slab(source, piece)
                start = piece * LANES
            right = slab[back, pl.ds(start, LANES), :]
            total += lax.dot_general(left, right, TN, preferred_element_type=F32)
    out_ref[...] = total.astype(BF16)


def multiply(arrays, parts, num_row, num_col, num_layer):
    return pl.pallas_call(
        functools.partial(product_kernel, num_row, num_col, num_layer, len(arrays)),
        out_shape=(
            jax.ShapeDtypeStruct((arrays[0].shape[-1], LANES), BF16),
            jax.ShapeDtypeStruct((8, LANES), F32),
        ),
        in_specs=[VMEM] * (num_row + len(arrays)),
        out_specs=(VMEM, VMEM),
        scratch_shapes=[pltpu.VMEM((num_layer, num_col * LANES, LANES), BF16)],
        compiler_params=PARAMS,
        cost_estimate=pl.CostEstimate(flops=500_000_000, bytes_accessed=1_000_000, transcendentals=0),
        name="multiply",
    )(*arrays, *parts)


def stack_kernel(own_ref, near_ref, far_ref, both_ref, out_ref):
    out_ref[0] = own_ref[BASE:, LANES:UNIT]
    out_ref[1] = near_ref[BASE:, 0:LANES]
    out_ref[2] = far_ref[BASE:, 0:LANES]
    out_ref[3] = both_ref[BASE:, LANES:UNIT]


def stack(own, near, far, both):
    return pl.pallas_call(
        stack_kernel,
        out_shape=jax.ShapeDtypeStruct((4, own.shape[0] - BASE, LANES), BF16),
        in_specs=[VMEM] * 4,
        out_specs=VMEM,
        compiler_params=PARAMS,
        name="stack",
    )(own, near, far, both)


def fold_kernel(core_ref, below_ref, above_ref, after_ref, out_ref):
    out_ref[0:HALO, :] = core_ref[0:HALO, :] + below_ref[...]
    out_ref[HALO : CORE - HALO, :] = core_ref[HALO : CORE - HALO, :]
    out_ref[CORE - HALO : CORE, :] = core_ref[CORE - HALO : CORE, :] + above_ref[...]


def fold(core, below, above, after):
    return pl.pallas_call(
        fold_kernel,
        out_shape=jax.ShapeDtypeStruct((CORE, GZ), F32),
        in_specs=[VMEM] * 4,
        out_specs=VMEM,
        compiler_params=PARAMS,
        cost_estimate=pl.CostEstimate(flops=1_000_000, bytes_accessed=400_000, transcendentals=0),
        name="fold",
    )(core, below, above, after)


def shifted(value, axis, count, step):
    return lax.ppermute(value, axis, [(i, (i + step) % count) for i in range(count)])


def crossed(value, col_bit, layer_bits):
    pairs = [(c * 4 + l, (c ^ col_bit) * 4 + (l ^ layer_bits)) for c in range(2) for l in range(4)]
    return lax.ppermute(value, ("col", "layer"), pairs)


def gather_paired(base, tall_y, tall_core):
    got_x = crossed(base, 1, 0)
    got_y = crossed(tall_y, 0, 2)
    got_xy = crossed(base, 1, 2)
    near = crossed(tall_core, 0, 1)
    near_x = crossed(got_x, 0, 1)
    near_y = crossed(got_y, 0, 1)
    near_xy = crossed(got_xy, 0, 1)
    return [tall_core, near, got_y, near_y, got_x, near_x, got_xy, near_xy]


def on_device(p_slabs, p_mask, h_slabs, h_mask, gauss_row, gauss_col, gauss_cell, gauss_expo, gauss_pref):
    num_row, num_col, num_layer = (lax.axis_size(axis) for axis in ("row", "col", "layer"))
    paired = num_col == 2 and num_layer == 4
    flat = [x.reshape(8, LANES) for x in (gauss_row, gauss_col, gauss_cell, gauss_expo, gauss_pref)]
    made = prepare(paired, p_slabs[0], p_mask[0].T, h_slabs[0], h_mask[0], *flat)
    if paired:
        arrays = gather_paired(*made)
        mine = stack(*arrays[:4])
    else:
        base, pieces = made
        arrays = [lax.all_gather(base, ("layer", "col"), axis=0)]
        mine = [pieces[0]] + [shifted(pieces[step], "layer", num_layer, step) for step in range(1, num_layer)]
        mine = jnp.stack(mine)
    low, high, depth, extra = rims(arrays, num_col, num_layer)
    parts = [mine] + [
        lax.ppermute(mine, "row", [(i, i ^ step) for i in range(num_row)]) for step in range(1, num_row)
    ]
    below = shifted(high, "row", num_row, 1)
    above = shifted(low, "row", num_row, num_row - 1)
    core = core_part(arrays, depth, extra, num_col, num_layer)
    product, token = multiply(arrays, parts, num_row, num_col, num_layer)
    density = fold(core, below, above, token).reshape(GX, GY, GZ)
    return (product, density)


def solution(mesh):
    placed = (P("layer", "row", "col"),) * 4 + (P(("row", "col", "layer")),) * 5
    return jax.shard_map(
        on_device,
        mesh=mesh,
        in_specs=placed,
        out_specs=(P("row", ("col", "layer")), P("row", "col", "layer")),
        check_vma=False,
    )
```

```python
import functools

import jax
import jax.numpy as jnp
from jax import lax
from jax.experimental import pallas as pl
from jax.experimental.pallas import tpu as pltpu
from jax.sharding import PartitionSpec as P

BS = 32
GX = 16
GY = 16
GZ = 128
R = 4
LANES = 128
F32 = jnp.float32
BF16 = jnp.bfloat16
HALO = R * GY
CORE = GX * GY
FULL = CORE + 2 * HALO
UNIT = 2 * LANES
PAIRS = 4
META = (PAIRS + 1) * 16
BASE = LANES + META
FLAG = 12
VMEM = pl.BlockSpec(memory_space=pltpu.VMEM)
HBM = pl.BlockSpec(memory_space=pltpu.HBM)
PARAMS = pltpu.CompilerParams(vmem_limit_bytes=40 * 1024 * 1024)
NT = (((1,), (1,)), ((), ()))
TN = (((0,), (0,)), ((), ()))


def iota(shape, axis):
    return lax.broadcasted_iota(jnp.int32, shape, axis).astype(F32)


def split3(value):
    first = value.astype(BF16).astype(F32)
    rest = value - first
    second = rest.astype(BF16).astype(F32)
    return first, second, rest - second


def masked(values, bits):
    lane = lax.broadcasted_iota(jnp.int32, values.shape, 1) // BS
    keep = jnp.zeros(values.shape, jnp.int32)
    for piece, bit in enumerate(bits):
        keep = jnp.where(lane == piece, bit, keep)
    return jnp.where(keep > 0, values.astype(F32), 0.0)


def ranks(flags):
    up = (iota((LANES, LANES), 0) <= iota((LANES, LANES), 1)).astype(F32).astype(BF16)
    ones = jnp.ones((LANES, LANES), BF16)
    within = jnp.dot(flags.astype(BF16), up, preferred_element_type=F32)
    totals = jnp.dot(flags.astype(BF16), ones, preferred_element_type=F32)
    row, other = iota((16, 16), 0), iota((16, 16), 1)
    same = (row < 8) == (other < 8)
    before = jnp.where(same & (other < row), 1.0, 0.0).astype(BF16)
    every = jnp.where(same, 1.0, 0.0).astype(BF16)
    earlier = jnp.dot(before, totals.astype(BF16), preferred_element_type=F32)
    count = jnp.dot(every, totals.astype(BF16), preferred_element_type=F32)
    return jnp.where(flags > 0, within + earlier - 1.0, -1.0), count


def h_piece(h_ref, hm_ref, chunk):
    pieces = LANES // BS
    out = []
    for block in range(h_ref.shape[0] // BS):
        bits = [hm_ref[block, chunk * pieces + at] for at in range(pieces)]
        value = h_ref[pl.ds(block * BS, BS), pl.ds(pl.multiple_of(chunk * LANES, LANES), LANES)]
        out.append(masked(value, bits).astype(BF16))
    return jnp.concatenate(out, axis=0)


def prepare_kernel(paired, *refs):
    sources, outs, refs = refs[:9], refs[9:-14], refs[-14:]
    landed, (tmp, fields, matrix, onehot, sems) = refs[:9], refs[9:]
    copies = [pltpu.make_async_copy(src, dst, sems.at[at]) for at, (src, dst) in enumerate(zip(sources, landed))]
    for copy in copies:
        copy.start()
    for copy in copies:
        copy.wait()
    p_ref, pm_ref, h_ref, hm_ref, row_ref, col_ref, cell_ref, expo_ref, pref_ref = landed
    layer = lax.axis_index("layer")
    count = lax.axis_size("layer")
    band = p_ref.shape[0]
    for block in range(band // BS):
        rows = pl.ds(block * BS, BS)
        tmp[rows, :] = masked(p_ref[rows, :], [pm_ref[piece, block] for piece in range(LANES // BS)])
    turned = tmp[...].T.astype(BF16)
    col = col_ref[...]
    cell = cell_ref[...]
    cell_z = (cell % GZ).astype(F32)
    values = [
        row_ref[...].astype(F32),
        (col // LANES).astype(F32),
        (col % LANES).astype(F32),
        (cell // (GY * GZ)).astype(F32),
        (cell // GZ % GY).astype(F32),
        cell_z,
        *split3(expo_ref[...]),
        *split3(pref_ref[...]),
    ]
    for index in range(16):
        fields[8 * index : 8 * index + 8, :] = values[index] if index < len(values) else jnp.zeros((8, LANES), F32)
    tiles = [fields[pl.ds(part, 16, stride=8), :].astype(BF16) for part in range(2 * PAIRS)]
    for part in range(2 * PAIRS):
        matrix[:, part * LANES : part * LANES + LANES] = tiles[part]
    faces = jnp.concatenate([jnp.where(cell_z < R, 1.0, 0.0), jnp.where(cell_z >= GZ - R, 1.0, 0.0)], axis=0)
    place, many = ranks(faces)
    slot = iota((LANES, LANES), 0)
    for part in range(2 * PAIRS):
        lanes = pl.ds(part * LANES, LANES)
        for face in range(2):
            hit = slot == place[face * 8 + part : face * 8 + part + 1, :]
            onehot[face * LANES : face * LANES + LANES, lanes] = jnp.where(hit, 1.0, 0.0).astype(BF16)
    listed = lax.dot_general(matrix[...], onehot[...], NT, preferred_element_type=F32)
    over = jnp.where(jnp.max(many, axis=0, keepdims=True) > LANES, 1.0, 0.0)
    over = jnp.concatenate([over, over], axis=1)
    listed = jnp.where(iota(listed.shape, 0) == FLAG, over, listed).astype(BF16)
    copies = outs[:3] if paired else outs[:1]
    for out in copies:
        out[0:LANES, :] = turned
        for pair in range(PAIRS):
            out[LANES + 16 * pair : LANES + 16 * pair + 16, :] = matrix[:, pair * UNIT : pair * UNIT + UNIT]
        out[LANES + 16 * PAIRS : BASE, :] = listed

    def piece(chunk):
        return h_piece(h_ref, hm_ref, chunk)

    if paired:
        outs[1][BASE:, 0:LANES] = piece(layer ^ 2)
        outs[1][BASE:, LANES:UNIT] = piece(layer ^ 3)
        outs[2][BASE:, 0:LANES] = piece(layer ^ 1)
        outs[2][BASE:, LANES:UNIT] = piece(layer)
    else:
        for back in range(h_ref.shape[1] // LANES):
            outs[1][back] = piece(lax.rem(layer + back, count))


def prepare(paired, p, p_mask, h, h_mask, *gauss):
    band = p.shape[0]
    base = jax.ShapeDtypeStruct((BASE, band), BF16)
    tall = jax.ShapeDtypeStruct((BASE + h.shape[0], band), BF16)
    if paired:
        outs = (base, tall, tall)
    else:
        outs = (base, jax.ShapeDtypeStruct((h.shape[1] // LANES, h.shape[0], LANES), BF16))
    return pl.pallas_call(
        functools.partial(prepare_kernel, paired),
        out_shape=outs,
        in_specs=[HBM] * 9,
        out_specs=(VMEM,) * len(outs),
        scratch_shapes=[
            pltpu.VMEM(p.shape, p.dtype),
            pltpu.SMEM(p_mask.shape, p_mask.dtype),
            pltpu.VMEM(h.shape, h.dtype),
            pltpu.SMEM(h_mask.shape, h_mask.dtype),
            *[pltpu.VMEM(x.shape, x.dtype) for x in gauss],
            pltpu.VMEM(p.shape, F32),
            pltpu.VMEM((16 * 8, LANES), F32),
            pltpu.VMEM((16, 2 * PAIRS * LANES), BF16),
            pltpu.VMEM((UNIT, 2 * PAIRS * LANES), BF16),
            pltpu.SemaphoreType.DMA((9,)),
        ],
        compiler_params=pltpu.CompilerParams(vmem_limit_bytes=62 * 1024 * 1024),
        name="prepare",
    )(p, p_mask, h, h_mask, *gauss)


class Blocks:
    def __init__(self, refs, num_col, num_layer):
        self.refs = refs
        self.num_col, self.num_layer = num_col, num_layer
        self.paired = len(refs) > 1
        self.col, self.layer = lax.axis_index("col"), lax.axis_index("layer")
        self.total = num_col * num_layer
        self.col_shifts = [0, 1] if num_col == 2 else [0, -1, 1]

    def ident(self, index):
        if not self.paired:
            return index
        return (self.layer ^ (index % 4)) * 2 + (self.col ^ (index // 4))

    def matrix(self, index):
        return self.refs[index][0:LANES, :] if self.paired else self.refs[0][index, 0:LANES, :]

    def slab(self, layer, piece):
        index = layer * self.num_col + piece
        return self.refs[0][index, 0:LANES, :]

    def tile(self, which, side, pair):
        rows = pl.ds(LANES + 16 * pair, 16)
        if self.paired:
            return self.refs[which * 4 + side][rows, :].astype(F32)
        shift_l = 0 if side == 0 else (1 if side == 1 else -1)
        index = lax.rem(self.layer + shift_l + self.num_layer, self.num_layer) * self.num_col
        index += lax.rem(self.col + self.col_shifts[which] + self.num_col, self.num_col)
        return self.refs[0][index, rows, :].astype(F32)

    def side_shift(self, side):
        if self.paired:
            even = (self.layer % 2) == 0
            return jnp.where(even, 1.0, -1.0) if side == 1 else jnp.where(even, -1.0, 1.0)
        return 1.0 if side == 1 else -1.0

    def sides(self):
        return (1, 3) if self.paired else (1, 2)

    def units(self):
        return [(which, pair) for which in range(len(self.col_shifts)) for pair in range(PAIRS + 1)]

    def listed(self, which):
        halves = []
        for side in self.sides():
            both = self.tile(which, side, PAIRS)
            upward = self.side_shift(side) > 0
            halves.append(jnp.where(upward, both[:, 0:LANES], both[:, LANES:UNIT]))
        return jnp.concatenate(halves, axis=1)

    def unit(self, which, pair):
        return self.tile(which, 0, pair) if pair < PAIRS else self.listed(which)

    def lifts(self, pair):
        if pair < PAIRS:
            return 0.0
        lane = iota((1, UNIT), 1)
        first, second = self.sides()
        return jnp.where(lane < LANES, self.side_shift(first), self.side_shift(second)) * float(GZ)

    def over(self):
        flags = [
            self.tile(which, side, PAIRS)[FLAG : FLAG + 1, :]
            for which in range(len(self.col_shifts))
            for side in self.sides()
        ]
        return functools.reduce(jnp.maximum, flags)

    def long_steps(self):
        return [(which, side) for which in range(len(self.col_shifts)) for side in self.sides()]


def weigh(blocks, whole, tile):
    band = whole.shape[1]
    onehot = jnp.where(iota((band, UNIT), 0) == tile[0:1, :], 1.0, 0.0).astype(BF16)
    found = jnp.dot(whole[...], onehot, preferred_element_type=F32)
    picked = jnp.zeros((LANES, UNIT), F32)
    for index in range(blocks.total):
        mine = tile[1:2, :] == jnp.asarray(blocks.ident(index)).astype(F32)
        picked = jnp.where(mine, found[index * LANES : index * LANES + LANES, :], picked)
    value = jnp.sum(jnp.where(iota((LANES, UNIT), 0) == tile[2:3, :], picked, 0.0), axis=0, keepdims=True)
    return (tile[9:10, :] + tile[10:11, :] + tile[11:12, :]) * value


def bell(dist, expo):
    square = dist * dist
    return jnp.where(square < (R + 0.5) ** 2, jnp.exp(-expo * square), 0.0)


RIM_X = tuple(range(R)) + tuple(range(GX + R, GX + 2 * R))
CORE_X = tuple(range(R, GX + R))
ALL_X = tuple(range(GX + 2 * R))


def decay(tile):
    return tile[6:7, :] + tile[7:8, :] + tile[8:9, :]


def shapes_x(tile):
    return bell(iota((GX + 2 * R, UNIT), 0) - float(R) - tile[3:4, :], decay(tile))


def shapes_y(tile, shift, wraps):
    dy = iota((GY, UNIT), 0) - tile[4:5, :] - float(shift * GY)
    if wraps:
        dy = jnp.where(dy < -float(GY), dy + 2.0 * GY, dy)
    return bell(dy, decay(tile))


def shapes_z(tile, lift):
    return bell(iota((GZ, UNIT), 0) - tile[5:6, :] - lift, decay(tile))


def fill_planes(ex, ey, places, at, planeh, planel):
    lanes = pl.ds(at * UNIT, UNIT)
    for spot, x in enumerate(places):
        plane = ex[x : x + 1, :] * ey
        plane_hi = plane.astype(BF16)
        planeh[spot * GY : spot * GY + GY, lanes] = plane_hi
        planel[spot * GY : spot * GY + GY, lanes] = (plane - plane_hi.astype(F32)).astype(BF16)


def fill_depth(ez, coef, at, depth):
    weighed = ez * coef
    lanes = pl.ds(at * UNIT, UNIT)
    weighed_hi = weighed.astype(BF16)
    depth[0:GZ, lanes] = weighed_hi
    depth[GZ : 2 * GZ, lanes] = (weighed - weighed_hi.astype(F32)).astype(BF16)


def set_planes(blocks, tile, which, places, at, planeh, planel):
    wraps = blocks.num_col == 2 and which == 1
    fill_planes(shapes_x(tile), shapes_y(tile, blocks.col_shifts[which], wraps), places, at, planeh, planel)


def summed(planeh, planel, depth):
    first = lax.dot_general(planeh, depth, NT, preferred_element_type=F32)
    second = lax.dot_general(planel, depth[0:GZ, :], NT, preferred_element_type=F32)
    return first[:, 0:GZ] + first[:, GZ : 2 * GZ] + second


def rims_kernel(num_col, num_layer, refs_in, *refs):
    blocks = Blocks(refs[:refs_in], num_col, num_layer)
    low_ref, high_ref, depth, extra, whole, planeh, planel, longh, longl, long_depth, acc = refs[refs_in:]
    for index in range(blocks.total):
        whole[index * LANES : index * LANES + LANES, :] = blocks.matrix(index)
    over = blocks.over()
    for at, (which, pair) in enumerate(blocks.units()):
        tile = blocks.unit(which, pair)
        coef = weigh(blocks, whole, tile)
        if pair == PAIRS:
            coef = jnp.where(over > 0, 0.0, coef)
        set_planes(blocks, tile, which, RIM_X, at, planeh, planel)
        fill_depth(shapes_z(tile, blocks.lifts(pair)), coef, at, depth)
    total = summed(planeh[...], planel[...], depth[...])
    low_ref[...] = total[0:HALO, :]
    high_ref[...] = total[HALO:, :]

    @pl.when(jnp.max(over) > 0)
    def _():
        acc[...] = jnp.zeros_like(acc)
        for which, side in blocks.long_steps():

            def step(pair, carry):
                tile = blocks.tile(which, side, pair)
                lift = blocks.side_shift(side) * float(GZ)
                set_planes(blocks, tile, which, ALL_X, 0, longh, longl)
                fill_depth(shapes_z(tile, lift), weigh(blocks, whole, tile), 0, long_depth)
                acc[...] += summed(longh[...], longl[...], long_depth[...])
                return carry

            lax.fori_loop(0, PAIRS, step, 0)
        low_ref[...] += acc[0:HALO, :]
        extra[...] = acc[HALO : HALO + CORE, :]
        high_ref[...] += acc[HALO + CORE : FULL, :]


def rims(arrays, num_col, num_layer):
    gaussians = (2 if num_col == 2 else 3) * (PAIRS + 1) * UNIT
    return pl.pallas_call(
        functools.partial(rims_kernel, num_col, num_layer, len(arrays)),
        out_shape=(
            jax.ShapeDtypeStruct((HALO, GZ), F32),
            jax.ShapeDtypeStruct((HALO, GZ), F32),
            jax.ShapeDtypeStruct((2 * GZ, gaussians), BF16),
            jax.ShapeDtypeStruct((CORE, GZ), F32),
        ),
        in_specs=[VMEM] * len(arrays),
        out_specs=(VMEM,) * 4,
        scratch_shapes=[
            pltpu.VMEM((num_col * num_layer * LANES, arrays[0].shape[-1]), BF16),
            pltpu.VMEM((2 * HALO, gaussians), BF16),
            pltpu.VMEM((2 * HALO, gaussians), BF16),
            pltpu.VMEM((FULL, UNIT), BF16),
            pltpu.VMEM((FULL, UNIT), BF16),
            pltpu.VMEM((2 * GZ, UNIT), BF16),
            pltpu.VMEM((FULL, GZ), F32),
        ],
        compiler_params=PARAMS,
        cost_estimate=pl.CostEstimate(flops=3_000_000_000, bytes_accessed=1_000_000, transcendentals=0),
        name="rims",
    )(*arrays)


def core_kernel(num_col, num_layer, refs_in, *refs):
    blocks = Blocks(refs[:refs_in], num_col, num_layer)
    depth, extra, core_ref, planeh, planel = refs[refs_in:]
    for at, (which, pair) in enumerate(blocks.units()):
        set_planes(blocks, blocks.unit(which, pair), which, CORE_X, at, planeh, planel)
    core_ref[...] = summed(planeh[...], planel[...], depth[...])

    @pl.when(jnp.max(blocks.over()) > 0)
    def _():
        core_ref[...] += extra[...]


def core_part(arrays, depth, extra, num_col, num_layer):
    gaussians = depth.shape[1]
    return pl.pallas_call(
        functools.partial(core_kernel, num_col, num_layer, len(arrays)),
        out_shape=jax.ShapeDtypeStruct((CORE, GZ), F32),
        in_specs=[VMEM] * (len(arrays) + 2),
        out_specs=VMEM,
        scratch_shapes=[pltpu.VMEM((CORE, gaussians), BF16), pltpu.VMEM((CORE, gaussians), BF16)],
        compiler_params=PARAMS,
        cost_estimate=pl.CostEstimate(flops=1_500_000_000, bytes_accessed=1_000_000, transcendentals=0),
        name="core",
    )(*arrays, depth, extra)


def product_kernel(num_row, num_col, num_layer, refs_in, *refs):
    blocks = Blocks(refs[:refs_in], num_col, num_layer)
    h_refs = refs[refs_in : refs_in + num_row]
    out_ref, token_ref, slab = refs[refs_in + num_row :]
    token_ref[...] = jnp.zeros_like(token_ref)
    row = lax.axis_index("row")
    rows = h_refs[0].shape[1]
    for back in range(num_layer):
        for step in range(num_row):
            start = pl.multiple_of((row ^ step) * rows, rows)
            slab[back, pl.ds(start, rows), :] = h_refs[step][back]
    total = jnp.zeros(out_ref.shape, F32)
    for back in range(num_layer):
        for piece in range(num_col):
            if blocks.paired:
                left = blocks.matrix(piece * 4 + back)
                start = pl.multiple_of((blocks.col ^ piece) * LANES, LANES)
            else:
                source = lax.rem(blocks.layer - back + num_layer, num_layer)
                left = blocks.slab(source, piece)
                start = piece * LANES
            right = slab[back, pl.ds(start, LANES), :]
            total += lax.dot_general(left, right, TN, preferred_element_type=F32)
    out_ref[...] = total.astype(BF16)


def multiply(arrays, parts, num_row, num_col, num_layer):
    return pl.pallas_call(
        functools.partial(product_kernel, num_row, num_col, num_layer, len(arrays)),
        out_shape=(
            jax.ShapeDtypeStruct((arrays[0].shape[-1], LANES), BF16),
            jax.ShapeDtypeStruct((8, LANES), F32),
        ),
        in_specs=[VMEM] * (num_row + len(arrays)),
        out_specs=(VMEM, VMEM),
        scratch_shapes=[pltpu.VMEM((num_layer, num_col * LANES, LANES), BF16)],
        compiler_params=PARAMS,
        cost_estimate=pl.CostEstimate(flops=500_000_000, bytes_accessed=1_000_000, transcendentals=0),
        name="multiply",
    )(*arrays, *parts)


def settle_kernel(block_ref, out_ref):
    out_ref[...] = block_ref[...]


def settle(block):
    return pl.pallas_call(
        settle_kernel,
        out_shape=jax.ShapeDtypeStruct(block.shape, BF16),
        in_specs=[VMEM],
        out_specs=VMEM,
        compiler_params=PARAMS,
        cost_estimate=pl.CostEstimate(flops=1000, bytes_accessed=1000, transcendentals=0),
        name="settle",
    )(block)


def stack_kernel(own_ref, near_ref, far_ref, both_ref, out_ref):
    out_ref[0] = own_ref[BASE:, LANES:UNIT]
    out_ref[1] = near_ref[BASE:, 0:LANES]
    out_ref[2] = far_ref[BASE:, 0:LANES]
    out_ref[3] = both_ref[BASE:, LANES:UNIT]


def stack(own, near, far, both):
    return pl.pallas_call(
        stack_kernel,
        out_shape=jax.ShapeDtypeStruct((4, own.shape[0] - BASE, LANES), BF16),
        in_specs=[VMEM] * 4,
        out_specs=VMEM,
        compiler_params=PARAMS,
        name="stack",
    )(own, near, far, both)


def fold_kernel(core_ref, below_ref, above_ref, after_ref, out_ref):
    out_ref[0:HALO, :] = core_ref[0:HALO, :] + below_ref[...]
    out_ref[HALO : CORE - HALO, :] = core_ref[HALO : CORE - HALO, :]
    out_ref[CORE - HALO : CORE, :] = core_ref[CORE - HALO : CORE, :] + above_ref[...]


def fold(core, below, above, after):
    return pl.pallas_call(
        fold_kernel,
        out_shape=jax.ShapeDtypeStruct((CORE, GZ), F32),
        in_specs=[VMEM] * 4,
        out_specs=VMEM,
        compiler_params=PARAMS,
        cost_estimate=pl.CostEstimate(flops=1_000_000, bytes_accessed=400_000, transcendentals=0),
        name="fold",
    )(core, below, above, after)


def shifted(value, axis, count, step):
    return lax.ppermute(value, axis, [(i, (i + step) % count) for i in range(count)])


def crossed(value, col_bit, layer_bits):
    pairs = [(c * 4 + l, (c ^ col_bit) * 4 + (l ^ layer_bits)) for c in range(2) for l in range(4)]
    return lax.ppermute(value, ("col", "layer"), pairs)


def gather_paired(base, tall_y, tall_core):
    got_x = crossed(base, 1, 0)
    got_y = crossed(tall_y, 0, 2)
    got_xy = crossed(base, 1, 2)
    near = crossed(tall_core, 0, 1)
    near_x = crossed(got_x, 0, 1)
    near_y = crossed(got_y, 0, 1)
    near_xy = crossed(got_xy, 0, 1)
    return [tall_core, near, got_y, near_y, got_x, near_x, got_xy, near_xy]


def on_device(p_slabs, p_mask, h_slabs, h_mask, gauss_row, gauss_col, gauss_cell, gauss_expo, gauss_pref):
    num_row, num_col, num_layer = (lax.axis_size(axis) for axis in ("row", "col", "layer"))
    paired = num_col == 2 and num_layer == 4
    flat = [x.reshape(8, LANES) for x in (gauss_row, gauss_col, gauss_cell, gauss_expo, gauss_pref)]
    made = prepare(paired, p_slabs[0], p_mask[0].T, h_slabs[0], h_mask[0], *flat)
    if paired:
        arrays = gather_paired(*made[:2], settle(made[2]))
        mine = stack(*arrays[:4])
    else:
        base, pieces = made
        arrays = [lax.all_gather(base, ("layer", "col"), axis=0)]
        mine = [pieces[0]] + [shifted(pieces[step], "layer", num_layer, step) for step in range(1, num_layer)]
        mine = jnp.stack(mine)
    low, high, depth, extra = rims(arrays, num_col, num_layer)
    parts = [mine] + [
        lax.ppermute(mine, "row", [(i, i ^ step) for i in range(num_row)]) for step in range(1, num_row)
    ]
    below = shifted(high, "row", num_row, 1)
    above = shifted(low, "row", num_row, num_row - 1)
    core = core_part(arrays, depth, extra, num_col, num_layer)
    product, token = multiply(arrays, parts, num_row, num_col, num_layer)
    density = fold(core, below, above, token).reshape(GX, GY, GZ)
    return (product, density)


def solution(mesh):
    placed = (P("layer", "row", "col"),) * 4 + (P(("row", "col", "layer")),) * 5
    return jax.shard_map(
        on_device,
        mesh=mesh,
        in_specs=placed,
        out_specs=(P("row", ("col", "layer")), P("row", "col", "layer")),
        check_vma=False,
    )
```

```python
import functools

import jax
import jax.numpy as jnp
from jax import lax
from jax.experimental import pallas as pl
from jax.experimental.pallas import tpu as pltpu
from jax.sharding import PartitionSpec as P

BS = 32
GX = 16
GY = 16
GZ = 128
R = 4
LANES = 128
F32 = jnp.float32
BF16 = jnp.bfloat16
HALO = R * GY
CORE = GX * GY
FULL = CORE + 2 * HALO
UNIT = 2 * LANES
PAIRS = 4
META = (PAIRS + 1) * 16
BASE = LANES + META
FLAG = 12
VMEM = pl.BlockSpec(memory_space=pltpu.VMEM)
HBM = pl.BlockSpec(memory_space=pltpu.HBM)
PARAMS = pltpu.CompilerParams(vmem_limit_bytes=40 * 1024 * 1024)
NT = (((1,), (1,)), ((), ()))
TN = (((0,), (0,)), ((), ()))


def iota(shape, axis):
    return lax.broadcasted_iota(jnp.int32, shape, axis).astype(F32)


def split3(value):
    first = value.astype(BF16).astype(F32)
    rest = value - first
    second = rest.astype(BF16).astype(F32)
    return first, second, rest - second


def masked(values, bits):
    lane = lax.broadcasted_iota(jnp.int32, values.shape, 1) // BS
    keep = jnp.zeros(values.shape, jnp.int32)
    for piece, bit in enumerate(bits):
        keep = jnp.where(lane == piece, bit, keep)
    return jnp.where(keep > 0, values.astype(F32), 0.0)


def ranks(flags):
    up = (iota((LANES, LANES), 0) <= iota((LANES, LANES), 1)).astype(F32).astype(BF16)
    ones = jnp.ones((LANES, LANES), BF16)
    within = jnp.dot(flags.astype(BF16), up, preferred_element_type=F32)
    totals = jnp.dot(flags.astype(BF16), ones, preferred_element_type=F32)
    row, other = iota((16, 16), 0), iota((16, 16), 1)
    same = (row < 8) == (other < 8)
    before = jnp.where(same & (other < row), 1.0, 0.0).astype(BF16)
    every = jnp.where(same, 1.0, 0.0).astype(BF16)
    earlier = jnp.dot(before, totals.astype(BF16), preferred_element_type=F32)
    count = jnp.dot(every, totals.astype(BF16), preferred_element_type=F32)
    return jnp.where(flags > 0, within + earlier - 1.0, -1.0), count


def h_piece(h_ref, hm_ref, chunk):
    pieces = LANES // BS
    out = []
    for block in range(h_ref.shape[0] // BS):
        bits = [hm_ref[block, chunk * pieces + at] for at in range(pieces)]
        value = h_ref[pl.ds(block * BS, BS), pl.ds(pl.multiple_of(chunk * LANES, LANES), LANES)]
        out.append(masked(value, bits).astype(BF16))
    return jnp.concatenate(out, axis=0)


def prepare_kernel(paired, *refs):
    sources, outs, refs = refs[:9], refs[9:-14], refs[-14:]
    landed, (tmp, fields, matrix, onehot, sems) = refs[:9], refs[9:]
    copies = [pltpu.make_async_copy(src, dst, sems.at[at]) for at, (src, dst) in enumerate(zip(sources, landed))]
    for copy in copies:
        copy.start()
    for copy in copies:
        copy.wait()
    p_ref, pm_ref, h_ref, hm_ref, row_ref, col_ref, cell_ref, expo_ref, pref_ref = landed
    layer = lax.axis_index("layer")
    count = lax.axis_size("layer")
    band = p_ref.shape[0]
    for block in range(band // BS):
        rows = pl.ds(block * BS, BS)
        tmp[rows, :] = masked(p_ref[rows, :], [pm_ref[piece, block] for piece in range(LANES // BS)])
    turned = tmp[...].T.astype(BF16)
    col = col_ref[...]
    cell = cell_ref[...]
    cell_z = (cell % GZ).astype(F32)
    values = [
        row_ref[...].astype(F32),
        (col // LANES).astype(F32),
        (col % LANES).astype(F32),
        (cell // (GY * GZ)).astype(F32),
        (cell // GZ % GY).astype(F32),
        cell_z,
        *split3(expo_ref[...]),
        *split3(pref_ref[...]),
    ]
    for index in range(16):
        fields[8 * index : 8 * index + 8, :] = values[index] if index < len(values) else jnp.zeros((8, LANES), F32)
    tiles = [fields[pl.ds(part, 16, stride=8), :].astype(BF16) for part in range(2 * PAIRS)]
    for part in range(2 * PAIRS):
        matrix[:, part * LANES : part * LANES + LANES] = tiles[part]
    faces = jnp.concatenate([jnp.where(cell_z < R, 1.0, 0.0), jnp.where(cell_z >= GZ - R, 1.0, 0.0)], axis=0)
    place, many = ranks(faces)
    slot = iota((LANES, LANES), 0)
    for part in range(2 * PAIRS):
        lanes = pl.ds(part * LANES, LANES)
        for face in range(2):
            hit = slot == place[face * 8 + part : face * 8 + part + 1, :]
            onehot[face * LANES : face * LANES + LANES, lanes] = jnp.where(hit, 1.0, 0.0).astype(BF16)
    listed = lax.dot_general(matrix[...], onehot[...], NT, preferred_element_type=F32)
    over = jnp.where(jnp.max(many, axis=0, keepdims=True) > LANES, 1.0, 0.0)
    over = jnp.concatenate([over, over], axis=1)
    listed = jnp.where(iota(listed.shape, 0) == FLAG, over, listed).astype(BF16)
    copies = outs[:3] if paired else outs[:1]
    for out in copies:
        out[0:LANES, :] = turned
        for pair in range(PAIRS):
            out[LANES + 16 * pair : LANES + 16 * pair + 16, :] = matrix[:, pair * UNIT : pair * UNIT + UNIT]
        out[LANES + 16 * PAIRS : BASE, :] = listed

    def piece(chunk):
        return h_piece(h_ref, hm_ref, chunk)

    if paired:
        outs[1][BASE:, 0:LANES] = piece(layer ^ 2)
        outs[1][BASE:, LANES:UNIT] = piece(layer ^ 3)
        outs[2][BASE:, 0:LANES] = piece(layer ^ 1)
        outs[2][BASE:, LANES:UNIT] = piece(layer)
    else:
        for back in range(h_ref.shape[1] // LANES):
            outs[1][back] = piece(lax.rem(layer + back, count))


def prepare(paired, p, p_mask, h, h_mask, *gauss):
    band = p.shape[0]
    base = jax.ShapeDtypeStruct((BASE, band), BF16)
    tall = jax.ShapeDtypeStruct((BASE + h.shape[0], band), BF16)
    if paired:
        outs = (base, tall, tall)
    else:
        outs = (base, jax.ShapeDtypeStruct((h.shape[1] // LANES, h.shape[0], LANES), BF16))
    return pl.pallas_call(
        functools.partial(prepare_kernel, paired),
        out_shape=outs,
        in_specs=[HBM] * 9,
        out_specs=(VMEM,) * len(outs),
        scratch_shapes=[
            pltpu.VMEM(p.shape, p.dtype),
            pltpu.SMEM(p_mask.shape, p_mask.dtype),
            pltpu.VMEM(h.shape, h.dtype),
            pltpu.SMEM(h_mask.shape, h_mask.dtype),
            *[pltpu.VMEM(x.shape, x.dtype) for x in gauss],
            pltpu.VMEM(p.shape, F32),
            pltpu.VMEM((16 * 8, LANES), F32),
            pltpu.VMEM((16, 2 * PAIRS * LANES), BF16),
            pltpu.VMEM((UNIT, 2 * PAIRS * LANES), BF16),
            pltpu.SemaphoreType.DMA((9,)),
        ],
        compiler_params=pltpu.CompilerParams(vmem_limit_bytes=62 * 1024 * 1024),
        name="prepare",
    )(p, p_mask, h, h_mask, *gauss)


class Blocks:
    def __init__(self, refs, num_col, num_layer):
        self.refs = refs
        self.num_col, self.num_layer = num_col, num_layer
        self.paired = len(refs) > 1
        self.col, self.layer = lax.axis_index("col"), lax.axis_index("layer")
        self.total = num_col * num_layer
        self.col_shifts = [0, 1] if num_col == 2 else [0, -1, 1]

    def ident(self, index):
        if not self.paired:
            return index
        return (self.layer ^ (index % 4)) * 2 + (self.col ^ (index // 4))

    def matrix(self, index):
        return self.refs[index][0:LANES, :] if self.paired else self.refs[0][index, 0:LANES, :]

    def slab(self, layer, piece):
        index = layer * self.num_col + piece
        return self.refs[0][index, 0:LANES, :]

    def tile(self, which, side, pair):
        rows = pl.ds(LANES + 16 * pair, 16)
        if self.paired:
            return self.refs[which * 4 + side][rows, :].astype(F32)
        shift_l = 0 if side == 0 else (1 if side == 1 else -1)
        index = lax.rem(self.layer + shift_l + self.num_layer, self.num_layer) * self.num_col
        index += lax.rem(self.col + self.col_shifts[which] + self.num_col, self.num_col)
        return self.refs[0][index, rows, :].astype(F32)

    def side_shift(self, side):
        if self.paired:
            even = (self.layer % 2) == 0
            return jnp.where(even, 1.0, -1.0) if side == 1 else jnp.where(even, -1.0, 1.0)
        return 1.0 if side == 1 else -1.0

    def sides(self):
        return (1, 3) if self.paired else (1, 2)

    def units(self):
        return [(which, pair) for which in range(len(self.col_shifts)) for pair in range(PAIRS + 1)]

    def listed(self, which):
        halves = []
        for side in self.sides():
            both = self.tile(which, side, PAIRS)
            upward = self.side_shift(side) > 0
            halves.append(jnp.where(upward, both[:, 0:LANES], both[:, LANES:UNIT]))
        return jnp.concatenate(halves, axis=1)

    def unit(self, which, pair):
        return self.tile(which, 0, pair) if pair < PAIRS else self.listed(which)

    def lifts(self, pair):
        if pair < PAIRS:
            return 0.0
        lane = iota((1, UNIT), 1)
        first, second = self.sides()
        return jnp.where(lane < LANES, self.side_shift(first), self.side_shift(second)) * float(GZ)

    def over(self):
        flags = [
            self.tile(which, side, PAIRS)[FLAG : FLAG + 1, :]
            for which in range(len(self.col_shifts))
            for side in self.sides()
        ]
        return functools.reduce(jnp.maximum, flags)

    def long_steps(self):
        return [(which, side) for which in range(len(self.col_shifts)) for side in self.sides()]


def weigh(blocks, whole, tile):
    band = whole.shape[1]
    onehot = jnp.where(iota((band, UNIT), 0) == tile[0:1, :], 1.0, 0.0).astype(BF16)
    found = jnp.dot(whole[...], onehot, preferred_element_type=F32)
    picked = jnp.zeros((LANES, UNIT), F32)
    for index in range(blocks.total):
        mine = tile[1:2, :] == jnp.asarray(blocks.ident(index)).astype(F32)
        picked = jnp.where(mine, found[index * LANES : index * LANES + LANES, :], picked)
    value = jnp.sum(jnp.where(iota((LANES, UNIT), 0) == tile[2:3, :], picked, 0.0), axis=0, keepdims=True)
    return (tile[9:10, :] + tile[10:11, :] + tile[11:12, :]) * value


def bell(dist, expo):
    square = dist * dist
    return jnp.where(square < (R + 0.5) ** 2, jnp.exp(-expo * square), 0.0)


RIM_X = tuple(range(R)) + tuple(range(GX + R, GX + 2 * R))
CORE_X = tuple(range(R, GX + R))
ALL_X = tuple(range(GX + 2 * R))


def decay(tile):
    return tile[6:7, :] + tile[7:8, :] + tile[8:9, :]


def shapes_x(tile):
    return bell(iota((GX + 2 * R, UNIT), 0) - float(R) - tile[3:4, :], decay(tile))


def shapes_y(tile, shift, wraps):
    dy = iota((GY, UNIT), 0) - tile[4:5, :] - float(shift * GY)
    if wraps:
        dy = jnp.where(dy < -float(GY), dy + 2.0 * GY, dy)
    return bell(dy, decay(tile))


def shapes_z(tile, lift):
    return bell(iota((GZ, UNIT), 0) - tile[5:6, :] - lift, decay(tile))


def fill_planes(ex, ey, places, at, planeh, planel):
    lanes = pl.ds(at * UNIT, UNIT)
    for spot, x in enumerate(places):
        plane = ex[x : x + 1, :] * ey
        plane_hi = plane.astype(BF16)
        planeh[spot * GY : spot * GY + GY, lanes] = plane_hi
        planel[spot * GY : spot * GY + GY, lanes] = (plane - plane_hi.astype(F32)).astype(BF16)


def fill_depth(ez, coef, at, depth):
    weighed = ez * coef
    lanes = pl.ds(at * UNIT, UNIT)
    weighed_hi = weighed.astype(BF16)
    depth[0:GZ, lanes] = weighed_hi
    depth[GZ : 2 * GZ, lanes] = (weighed - weighed_hi.astype(F32)).astype(BF16)


def set_planes(blocks, tile, which, places, at, planeh, planel):
    wraps = blocks.num_col == 2 and which == 1
    fill_planes(shapes_x(tile), shapes_y(tile, blocks.col_shifts[which], wraps), places, at, planeh, planel)


def summed(planeh, planel, depth):
    first = lax.dot_general(planeh, depth, NT, preferred_element_type=F32)
    second = lax.dot_general(planel, depth[0:GZ, :], NT, preferred_element_type=F32)
    return first[:, 0:GZ] + first[:, GZ : 2 * GZ] + second


def rims_kernel(num_col, num_layer, refs_in, *refs):
    blocks = Blocks(refs[:refs_in], num_col, num_layer)
    low_ref, high_ref, depth, extra, whole, planeh, planel, longh, longl, long_depth, acc = refs[refs_in:]
    for index in range(blocks.total):
        whole[index * LANES : index * LANES + LANES, :] = blocks.matrix(index)
    over = blocks.over()
    for at, (which, pair) in enumerate(blocks.units()):
        tile = blocks.unit(which, pair)
        coef = weigh(blocks, whole, tile)
        if pair == PAIRS:
            coef = jnp.where(over > 0, 0.0, coef)
        set_planes(blocks, tile, which, RIM_X, at, planeh, planel)
        fill_depth(shapes_z(tile, blocks.lifts(pair)), coef, at, depth)
    total = summed(planeh[...], planel[...], depth[...])
    swap = lax.rem(lax.axis_index("row"), 2) * int(lax.axis_size("row") == 4)

    def put(low, high, base_low, base_high):
        low_ref[...] = jnp.where(swap > 0, high, low) + base_low
        high_ref[...] = jnp.where(swap > 0, low, high) + base_high

    put(total[0:HALO, :], total[HALO:, :], 0.0, 0.0)

    @pl.when(jnp.max(over) > 0)
    def _():
        acc[...] = jnp.zeros_like(acc)
        for which, side in blocks.long_steps():

            def step(pair, carry):
                tile = blocks.tile(which, side, pair)
                lift = blocks.side_shift(side) * float(GZ)
                set_planes(blocks, tile, which, ALL_X, 0, longh, longl)
                fill_depth(shapes_z(tile, lift), weigh(blocks, whole, tile), 0, long_depth)
                acc[...] += summed(longh[...], longl[...], long_depth[...])
                return carry

            lax.fori_loop(0, PAIRS, step, 0)
        put(acc[0:HALO, :], acc[HALO + CORE : FULL, :], low_ref[...], high_ref[...])
        extra[...] = acc[HALO : HALO + CORE, :]


def rims(arrays, num_col, num_layer):
    gaussians = (2 if num_col == 2 else 3) * (PAIRS + 1) * UNIT
    return pl.pallas_call(
        functools.partial(rims_kernel, num_col, num_layer, len(arrays)),
        out_shape=(
            jax.ShapeDtypeStruct((HALO, GZ), F32),
            jax.ShapeDtypeStruct((HALO, GZ), F32),
            jax.ShapeDtypeStruct((2 * GZ, gaussians), BF16),
            jax.ShapeDtypeStruct((CORE, GZ), F32),
        ),
        in_specs=[VMEM] * len(arrays),
        out_specs=(VMEM,) * 4,
        scratch_shapes=[
            pltpu.VMEM((num_col * num_layer * LANES, arrays[0].shape[-1]), BF16),
            pltpu.VMEM((2 * HALO, gaussians), BF16),
            pltpu.VMEM((2 * HALO, gaussians), BF16),
            pltpu.VMEM((FULL, UNIT), BF16),
            pltpu.VMEM((FULL, UNIT), BF16),
            pltpu.VMEM((2 * GZ, UNIT), BF16),
            pltpu.VMEM((FULL, GZ), F32),
        ],
        compiler_params=PARAMS,
        cost_estimate=pl.CostEstimate(flops=3_000_000_000, bytes_accessed=1_000_000, transcendentals=0),
        name="rims",
    )(*arrays)


def core_kernel(num_col, num_layer, refs_in, *refs):
    blocks = Blocks(refs[:refs_in], num_col, num_layer)
    depth, extra, core_ref, planeh, planel = refs[refs_in:]
    for at, (which, pair) in enumerate(blocks.units()):
        set_planes(blocks, blocks.unit(which, pair), which, CORE_X, at, planeh, planel)
    core_ref[...] = summed(planeh[...], planel[...], depth[...])

    @pl.when(jnp.max(blocks.over()) > 0)
    def _():
        core_ref[...] += extra[...]


def core_part(arrays, depth, extra, num_col, num_layer):
    gaussians = depth.shape[1]
    return pl.pallas_call(
        functools.partial(core_kernel, num_col, num_layer, len(arrays)),
        out_shape=jax.ShapeDtypeStruct((CORE, GZ), F32),
        in_specs=[VMEM] * (len(arrays) + 2),
        out_specs=VMEM,
        scratch_shapes=[pltpu.VMEM((CORE, gaussians), BF16), pltpu.VMEM((CORE, gaussians), BF16)],
        compiler_params=PARAMS,
        cost_estimate=pl.CostEstimate(flops=1_500_000_000, bytes_accessed=1_000_000, transcendentals=0),
        name="core",
    )(*arrays, depth, extra)


def product_kernel(num_row, num_col, num_layer, refs_in, *refs):
    blocks = Blocks(refs[:refs_in], num_col, num_layer)
    h_refs = refs[refs_in : refs_in + num_row]
    out_ref, token_ref, slab = refs[refs_in + num_row :]
    token_ref[...] = jnp.zeros_like(token_ref)
    row = lax.axis_index("row")
    rows = h_refs[0].shape[1]
    for back in range(num_layer):
        for step in range(num_row):
            start = pl.multiple_of((row ^ step) * rows, rows)
            slab[back, pl.ds(start, rows), :] = h_refs[step][back]
    total = jnp.zeros(out_ref.shape, F32)
    for back in range(num_layer):
        for piece in range(num_col):
            if blocks.paired:
                left = blocks.matrix(piece * 4 + back)
                start = pl.multiple_of((blocks.col ^ piece) * LANES, LANES)
            else:
                source = lax.rem(blocks.layer - back + num_layer, num_layer)
                left = blocks.slab(source, piece)
                start = piece * LANES
            right = slab[back, pl.ds(start, LANES), :]
            total += lax.dot_general(left, right, TN, preferred_element_type=F32)
    out_ref[...] = total.astype(BF16)


def multiply(arrays, parts, num_row, num_col, num_layer):
    return pl.pallas_call(
        functools.partial(product_kernel, num_row, num_col, num_layer, len(arrays)),
        out_shape=(
            jax.ShapeDtypeStruct((arrays[0].shape[-1], LANES), BF16),
            jax.ShapeDtypeStruct((8, LANES), F32),
        ),
        in_specs=[VMEM] * (num_row + len(arrays)),
        out_specs=(VMEM, VMEM),
        scratch_shapes=[pltpu.VMEM((num_layer, num_col * LANES, LANES), BF16)],
        compiler_params=PARAMS,
        cost_estimate=pl.CostEstimate(flops=500_000_000, bytes_accessed=1_000_000, transcendentals=0),
        name="multiply",
    )(*arrays, *parts)


def settle_kernel(block_ref, out_ref):
    out_ref[...] = block_ref[...]


def settle(block):
    return pl.pallas_call(
        settle_kernel,
        out_shape=jax.ShapeDtypeStruct(block.shape, BF16),
        in_specs=[VMEM],
        out_specs=VMEM,
        compiler_params=PARAMS,
        cost_estimate=pl.CostEstimate(flops=1000, bytes_accessed=1000, transcendentals=0),
        name="settle",
    )(block)


def stack_kernel(own_ref, near_ref, far_ref, both_ref, out_ref):
    out_ref[0] = own_ref[BASE:, LANES:UNIT]
    out_ref[1] = near_ref[BASE:, 0:LANES]
    out_ref[2] = far_ref[BASE:, 0:LANES]
    out_ref[3] = both_ref[BASE:, LANES:UNIT]


def stack(own, near, far, both):
    return pl.pallas_call(
        stack_kernel,
        out_shape=jax.ShapeDtypeStruct((4, own.shape[0] - BASE, LANES), BF16),
        in_specs=[VMEM] * 4,
        out_specs=VMEM,
        compiler_params=PARAMS,
        name="stack",
    )(own, near, far, both)


def fold_kernel(core_ref, below_ref, above_ref, after_ref, out_ref):
    swap = lax.rem(lax.axis_index("row"), 2) * int(lax.axis_size("row") == 4)
    below, above = below_ref[...], above_ref[...]
    out_ref[0:HALO, :] = core_ref[0:HALO, :] + jnp.where(swap > 0, above, below)
    out_ref[HALO : CORE - HALO, :] = core_ref[HALO : CORE - HALO, :]
    out_ref[CORE - HALO : CORE, :] = core_ref[CORE - HALO : CORE, :] + jnp.where(swap > 0, below, above)


def fold(core, below, above, after):
    return pl.pallas_call(
        fold_kernel,
        out_shape=jax.ShapeDtypeStruct((CORE, GZ), F32),
        in_specs=[VMEM] * 4,
        out_specs=VMEM,
        compiler_params=PARAMS,
        cost_estimate=pl.CostEstimate(flops=1_000_000, bytes_accessed=400_000, transcendentals=0),
        name="fold",
    )(core, below, above, after)


def shifted(value, axis, count, step):
    return lax.ppermute(value, axis, [(i, (i + step) % count) for i in range(count)])


def crossed(value, col_bit, layer_bits):
    pairs = [(c * 4 + l, (c ^ col_bit) * 4 + (l ^ layer_bits)) for c in range(2) for l in range(4)]
    return lax.ppermute(value, ("col", "layer"), pairs)


def gather_paired(base, tall_y, tall_core):
    got_x = crossed(base, 1, 0)
    got_y = crossed(tall_y, 0, 2)
    got_xy = crossed(base, 1, 2)
    near = crossed(tall_core, 0, 1)
    near_x = crossed(got_x, 0, 1)
    near_y = crossed(got_y, 0, 1)
    near_xy = crossed(got_xy, 0, 1)
    return [tall_core, near, got_y, near_y, got_x, near_x, got_xy, near_xy]


def on_device(p_slabs, p_mask, h_slabs, h_mask, gauss_row, gauss_col, gauss_cell, gauss_expo, gauss_pref):
    num_row, num_col, num_layer = (lax.axis_size(axis) for axis in ("row", "col", "layer"))
    paired = num_col == 2 and num_layer == 4
    flat = [x.reshape(8, LANES) for x in (gauss_row, gauss_col, gauss_cell, gauss_expo, gauss_pref)]
    made = prepare(paired, p_slabs[0], p_mask[0].T, h_slabs[0], h_mask[0], *flat)
    if paired:
        arrays = gather_paired(*made[:2], settle(made[2]))
        mine = stack(*arrays[:4])
    else:
        base, pieces = made
        arrays = [lax.all_gather(base, ("layer", "col"), axis=0)]
        mine = [pieces[0]] + [shifted(pieces[step], "layer", num_layer, step) for step in range(1, num_layer)]
        mine = jnp.stack(mine)
    low, high, depth, extra = rims(arrays, num_col, num_layer)
    parts = [mine] + [
        lax.ppermute(mine, "row", [(i, i ^ step) for i in range(num_row)]) for step in range(1, num_row)
    ]
    if num_row == 4:
        below = lax.ppermute(low, "row", [(i, i ^ 3) for i in range(4)])
        above = lax.ppermute(high, "row", [(i, i ^ 1) for i in range(4)])
    else:
        below = shifted(high, "row", num_row, 1)
        above = shifted(low, "row", num_row, num_row - 1)
    core = core_part(arrays, depth, extra, num_col, num_layer)
    product, token = multiply(arrays, parts, num_row, num_col, num_layer)
    density = fold(core, below, above, token).reshape(GX, GY, GZ)
    return (product, density)


def solution(mesh):
    placed = (P("layer", "row", "col"),) * 4 + (P(("row", "col", "layer")),) * 5
    return jax.shard_map(
        on_device,
        mesh=mesh,
        in_specs=placed,
        out_specs=(P("row", ("col", "layer")), P("row", "col", "layer")),
        check_vma=False,
    )
```

```python
import functools

import jax
import jax.numpy as jnp
from jax import lax
from jax.experimental import pallas as pl
from jax.experimental.pallas import tpu as pltpu
from jax.sharding import PartitionSpec as P

BS = 32
GX = 16
GY = 16
GZ = 128
R = 4
LANES = 128
F32 = jnp.float32
BF16 = jnp.bfloat16
HALO = R * GY
CORE = GX * GY
FULL = CORE + 2 * HALO
UNIT = 2 * LANES
PAIRS = 4
META = (PAIRS // 2 + 1) * 16
BASE = LANES + META
FLAG = 8
FIELDS = 8
VMEM = pl.BlockSpec(memory_space=pltpu.VMEM)
HBM = pl.BlockSpec(memory_space=pltpu.HBM)
PARAMS = pltpu.CompilerParams(vmem_limit_bytes=40 * 1024 * 1024)
NT = (((1,), (1,)), ((), ()))
TN = (((0,), (0,)), ((), ()))


def iota(shape, axis):
    return lax.broadcasted_iota(jnp.int32, shape, axis).astype(F32)


def split2(value):
    first = value.astype(BF16).astype(F32)
    return first, value - first


class Gaussians:
    def __init__(self, tile):
        first, second, third, fourth = (tile[at : at + 1, :].astype(jnp.int32) for at in range(4))
        first, second, third = first + 256, second + 256, third + 256
        column = third + ((fourth >> 7) << 9) + ((second >> 8) << 10) + ((first >> 8) << 11)
        cell = second & 255
        self.row = (first & 255).astype(F32)
        self.block = (column // LANES).astype(F32)
        self.lane = (column % LANES).astype(F32)
        self.x = (cell // GY).astype(F32)
        self.y = (cell % GY).astype(F32)
        self.z = (fourth & 127).astype(F32)
        self.expo = tile[4:5, :] + tile[5:6, :]
        self.pref = tile[6:7, :] + tile[7:8, :]


def masked(values, bits):
    lane = lax.broadcasted_iota(jnp.int32, values.shape, 1) // BS
    keep = jnp.zeros(values.shape, jnp.int32)
    for piece, bit in enumerate(bits):
        keep = jnp.where(lane == piece, bit, keep)
    return jnp.where(keep > 0, values.astype(F32), 0.0)


def ranks(flags):
    up = (iota((LANES, LANES), 0) <= iota((LANES, LANES), 1)).astype(F32).astype(BF16)
    ones = jnp.ones((LANES, LANES), BF16)
    within = jnp.dot(flags.astype(BF16), up, preferred_element_type=F32)
    totals = jnp.dot(flags.astype(BF16), ones, preferred_element_type=F32)
    row, other = iota((16, 16), 0), iota((16, 16), 1)
    same = (row < 8) == (other < 8)
    before = jnp.where(same & (other < row), 1.0, 0.0).astype(BF16)
    every = jnp.where(same, 1.0, 0.0).astype(BF16)
    earlier = jnp.dot(before, totals.astype(BF16), preferred_element_type=F32)
    count = jnp.dot(every, totals.astype(BF16), preferred_element_type=F32)
    return jnp.where(flags > 0, within + earlier - 1.0, -1.0), count


def h_piece(h_ref, hm_ref, chunk):
    pieces = LANES // BS
    out = []
    for block in range(h_ref.shape[0] // BS):
        bits = [hm_ref[block, chunk * pieces + at] for at in range(pieces)]
        value = h_ref[pl.ds(block * BS, BS), pl.ds(pl.multiple_of(chunk * LANES, LANES), LANES)]
        out.append(masked(value, bits).astype(BF16))
    return jnp.concatenate(out, axis=0)


def prepare_kernel(paired, *refs):
    sources, outs, refs = refs[:9], refs[9:-14], refs[-14:]
    landed, (tmp, fields, matrix, onehot, sems) = refs[:9], refs[9:]
    copies = [pltpu.make_async_copy(src, dst, sems.at[at]) for at, (src, dst) in enumerate(zip(sources, landed))]
    for copy in copies:
        copy.start()
    for copy in copies:
        copy.wait()
    p_ref, pm_ref, h_ref, hm_ref, row_ref, col_ref, cell_ref, expo_ref, pref_ref = landed
    layer = lax.axis_index("layer")
    count = lax.axis_size("layer")
    band = p_ref.shape[0]
    for block in range(band // BS):
        rows = pl.ds(block * BS, BS)
        tmp[rows, :] = masked(p_ref[rows, :], [pm_ref[piece, block] for piece in range(LANES // BS)])
    turned = tmp[...].T.astype(BF16)
    col = col_ref[...]
    cell = cell_ref[...]
    cell_z = (cell % GZ).astype(F32)
    values = [
        (row_ref[...] + ((col >> 11) & 1) * 256 - 256).astype(F32),
        (cell // GZ + ((col >> 10) & 1) * 256 - 256).astype(F32),
        ((col & 511) - 256).astype(F32),
        (cell % GZ + ((col >> 9) & 1) * 128).astype(F32),
        *split2(expo_ref[...]),
        *split2(pref_ref[...]),
    ]
    for index in range(FIELDS):
        fields[8 * index : 8 * index + 8, :] = values[index]
    for part in range(2 * PAIRS):
        matrix[0:FIELDS, part * LANES : part * LANES + LANES] = fields[pl.ds(part, FIELDS, stride=8), :]
    matrix[FIELDS : 2 * FIELDS, :] = jnp.zeros((FIELDS, 2 * PAIRS * LANES), F32)
    faces = jnp.concatenate([jnp.where(cell_z < R, 1.0, 0.0), jnp.where(cell_z >= GZ - R, 1.0, 0.0)], axis=0)
    place, many = ranks(faces)
    slot = iota((LANES, LANES), 0)
    for part in range(2 * PAIRS):
        lanes = pl.ds(part * LANES, LANES)
        for face in range(2):
            hit = slot == place[face * 8 + part : face * 8 + part + 1, :]
            onehot[face * LANES : face * LANES + LANES, lanes] = jnp.where(hit, 1.0, 0.0).astype(BF16)
    listed = lax.dot_general(matrix[...].astype(BF16), onehot[...], NT, preferred_element_type=F32)
    over = jnp.where(jnp.max(many, axis=0, keepdims=True) > LANES, 1.0, 0.0)
    over = jnp.concatenate([over, over], axis=1)
    listed = jnp.where(iota(listed.shape, 0) == FLAG, over, listed).astype(BF16)
    copies = outs[:3] if paired else outs[:1]
    for out in copies:
        out[0:LANES, :] = turned
        for at in range(PAIRS // 2):
            halves = [matrix[0:FIELDS, pair * UNIT : pair * UNIT + UNIT] for pair in (2 * at, 2 * at + 1)]
            out[LANES + 16 * at : LANES + 16 * at + 16, :] = jnp.concatenate(halves, axis=0).astype(BF16)
        out[LANES + 8 * PAIRS : BASE, :] = listed

    def piece(chunk):
        return h_piece(h_ref, hm_ref, chunk)

    if paired:
        outs[1][BASE:, 0:LANES] = piece(layer ^ 2)
        outs[1][BASE:, LANES:UNIT] = piece(layer ^ 3)
        outs[2][BASE:, 0:LANES] = piece(layer ^ 1)
        outs[2][BASE:, LANES:UNIT] = piece(layer)
    else:
        for back in range(h_ref.shape[1] // LANES):
            outs[1][back] = piece(lax.rem(layer + back, count))


def prepare(paired, p, p_mask, h, h_mask, *gauss):
    band = p.shape[0]
    base = jax.ShapeDtypeStruct((BASE, band), BF16)
    tall = jax.ShapeDtypeStruct((BASE + h.shape[0], band), BF16)
    if paired:
        outs = (base, tall, tall)
    else:
        outs = (base, jax.ShapeDtypeStruct((h.shape[1] // LANES, h.shape[0], LANES), BF16))
    return pl.pallas_call(
        functools.partial(prepare_kernel, paired),
        out_shape=outs,
        in_specs=[HBM] * 9,
        out_specs=(VMEM,) * len(outs),
        scratch_shapes=[
            pltpu.VMEM(p.shape, p.dtype),
            pltpu.SMEM(p_mask.shape, p_mask.dtype),
            pltpu.VMEM(h.shape, h.dtype),
            pltpu.SMEM(h_mask.shape, h_mask.dtype),
            *[pltpu.VMEM(x.shape, x.dtype) for x in gauss],
            pltpu.VMEM(p.shape, F32),
            pltpu.VMEM((FIELDS * 8, LANES), F32),
            pltpu.VMEM((2 * FIELDS, 2 * PAIRS * LANES), F32),
            pltpu.VMEM((UNIT, 2 * PAIRS * LANES), BF16),
            pltpu.SemaphoreType.DMA((9,)),
        ],
        compiler_params=pltpu.CompilerParams(vmem_limit_bytes=62 * 1024 * 1024),
        name="prepare",
    )(p, p_mask, h, h_mask, *gauss)


class Blocks:
    def __init__(self, refs, num_col, num_layer):
        self.refs = refs
        self.num_col, self.num_layer = num_col, num_layer
        self.paired = len(refs) > 1
        self.col, self.layer = lax.axis_index("col"), lax.axis_index("layer")
        self.total = num_col * num_layer
        self.col_shifts = [0, 1] if num_col == 2 else [0, -1, 1]

    def ident(self, index):
        if not self.paired:
            return index
        return (self.layer ^ (index % 4)) * 2 + (self.col ^ (index // 4))

    def matrix(self, index):
        return self.refs[index][0:LANES, :] if self.paired else self.refs[0][index, 0:LANES, :]

    def slab(self, layer, piece):
        index = layer * self.num_col + piece
        return self.refs[0][index, 0:LANES, :]

    def tile(self, which, side, at):
        rows = pl.ds(LANES + 16 * at, 16)
        if self.paired:
            return self.refs[which * 4 + side][rows, :].astype(F32)
        shift_l = 0 if side == 0 else (1 if side == 1 else -1)
        index = lax.rem(self.layer + shift_l + self.num_layer, self.num_layer) * self.num_col
        index += lax.rem(self.col + self.col_shifts[which] + self.num_col, self.num_col)
        return self.refs[0][index, rows, :].astype(F32)

    def side_shift(self, side):
        if self.paired:
            even = (self.layer % 2) == 0
            return jnp.where(even, 1.0, -1.0) if side == 1 else jnp.where(even, -1.0, 1.0)
        return 1.0 if side == 1 else -1.0

    def sides(self):
        return (1, 3) if self.paired else (1, 2)

    def units(self):
        return [(which, pair) for which in range(len(self.col_shifts)) for pair in range(PAIRS + 1)]

    def listed(self, which):
        halves = []
        for side in self.sides():
            both = self.tile(which, side, PAIRS // 2)[0:FIELDS, :]
            upward = self.side_shift(side) > 0
            halves.append(jnp.where(upward, both[:, 0:LANES], both[:, LANES:UNIT]))
        return jnp.concatenate(halves, axis=1)

    def unit(self, which, pair):
        if pair == PAIRS:
            return Gaussians(self.listed(which))
        half = (pair % 2) * FIELDS
        return Gaussians(self.tile(which, 0, pair // 2)[half : half + FIELDS, :])

    def lifts(self, pair):
        if pair < PAIRS:
            return 0.0
        lane = iota((1, UNIT), 1)
        first, second = self.sides()
        return jnp.where(lane < LANES, self.side_shift(first), self.side_shift(second)) * float(GZ)

    def over(self):
        flags = [
            self.tile(which, side, PAIRS // 2)[FLAG : FLAG + 1, :]
            for which in range(len(self.col_shifts))
            for side in self.sides()
        ]
        return functools.reduce(jnp.maximum, flags)

    def long_steps(self):
        return [(which, side) for which in range(len(self.col_shifts)) for side in self.sides()]


def weigh(blocks, whole, tile):
    band = whole.shape[1]
    onehot = jnp.where(iota((band, UNIT), 0) == tile.row, 1.0, 0.0).astype(BF16)
    found = jnp.dot(whole[...], onehot, preferred_element_type=F32)
    picked = jnp.zeros((LANES, UNIT), F32)
    for index in range(blocks.total):
        mine = tile.block == jnp.asarray(blocks.ident(index)).astype(F32)
        picked = jnp.where(mine, found[index * LANES : index * LANES + LANES, :], picked)
    value = jnp.sum(jnp.where(iota((LANES, UNIT), 0) == tile.lane, picked, 0.0), axis=0, keepdims=True)
    return tile.pref * value


def bell(dist, expo):
    square = dist * dist
    return jnp.where(square < (R + 0.5) ** 2, jnp.exp(-expo * square), 0.0)


RIM_X = tuple(range(R)) + tuple(range(GX + R, GX + 2 * R))
CORE_X = tuple(range(R, GX + R))
ALL_X = tuple(range(GX + 2 * R))


def shapes_x(tile):
    return bell(iota((GX + 2 * R, UNIT), 0) - float(R) - tile.x, tile.expo)


def shapes_y(tile, shift, wraps):
    dy = iota((GY, UNIT), 0) - tile.y - float(shift * GY)
    if wraps:
        dy = jnp.where(dy < -float(GY), dy + 2.0 * GY, dy)
    return bell(dy, tile.expo)


def shapes_z(tile, lift):
    return bell(iota((GZ, UNIT), 0) - tile.z - lift, tile.expo)


def fill_planes(ex, ey, places, at, planeh, planel):
    lanes = pl.ds(at * UNIT, UNIT)
    for spot, x in enumerate(places):
        plane = ex[x : x + 1, :] * ey
        plane_hi = plane.astype(BF16)
        planeh[spot * GY : spot * GY + GY, lanes] = plane_hi
        planel[spot * GY : spot * GY + GY, lanes] = (plane - plane_hi.astype(F32)).astype(BF16)


def fill_depth(ez, coef, at, depth):
    weighed = ez * coef
    lanes = pl.ds(at * UNIT, UNIT)
    weighed_hi = weighed.astype(BF16)
    depth[0:GZ, lanes] = weighed_hi
    depth[GZ : 2 * GZ, lanes] = (weighed - weighed_hi.astype(F32)).astype(BF16)


def set_planes(blocks, tile, which, places, at, planeh, planel):
    wraps = blocks.num_col == 2 and which == 1
    fill_planes(shapes_x(tile), shapes_y(tile, blocks.col_shifts[which], wraps), places, at, planeh, planel)


def summed(planeh, planel, depth):
    first = lax.dot_general(planeh, depth, NT, preferred_element_type=F32)
    second = lax.dot_general(planel, depth[0:GZ, :], NT, preferred_element_type=F32)
    return first[:, 0:GZ] + first[:, GZ : 2 * GZ] + second


def rims_kernel(num_col, num_layer, refs_in, *refs):
    blocks = Blocks(refs[:refs_in], num_col, num_layer)
    low_ref, high_ref, depth, extra, whole, planeh, planel, longh, longl, long_depth, acc = refs[refs_in:]
    for index in range(blocks.total):
        whole[index * LANES : index * LANES + LANES, :] = blocks.matrix(index)
    over = blocks.over()
    for at, (which, pair) in enumerate(blocks.units()):
        tile = blocks.unit(which, pair)
        coef = weigh(blocks, whole, tile)
        if pair == PAIRS:
            coef = jnp.where(over > 0, 0.0, coef)
        set_planes(blocks, tile, which, RIM_X, at, planeh, planel)
        fill_depth(shapes_z(tile, blocks.lifts(pair)), coef, at, depth)
    total = summed(planeh[...], planel[...], depth[...])
    low_ref[...] = total[0:HALO, :]
    high_ref[...] = total[HALO:, :]

    @pl.when(jnp.max(over) > 0)
    def _():
        acc[...] = jnp.zeros_like(acc)
        for which, side in blocks.long_steps():

            def step(at, carry):
                both = blocks.tile(which, side, at)
                lift = blocks.side_shift(side) * float(GZ)
                for half in range(2):
                    tile = Gaussians(both[half * FIELDS : half * FIELDS + FIELDS, :])
                    set_planes(blocks, tile, which, ALL_X, 0, longh, longl)
                    fill_depth(shapes_z(tile, lift), weigh(blocks, whole, tile), 0, long_depth)
                    acc[...] += summed(longh[...], longl[...], long_depth[...])
                return carry

            lax.fori_loop(0, PAIRS // 2, step, 0)
        low_ref[...] += acc[0:HALO, :]
        extra[...] = acc[HALO : HALO + CORE, :]
        high_ref[...] += acc[HALO + CORE : FULL, :]


def rims(arrays, num_col, num_layer):
    gaussians = (2 if num_col == 2 else 3) * (PAIRS + 1) * UNIT
    return pl.pallas_call(
        functools.partial(rims_kernel, num_col, num_layer, len(arrays)),
        out_shape=(
            jax.ShapeDtypeStruct((HALO, GZ), F32),
            jax.ShapeDtypeStruct((HALO, GZ), F32),
            jax.ShapeDtypeStruct((2 * GZ, gaussians), BF16),
            jax.ShapeDtypeStruct((CORE, GZ), F32),
        ),
        in_specs=[VMEM] * len(arrays),
        out_specs=(VMEM,) * 4,
        scratch_shapes=[
            pltpu.VMEM((num_col * num_layer * LANES, arrays[0].shape[-1]), BF16),
            pltpu.VMEM((2 * HALO, gaussians), BF16),
            pltpu.VMEM((2 * HALO, gaussians), BF16),
            pltpu.VMEM((FULL, UNIT), BF16),
            pltpu.VMEM((FULL, UNIT), BF16),
            pltpu.VMEM((2 * GZ, UNIT), BF16),
            pltpu.VMEM((FULL, GZ), F32),
        ],
        compiler_params=PARAMS,
        cost_estimate=pl.CostEstimate(flops=3_000_000_000, bytes_accessed=1_000_000, transcendentals=0),
        name="rims",
    )(*arrays)


def core_kernel(num_col, num_layer, refs_in, *refs):
    blocks = Blocks(refs[:refs_in], num_col, num_layer)
    depth, extra, core_ref, planeh, planel = refs[refs_in:]
    for at, (which, pair) in enumerate(blocks.units()):
        set_planes(blocks, blocks.unit(which, pair), which, CORE_X, at, planeh, planel)
    core_ref[...] = summed(planeh[...], planel[...], depth[...])

    @pl.when(jnp.max(blocks.over()) > 0)
    def _():
        core_ref[...] += extra[...]


def core_part(arrays, depth, extra, num_col, num_layer):
    gaussians = depth.shape[1]
    return pl.pallas_call(
        functools.partial(core_kernel, num_col, num_layer, len(arrays)),
        out_shape=jax.ShapeDtypeStruct((CORE, GZ), F32),
        in_specs=[VMEM] * (len(arrays) + 2),
        out_specs=VMEM,
        scratch_shapes=[pltpu.VMEM((CORE, gaussians), BF16), pltpu.VMEM((CORE, gaussians), BF16)],
        compiler_params=PARAMS,
        cost_estimate=pl.CostEstimate(flops=1_500_000_000, bytes_accessed=1_000_000, transcendentals=0),
        name="core",
    )(*arrays, depth, extra)


def product_kernel(num_row, num_col, num_layer, refs_in, *refs):
    blocks = Blocks(refs[:refs_in], num_col, num_layer)
    h_refs = refs[refs_in : refs_in + num_row]
    out_ref, token_ref, slab = refs[refs_in + num_row :]
    token_ref[...] = jnp.zeros_like(token_ref)
    row = lax.axis_index("row")
    rows = h_refs[0].shape[1]
    for back in range(num_layer):
        for step in range(num_row):
            start = pl.multiple_of((row ^ step) * rows, rows)
            slab[back, pl.ds(start, rows), :] = h_refs[step][back]
    total = jnp.zeros(out_ref.shape, F32)
    for back in range(num_layer):
        for piece in range(num_col):
            if blocks.paired:
                left = blocks.matrix(piece * 4 + back)
                start = pl.multiple_of((blocks.col ^ piece) * LANES, LANES)
            else:
                source = lax.rem(blocks.layer - back + num_layer, num_layer)
                left = blocks.slab(source, piece)
                start = piece * LANES
            right = slab[back, pl.ds(start, LANES), :]
            total += lax.dot_general(left, right, TN, preferred_element_type=F32)
    out_ref[...] = total.astype(BF16)


def multiply(arrays, parts, num_row, num_col, num_layer):
    return pl.pallas_call(
        functools.partial(product_kernel, num_row, num_col, num_layer, len(arrays)),
        out_shape=(
            jax.ShapeDtypeStruct((arrays[0].shape[-1], LANES), BF16),
            jax.ShapeDtypeStruct((8, LANES), F32),
        ),
        in_specs=[VMEM] * (num_row + len(arrays)),
        out_specs=(VMEM, VMEM),
        scratch_shapes=[pltpu.VMEM((num_layer, num_col * LANES, LANES), BF16)],
        compiler_params=PARAMS,
        cost_estimate=pl.CostEstimate(flops=500_000_000, bytes_accessed=1_000_000, transcendentals=0),
        name="multiply",
    )(*arrays, *parts)


def settle_kernel(block_ref, out_ref):
    out_ref[...] = block_ref[...]


def settle(block):
    return pl.pallas_call(
        settle_kernel,
        out_shape=jax.ShapeDtypeStruct(block.shape, BF16),
        in_specs=[VMEM],
        out_specs=VMEM,
        compiler_params=PARAMS,
        cost_estimate=pl.CostEstimate(flops=1000, bytes_accessed=1000, transcendentals=0),
        name="settle",
    )(block)


def stack_kernel(own_ref, near_ref, far_ref, both_ref, out_ref):
    out_ref[0] = own_ref[BASE:, LANES:UNIT]
    out_ref[1] = near_ref[BASE:, 0:LANES]
    out_ref[2] = far_ref[BASE:, 0:LANES]
    out_ref[3] = both_ref[BASE:, LANES:UNIT]


def stack(own, near, far, both):
    return pl.pallas_call(
        stack_kernel,
        out_shape=jax.ShapeDtypeStruct((4, own.shape[0] - BASE, LANES), BF16),
        in_specs=[VMEM] * 4,
        out_specs=VMEM,
        compiler_params=PARAMS,
        name="stack",
    )(own, near, far, both)


def fold_kernel(core_ref, below_ref, above_ref, after_ref, out_ref):
    out_ref[0:HALO, :] = core_ref[0:HALO, :] + below_ref[...]
    out_ref[HALO : CORE - HALO, :] = core_ref[HALO : CORE - HALO, :]
    out_ref[CORE - HALO : CORE, :] = core_ref[CORE - HALO : CORE, :] + above_ref[...]


def fold(core, below, above, after):
    return pl.pallas_call(
        fold_kernel,
        out_shape=jax.ShapeDtypeStruct((CORE, GZ), F32),
        in_specs=[VMEM] * 4,
        out_specs=VMEM,
        compiler_params=PARAMS,
        cost_estimate=pl.CostEstimate(flops=1_000_000, bytes_accessed=400_000, transcendentals=0),
        name="fold",
    )(core, below, above, after)


def shifted(value, axis, count, step):
    return lax.ppermute(value, axis, [(i, (i + step) % count) for i in range(count)])


def crossed(value, col_bit, layer_bits):
    pairs = [(c * 4 + l, (c ^ col_bit) * 4 + (l ^ layer_bits)) for c in range(2) for l in range(4)]
    return lax.ppermute(value, ("col", "layer"), pairs)


def gather_paired(base, tall_y, tall_core):
    got_x = crossed(base, 1, 0)
    got_y = crossed(tall_y, 0, 2)
    got_xy = crossed(base, 1, 2)
    near = crossed(tall_core, 0, 1)
    near_x = crossed(got_x, 0, 1)
    near_y = crossed(got_y, 0, 1)
    near_xy = crossed(got_xy, 0, 1)
    return [tall_core, near, got_y, near_y, got_x, near_x, got_xy, near_xy]


def on_device(p_slabs, p_mask, h_slabs, h_mask, gauss_row, gauss_col, gauss_cell, gauss_expo, gauss_pref):
    num_row, num_col, num_layer = (lax.axis_size(axis) for axis in ("row", "col", "layer"))
    paired = num_col == 2 and num_layer == 4
    flat = [x.reshape(8, LANES) for x in (gauss_row, gauss_col, gauss_cell, gauss_expo, gauss_pref)]
    made = prepare(paired, p_slabs[0], p_mask[0].T, h_slabs[0], h_mask[0], *flat)
    if paired:
        arrays = gather_paired(*made[:2], settle(made[2]))
        mine = stack(*arrays[:4])
    else:
        base, pieces = made
        arrays = [lax.all_gather(base, ("layer", "col"), axis=0)]
        mine = [pieces[0]] + [shifted(pieces[step], "layer", num_layer, step) for step in range(1, num_layer)]
        mine = jnp.stack(mine)
    low, high, depth, extra = rims(arrays, num_col, num_layer)
    parts = [mine] + [
        lax.ppermute(mine, "row", [(i, i ^ step) for i in range(num_row)]) for step in range(1, num_row)
    ]
    below = shifted(high, "row", num_row, 1)
    above = shifted(low, "row", num_row, num_row - 1)
    core = core_part(arrays, depth, extra, num_col, num_layer)
    product, token = multiply(arrays, parts, num_row, num_col, num_layer)
    density = fold(core, below, above, token).reshape(GX, GY, GZ)
    return (product, density)


def solution(mesh):
    placed = (P("layer", "row", "col"),) * 4 + (P(("row", "col", "layer")),) * 5
    return jax.shard_map(
        on_device,
        mesh=mesh,
        in_specs=placed,
        out_specs=(P("row", ("col", "layer")), P("row", "col", "layer")),
        check_vma=False,
    )
```

```python
import functools

import jax
import jax.numpy as jnp
from jax import lax
from jax.experimental import pallas as pl
from jax.experimental.pallas import tpu as pltpu
from jax.sharding import PartitionSpec as P

BS = 32
GX = 16
GY = 16
GZ = 128
R = 4
LANES = 128
F32 = jnp.float32
BF16 = jnp.bfloat16
HALO = R * GY
CORE = GX * GY
FULL = CORE + 2 * HALO
UNIT = 2 * LANES
PAIRS = 4
META = (PAIRS // 2 + 1) * 16
BASE = LANES + META
FLAG = 8
FIELDS = 8
VMEM = pl.BlockSpec(memory_space=pltpu.VMEM)
HBM = pl.BlockSpec(memory_space=pltpu.HBM)
PARAMS = pltpu.CompilerParams(vmem_limit_bytes=40 * 1024 * 1024)
NT = (((1,), (1,)), ((), ()))
TN = (((0,), (0,)), ((), ()))


def iota(shape, axis):
    return lax.broadcasted_iota(jnp.int32, shape, axis).astype(F32)


def split2(value):
    first = value.astype(BF16).astype(F32)
    return first, value - first


class Gaussians:
    def __init__(self, tile):
        first, second, third, fourth = (tile[at : at + 1, :].astype(jnp.int32) for at in range(4))
        first, second, third = first + 256, second + 256, third + 256
        column = third + ((fourth >> 7) << 9) + ((second >> 8) << 10) + ((first >> 8) << 11)
        cell = second & 255
        self.row = (first & 255).astype(F32)
        self.block = (column // LANES).astype(F32)
        self.lane = (column % LANES).astype(F32)
        self.x = (cell // GY).astype(F32)
        self.y = (cell % GY).astype(F32)
        self.z = (fourth & 127).astype(F32)
        self.expo = tile[4:5, :] + tile[5:6, :]
        self.pref = tile[6:7, :] + tile[7:8, :]


def masked(values, bits):
    lane = lax.broadcasted_iota(jnp.int32, values.shape, 1) // BS
    keep = jnp.zeros(values.shape, jnp.int32)
    for piece, bit in enumerate(bits):
        keep = jnp.where(lane == piece, bit, keep)
    return jnp.where(keep > 0, values.astype(F32), 0.0)


def ranks(flags):
    up = (iota((LANES, LANES), 0) <= iota((LANES, LANES), 1)).astype(F32).astype(BF16)
    ones = jnp.ones((LANES, LANES), BF16)
    within = jnp.dot(flags.astype(BF16), up, preferred_element_type=F32)
    totals = jnp.dot(flags.astype(BF16), ones, preferred_element_type=F32)
    row, other = iota((16, 16), 0), iota((16, 16), 1)
    same = (row < 8) == (other < 8)
    before = jnp.where(same & (other < row), 1.0, 0.0).astype(BF16)
    every = jnp.where(same, 1.0, 0.0).astype(BF16)
    earlier = jnp.dot(before, totals.astype(BF16), preferred_element_type=F32)
    count = jnp.dot(every, totals.astype(BF16), preferred_element_type=F32)
    return jnp.where(flags > 0, within + earlier - 1.0, -1.0), count


def h_piece(h_ref, hm_ref, chunk):
    pieces = LANES // BS
    out = []
    for block in range(h_ref.shape[0] // BS):
        bits = [hm_ref[block, chunk * pieces + at] for at in range(pieces)]
        value = h_ref[pl.ds(block * BS, BS), pl.ds(pl.multiple_of(chunk * LANES, LANES), LANES)]
        out.append(masked(value, bits).astype(BF16))
    return jnp.concatenate(out, axis=0)


def prepare_kernel(paired, *refs):
    sources, outs, refs = refs[:9], refs[9:-14], refs[-14:]
    landed, (tmp, fields, matrix, onehot, sems) = refs[:9], refs[9:]
    copies = [pltpu.make_async_copy(src, dst, sems.at[at]) for at, (src, dst) in enumerate(zip(sources, landed))]
    for copy in copies:
        copy.start()
    for copy in copies:
        copy.wait()
    p_ref, pm_ref, h_ref, hm_ref, row_ref, col_ref, cell_ref, expo_ref, pref_ref = landed
    layer = lax.axis_index("layer")
    count = lax.axis_size("layer")
    band = p_ref.shape[0]
    for block in range(band // BS):
        rows = pl.ds(block * BS, BS)
        tmp[rows, :] = masked(p_ref[rows, :], [pm_ref[piece, block] for piece in range(LANES // BS)])
    turned = tmp[...].T.astype(BF16)
    col = col_ref[...]
    cell = cell_ref[...]
    cell_z = (cell % GZ).astype(F32)
    values = [
        (row_ref[...] + ((col >> 11) & 1) * 256 - 256).astype(F32),
        (cell // GZ + ((col >> 10) & 1) * 256 - 256).astype(F32),
        ((col & 511) - 256).astype(F32),
        (cell % GZ + ((col >> 9) & 1) * 128).astype(F32),
        *split2(expo_ref[...]),
        *split2(pref_ref[...]),
    ]
    for index in range(FIELDS):
        fields[8 * index : 8 * index + 8, :] = values[index]
    for part in range(2 * PAIRS):
        matrix[0:FIELDS, part * LANES : part * LANES + LANES] = fields[pl.ds(part, FIELDS, stride=8), :]
    matrix[FIELDS : 2 * FIELDS, :] = jnp.zeros((FIELDS, 2 * PAIRS * LANES), F32)
    faces = jnp.concatenate([jnp.where(cell_z < R, 1.0, 0.0), jnp.where(cell_z >= GZ - R, 1.0, 0.0)], axis=0)
    place, many = ranks(faces)
    slot = iota((LANES, LANES), 0)
    for part in range(2 * PAIRS):
        lanes = pl.ds(part * LANES, LANES)
        for face in range(2):
            hit = slot == place[face * 8 + part : face * 8 + part + 1, :]
            onehot[face * LANES : face * LANES + LANES, lanes] = jnp.where(hit, 1.0, 0.0).astype(BF16)
    listed = lax.dot_general(matrix[...].astype(BF16), onehot[...], NT, preferred_element_type=F32)
    over = jnp.where(jnp.max(many, axis=0, keepdims=True) > LANES, 1.0, 0.0)
    over = jnp.concatenate([over, over], axis=1)
    listed = jnp.where(iota(listed.shape, 0) == FLAG, over, listed).astype(BF16)
    copies = outs[:3] if paired else outs[:1]
    for out in copies:
        out[0:LANES, :] = turned
        for at in range(PAIRS // 2):
            halves = [matrix[0:FIELDS, pair * UNIT : pair * UNIT + UNIT] for pair in (2 * at, 2 * at + 1)]
            out[LANES + 16 * at : LANES + 16 * at + 16, :] = jnp.concatenate(halves, axis=0).astype(BF16)
        out[LANES + 8 * PAIRS : BASE, :] = listed

    def piece(chunk):
        return h_piece(h_ref, hm_ref, chunk)

    if paired:
        outs[1][BASE:, 0:LANES] = piece(layer ^ 2)
        outs[1][BASE:, LANES:UNIT] = piece(layer ^ 3)
        outs[2][BASE:, 0:LANES] = piece(layer ^ 1)
        outs[2][BASE:, LANES:UNIT] = piece(layer)
    else:
        for back in range(h_ref.shape[1] // LANES):
            outs[1][back] = piece(lax.rem(layer + back, count))


def prepare(paired, p, p_mask, h, h_mask, *gauss):
    band = p.shape[0]
    base = jax.ShapeDtypeStruct((BASE, band), BF16)
    tall = jax.ShapeDtypeStruct((BASE + h.shape[0], band), BF16)
    if paired:
        outs = (base, tall, tall)
    else:
        outs = (base, jax.ShapeDtypeStruct((h.shape[1] // LANES, h.shape[0], LANES), BF16))
    return pl.pallas_call(
        functools.partial(prepare_kernel, paired),
        out_shape=outs,
        in_specs=[HBM] * 9,
        out_specs=(VMEM,) * len(outs),
        scratch_shapes=[
            pltpu.VMEM(p.shape, p.dtype),
            pltpu.SMEM(p_mask.shape, p_mask.dtype),
            pltpu.VMEM(h.shape, h.dtype),
            pltpu.SMEM(h_mask.shape, h_mask.dtype),
            *[pltpu.VMEM(x.shape, x.dtype) for x in gauss],
            pltpu.VMEM(p.shape, F32),
            pltpu.VMEM((FIELDS * 8, LANES), F32),
            pltpu.VMEM((2 * FIELDS, 2 * PAIRS * LANES), F32),
            pltpu.VMEM((UNIT, 2 * PAIRS * LANES), BF16),
            pltpu.SemaphoreType.DMA((9,)),
        ],
        compiler_params=pltpu.CompilerParams(vmem_limit_bytes=62 * 1024 * 1024),
        name="prepare",
    )(p, p_mask, h, h_mask, *gauss)


class Blocks:
    def __init__(self, refs, num_col, num_layer):
        self.refs = refs
        self.num_col, self.num_layer = num_col, num_layer
        self.paired = len(refs) > 1
        self.col, self.layer = lax.axis_index("col"), lax.axis_index("layer")
        self.total = num_col * num_layer
        self.col_shifts = [0, 1] if num_col == 2 else [0, -1, 1]

    def ident(self, index):
        if not self.paired:
            return index
        return (self.layer ^ (index % 4)) * 2 + (self.col ^ (index // 4))

    def matrix(self, index):
        return self.refs[index][0:LANES, :] if self.paired else self.refs[0][index, 0:LANES, :]

    def slab(self, layer, piece):
        index = layer * self.num_col + piece
        return self.refs[0][index, 0:LANES, :]

    def tile(self, which, side, at):
        rows = pl.ds(LANES + 16 * at, 16)
        if self.paired:
            return self.refs[which * 4 + side][rows, :].astype(F32)
        shift_l = 0 if side == 0 else (1 if side == 1 else -1)
        index = lax.rem(self.layer + shift_l + self.num_layer, self.num_layer) * self.num_col
        index += lax.rem(self.col + self.col_shifts[which] + self.num_col, self.num_col)
        return self.refs[0][index, rows, :].astype(F32)

    def side_shift(self, side):
        if self.paired:
            even = (self.layer % 2) == 0
            return jnp.where(even, 1.0, -1.0) if side == 1 else jnp.where(even, -1.0, 1.0)
        return 1.0 if side == 1 else -1.0

    def sides(self):
        return (1, 3) if self.paired else (1, 2)

    def units(self):
        return [(which, pair) for which in range(len(self.col_shifts)) for pair in range(PAIRS + 1)]

    def listed(self, which):
        halves = []
        for side in self.sides():
            both = self.tile(which, side, PAIRS // 2)[0:FIELDS, :]
            upward = self.side_shift(side) > 0
            halves.append(jnp.where(upward, both[:, 0:LANES], both[:, LANES:UNIT]))
        return jnp.concatenate(halves, axis=1)

    def unit(self, which, pair):
        if pair == PAIRS:
            return Gaussians(self.listed(which))
        half = (pair % 2) * FIELDS
        return Gaussians(self.tile(which, 0, pair // 2)[half : half + FIELDS, :])

    def lifts(self, pair):
        if pair < PAIRS:
            return 0.0
        lane = iota((1, UNIT), 1)
        first, second = self.sides()
        return jnp.where(lane < LANES, self.side_shift(first), self.side_shift(second)) * float(GZ)

    def over(self):
        flags = [
            self.tile(which, side, PAIRS // 2)[FLAG : FLAG + 1, :]
            for which in range(len(self.col_shifts))
            for side in self.sides()
        ]
        return functools.reduce(jnp.maximum, flags)

    def long_steps(self):
        return [(which, side) for which in range(len(self.col_shifts)) for side in self.sides()]


def weigh(blocks, whole, tile):
    band = whole.shape[1]
    onehot = jnp.where(iota((band, UNIT), 0) == tile.row, 1.0, 0.0).astype(BF16)
    found = jnp.dot(whole[...], onehot, preferred_element_type=F32)
    picked = jnp.zeros((LANES, UNIT), F32)
    for index in range(blocks.total):
        mine = tile.block == jnp.asarray(blocks.ident(index)).astype(F32)
        picked = jnp.where(mine, found[index * LANES : index * LANES + LANES, :], picked)
    value = jnp.sum(jnp.where(iota((LANES, UNIT), 0) == tile.lane, picked, 0.0), axis=0, keepdims=True)
    return tile.pref * value


def bell(dist, expo):
    square = dist * dist
    return jnp.where(square < (R + 0.5) ** 2, jnp.exp(-expo * square), 0.0)


RIM_X = tuple(range(R)) + tuple(range(GX + R, GX + 2 * R))
CORE_X = tuple(range(R, GX + R))
ALL_X = tuple(range(GX + 2 * R))


def shapes_x(tile):
    return bell(iota((GX + 2 * R, UNIT), 0) - float(R) - tile.x, tile.expo)


def shapes_y(tile, shift, wraps):
    dy = iota((GY, UNIT), 0) - tile.y - float(shift * GY)
    if wraps:
        dy = jnp.where(dy < -float(GY), dy + 2.0 * GY, dy)
    return bell(dy, tile.expo)


def shapes_z(tile, lift):
    return bell(iota((GZ, UNIT), 0) - tile.z - lift, tile.expo)


def fill_planes(ex, ey, places, at, planeh, planel):
    lanes = pl.ds(at * UNIT, UNIT)
    for spot, x in enumerate(places):
        plane = ex[x : x + 1, :] * ey
        plane_hi = plane.astype(BF16)
        planeh[spot * GY : spot * GY + GY, lanes] = plane_hi
        planel[spot * GY : spot * GY + GY, lanes] = (plane - plane_hi.astype(F32)).astype(BF16)


def fill_depth(ez, coef, at, depth):
    weighed = ez * coef
    lanes = pl.ds(at * UNIT, UNIT)
    weighed_hi = weighed.astype(BF16)
    depth[0:GZ, lanes] = weighed_hi
    depth[GZ : 2 * GZ, lanes] = (weighed - weighed_hi.astype(F32)).astype(BF16)


def set_planes(blocks, tile, which, places, at, planeh, planel):
    wraps = blocks.num_col == 2 and which == 1
    fill_planes(shapes_x(tile), shapes_y(tile, blocks.col_shifts[which], wraps), places, at, planeh, planel)


def summed(planeh, planel, depth):
    first = lax.dot_general(planeh, depth, NT, preferred_element_type=F32)
    second = lax.dot_general(planel, depth[0:GZ, :], NT, preferred_element_type=F32)
    return first[:, 0:GZ] + first[:, GZ : 2 * GZ] + second


def rims_kernel(num_col, num_layer, refs_in, *refs):
    blocks = Blocks(refs[:refs_in], num_col, num_layer)
    low_ref, high_ref, depth, extra, whole, planeh, planel, longh, longl, long_depth, acc = refs[refs_in:]
    for index in range(blocks.total):
        whole[index * LANES : index * LANES + LANES, :] = blocks.matrix(index)
    over = blocks.over()
    for at, (which, pair) in enumerate(blocks.units()):
        tile = blocks.unit(which, pair)
        coef = weigh(blocks, whole, tile)
        if pair == PAIRS:
            coef = jnp.where(over > 0, 0.0, coef)
        set_planes(blocks, tile, which, RIM_X, at, planeh, planel)
        fill_depth(shapes_z(tile, blocks.lifts(pair)), coef, at, depth)
    total = summed(planeh[...], planel[...], depth[...])
    swap = lax.rem(lax.axis_index("row"), 2) * int(lax.axis_size("row") == 4)

    def put(low, high, base_low, base_high):
        low_ref[...] = jnp.where(swap > 0, high, low) + base_low
        high_ref[...] = jnp.where(swap > 0, low, high) + base_high

    put(total[0:HALO, :], total[HALO:, :], 0.0, 0.0)

    @pl.when(jnp.max(over) > 0)
    def _():
        acc[...] = jnp.zeros_like(acc)
        for which, side in blocks.long_steps():

            def step(at, carry):
                both = blocks.tile(which, side, at)
                lift = blocks.side_shift(side) * float(GZ)
                for half in range(2):
                    tile = Gaussians(both[half * FIELDS : half * FIELDS + FIELDS, :])
                    set_planes(blocks, tile, which, ALL_X, 0, longh, longl)
                    fill_depth(shapes_z(tile, lift), weigh(blocks, whole, tile), 0, long_depth)
                    acc[...] += summed(longh[...], longl[...], long_depth[...])
                return carry

            lax.fori_loop(0, PAIRS // 2, step, 0)
        put(acc[0:HALO, :], acc[HALO + CORE : FULL, :], low_ref[...], high_ref[...])
        extra[...] = acc[HALO : HALO + CORE, :]


def rims(arrays, num_col, num_layer):
    gaussians = (2 if num_col == 2 else 3) * (PAIRS + 1) * UNIT
    return pl.pallas_call(
        functools.partial(rims_kernel, num_col, num_layer, len(arrays)),
        out_shape=(
            jax.ShapeDtypeStruct((HALO, GZ), F32),
            jax.ShapeDtypeStruct((HALO, GZ), F32),
            jax.ShapeDtypeStruct((2 * GZ, gaussians), BF16),
            jax.ShapeDtypeStruct((CORE, GZ), F32),
        ),
        in_specs=[VMEM] * len(arrays),
        out_specs=(VMEM,) * 4,
        scratch_shapes=[
            pltpu.VMEM((num_col * num_layer * LANES, arrays[0].shape[-1]), BF16),
            pltpu.VMEM((2 * HALO, gaussians), BF16),
            pltpu.VMEM((2 * HALO, gaussians), BF16),
            pltpu.VMEM((FULL, UNIT), BF16),
            pltpu.VMEM((FULL, UNIT), BF16),
            pltpu.VMEM((2 * GZ, UNIT), BF16),
            pltpu.VMEM((FULL, GZ), F32),
        ],
        compiler_params=PARAMS,
        cost_estimate=pl.CostEstimate(flops=3_000_000_000, bytes_accessed=1_000_000, transcendentals=0),
        name="rims",
    )(*arrays)


def core_kernel(num_col, num_layer, refs_in, *refs):
    blocks = Blocks(refs[:refs_in], num_col, num_layer)
    depth, extra, core_ref, planeh, planel = refs[refs_in:]
    for at, (which, pair) in enumerate(blocks.units()):
        set_planes(blocks, blocks.unit(which, pair), which, CORE_X, at, planeh, planel)
    core_ref[...] = summed(planeh[...], planel[...], depth[...])

    @pl.when(jnp.max(blocks.over()) > 0)
    def _():
        core_ref[...] += extra[...]


def core_part(arrays, depth, extra, num_col, num_layer):
    gaussians = depth.shape[1]
    return pl.pallas_call(
        functools.partial(core_kernel, num_col, num_layer, len(arrays)),
        out_shape=jax.ShapeDtypeStruct((CORE, GZ), F32),
        in_specs=[VMEM] * (len(arrays) + 2),
        out_specs=VMEM,
        scratch_shapes=[pltpu.VMEM((CORE, gaussians), BF16), pltpu.VMEM((CORE, gaussians), BF16)],
        compiler_params=PARAMS,
        cost_estimate=pl.CostEstimate(flops=1_500_000_000, bytes_accessed=1_000_000, transcendentals=0),
        name="core",
    )(*arrays, depth, extra)


def row_steps(num_row):
    return [0, 1, num_row - 1] + list(range(2, num_row - 1))


def product_kernel(num_row, num_col, num_layer, refs_in, *refs):
    blocks = Blocks(refs[:refs_in], num_col, num_layer)
    h_refs = refs[refs_in : refs_in + num_row]
    out_ref, token_ref, slab = refs[refs_in + num_row :]
    token_ref[...] = jnp.zeros_like(token_ref)
    row = lax.axis_index("row")
    rows = h_refs[0].shape[1]
    for back in range(num_layer):
        for spot, step in enumerate(row_steps(num_row)):
            start = pl.multiple_of(lax.rem(row - step + num_row, num_row) * rows, rows)
            slab[back, pl.ds(start, rows), :] = h_refs[spot][back]
    total = jnp.zeros(out_ref.shape, F32)
    for back in range(num_layer):
        for piece in range(num_col):
            if blocks.paired:
                left = blocks.matrix(piece * 4 + back)
                start = pl.multiple_of((blocks.col ^ piece) * LANES, LANES)
            else:
                source = lax.rem(blocks.layer - back + num_layer, num_layer)
                left = blocks.slab(source, piece)
                start = piece * LANES
            right = slab[back, pl.ds(start, LANES), :]
            total += lax.dot_general(left, right, TN, preferred_element_type=F32)
    out_ref[...] = total.astype(BF16)


def multiply(arrays, parts, num_row, num_col, num_layer):
    return pl.pallas_call(
        functools.partial(product_kernel, num_row, num_col, num_layer, len(arrays)),
        out_shape=(
            jax.ShapeDtypeStruct((arrays[0].shape[-1], LANES), BF16),
            jax.ShapeDtypeStruct((8, LANES), F32),
        ),
        in_specs=[VMEM] * (num_row + len(arrays)),
        out_specs=(VMEM, VMEM),
        scratch_shapes=[pltpu.VMEM((num_layer, num_col * LANES, LANES), BF16)],
        compiler_params=PARAMS,
        cost_estimate=pl.CostEstimate(flops=500_000_000, bytes_accessed=1_000_000, transcendentals=0),
        name="multiply",
    )(*arrays, *parts)


def settle_kernel(block_ref, out_ref):
    out_ref[...] = block_ref[...]


def settle(block):
    return pl.pallas_call(
        settle_kernel,
        out_shape=jax.ShapeDtypeStruct(block.shape, BF16),
        in_specs=[VMEM],
        out_specs=VMEM,
        compiler_params=PARAMS,
        cost_estimate=pl.CostEstimate(flops=1000, bytes_accessed=1000, transcendentals=0),
        name="settle",
    )(block)


def stack_kernel(own_ref, near_ref, far_ref, both_ref, out_ref):
    out_ref[0] = own_ref[BASE:, LANES:UNIT]
    out_ref[1] = near_ref[BASE:, 0:LANES]
    out_ref[2] = far_ref[BASE:, 0:LANES]
    out_ref[3] = both_ref[BASE:, LANES:UNIT]


def stack(own, near, far, both):
    return pl.pallas_call(
        stack_kernel,
        out_shape=jax.ShapeDtypeStruct((4, own.shape[0] - BASE, LANES), BF16),
        in_specs=[VMEM] * 4,
        out_specs=VMEM,
        compiler_params=PARAMS,
        name="stack",
    )(own, near, far, both)


def fold_kernel(core_ref, below_ref, above_ref, after_ref, out_ref):
    swap = lax.rem(lax.axis_index("row"), 2) * int(lax.axis_size("row") == 4)
    below, above = below_ref[...], above_ref[...]
    out_ref[0:HALO, :] = core_ref[0:HALO, :] + jnp.where(swap > 0, above, below)
    out_ref[HALO : CORE - HALO, :] = core_ref[HALO : CORE - HALO, :]
    out_ref[CORE - HALO : CORE, :] = core_ref[CORE - HALO : CORE, :] + jnp.where(swap > 0, below, above)


def fold(core, below, above, after):
    return pl.pallas_call(
        fold_kernel,
        out_shape=jax.ShapeDtypeStruct((CORE, GZ), F32),
        in_specs=[VMEM] * 4,
        out_specs=VMEM,
        compiler_params=PARAMS,
        cost_estimate=pl.CostEstimate(flops=1_000_000, bytes_accessed=400_000, transcendentals=0),
        name="fold",
    )(core, below, above, after)


def shifted(value, axis, count, step):
    return lax.ppermute(value, axis, [(i, (i + step) % count) for i in range(count)])


def crossed(value, col_bit, layer_bits):
    pairs = [(c * 4 + l, (c ^ col_bit) * 4 + (l ^ layer_bits)) for c in range(2) for l in range(4)]
    return lax.ppermute(value, ("col", "layer"), pairs)


def gather_paired(base, tall_y, tall_core):
    got_x = crossed(base, 1, 0)
    got_y = crossed(tall_y, 0, 2)
    got_xy = crossed(base, 1, 2)
    near = crossed(tall_core, 0, 1)
    near_x = crossed(got_x, 0, 1)
    near_y = crossed(got_y, 0, 1)
    near_xy = crossed(got_xy, 0, 1)
    return [tall_core, near, got_y, near_y, got_x, near_x, got_xy, near_xy]


def on_device(p_slabs, p_mask, h_slabs, h_mask, gauss_row, gauss_col, gauss_cell, gauss_expo, gauss_pref):
    num_row, num_col, num_layer = (lax.axis_size(axis) for axis in ("row", "col", "layer"))
    paired = num_col == 2 and num_layer == 4
    flat = [x.reshape(8, LANES) for x in (gauss_row, gauss_col, gauss_cell, gauss_expo, gauss_pref)]
    made = prepare(paired, p_slabs[0], p_mask[0].T, h_slabs[0], h_mask[0], *flat)
    if paired:
        arrays = gather_paired(*made[:2], settle(made[2]))
        mine = stack(*arrays[:4])
    else:
        base, pieces = made
        arrays = [lax.all_gather(base, ("layer", "col"), axis=0)]
        mine = [pieces[0]] + [shifted(pieces[step], "layer", num_layer, step) for step in range(1, num_layer)]
        mine = jnp.stack(mine)
    low, high, depth, extra = rims(arrays, num_col, num_layer)
    parts = [mine] + [shifted(mine, "row", num_row, step) for step in row_steps(num_row)[1:]]
    if num_row == 4:
        below = lax.ppermute(low, "row", [(i, i ^ 3) for i in range(4)])
        above = lax.ppermute(high, "row", [(i, i ^ 1) for i in range(4)])
    else:
        below = shifted(high, "row", num_row, 1)
        above = shifted(low, "row", num_row, num_row - 1)
    core = core_part(arrays, depth, extra, num_col, num_layer)
    product, token = multiply(arrays, parts, num_row, num_col, num_layer)
    density = fold(core, below, above, token).reshape(GX, GY, GZ)
    return (product, density)


def solution(mesh):
    placed = (P("layer", "row", "col"),) * 4 + (P(("row", "col", "layer")),) * 5
    return jax.shard_map(
        on_device,
        mesh=mesh,
        in_specs=placed,
        out_specs=(P("row", ("col", "layer")), P("row", "col", "layer")),
        check_vma=False,
    )
```

```python
import functools

import jax
import jax.numpy as jnp
from jax import lax
from jax.experimental import pallas as pl
from jax.experimental.pallas import tpu as pltpu
from jax.sharding import PartitionSpec as P

BS = 32
GX = 16
GY = 16
GZ = 128
R = 4
LANES = 128
F32 = jnp.float32
BF16 = jnp.bfloat16
HALO = R * GY
CORE = GX * GY
FULL = CORE + 2 * HALO
UNIT = 2 * LANES
PAIRS = 4
META = (PAIRS // 2 + 1) * 16
BASE = LANES + META
FLAG = 8
FIELDS = 8
VMEM = pl.BlockSpec(memory_space=pltpu.VMEM)
HBM = pl.BlockSpec(memory_space=pltpu.HBM)
PARAMS = pltpu.CompilerParams(vmem_limit_bytes=40 * 1024 * 1024)
NT = (((1,), (1,)), ((), ()))
TN = (((0,), (0,)), ((), ()))


def iota(shape, axis):
    return lax.broadcasted_iota(jnp.int32, shape, axis).astype(F32)


def split2(value):
    first = value.astype(BF16).astype(F32)
    return first, value - first


class Gaussians:
    def __init__(self, tile):
        first, second, third, fourth = (tile[at : at + 1, :].astype(jnp.int32) for at in range(4))
        first, second, third = first + 256, second + 256, third + 256
        column = third + ((fourth >> 7) << 9) + ((second >> 8) << 10) + ((first >> 8) << 11)
        cell = second & 255
        self.row = (first & 255).astype(F32)
        self.block = (column // LANES).astype(F32)
        self.lane = (column % LANES).astype(F32)
        self.x = (cell // GY).astype(F32)
        self.y = (cell % GY).astype(F32)
        self.z = (fourth & 127).astype(F32)
        self.expo = tile[4:5, :] + tile[5:6, :]
        self.pref = tile[6:7, :] + tile[7:8, :]


def masked(values, bits):
    lane = lax.broadcasted_iota(jnp.int32, values.shape, 1) // BS
    keep = jnp.zeros(values.shape, jnp.int32)
    for piece, bit in enumerate(bits):
        keep = jnp.where(lane == piece, bit, keep)
    return jnp.where(keep > 0, values.astype(F32), 0.0)


def ranks(flags):
    up = (iota((LANES, LANES), 0) <= iota((LANES, LANES), 1)).astype(F32).astype(BF16)
    ones = jnp.ones((LANES, LANES), BF16)
    within = jnp.dot(flags.astype(BF16), up, preferred_element_type=F32)
    totals = jnp.dot(flags.astype(BF16), ones, preferred_element_type=F32)
    row, other = iota((16, 16), 0), iota((16, 16), 1)
    same = (row < 8) == (other < 8)
    before = jnp.where(same & (other < row), 1.0, 0.0).astype(BF16)
    every = jnp.where(same, 1.0, 0.0).astype(BF16)
    earlier = jnp.dot(before, totals.astype(BF16), preferred_element_type=F32)
    count = jnp.dot(every, totals.astype(BF16), preferred_element_type=F32)
    return jnp.where(flags > 0, within + earlier - 1.0, -1.0), count


def h_piece(h_ref, hm_ref, chunk):
    pieces = LANES // BS
    out = []
    for block in range(h_ref.shape[0] // BS):
        bits = [hm_ref[block, chunk * pieces + at] for at in range(pieces)]
        value = h_ref[pl.ds(block * BS, BS), pl.ds(pl.multiple_of(chunk * LANES, LANES), LANES)]
        out.append(masked(value, bits).astype(BF16))
    return jnp.concatenate(out, axis=0)


def prepare_kernel(paired, *refs):
    sources, outs, refs = refs[:9], refs[9:-14], refs[-14:]
    landed, (tmp, fields, matrix, onehot, sems) = refs[:9], refs[9:]
    copies = [pltpu.make_async_copy(src, dst, sems.at[at]) for at, (src, dst) in enumerate(zip(sources, landed))]
    for copy in copies:
        copy.start()
    for copy in copies:
        copy.wait()
    p_ref, pm_ref, h_ref, hm_ref, row_ref, col_ref, cell_ref, expo_ref, pref_ref = landed
    layer = lax.axis_index("layer")
    count = lax.axis_size("layer")
    band = p_ref.shape[0]
    for block in range(band // BS):
        rows = pl.ds(block * BS, BS)
        tmp[rows, :] = masked(p_ref[rows, :], [pm_ref[piece, block] for piece in range(LANES // BS)])
    turned = tmp[...].T.astype(BF16)
    col = col_ref[...]
    cell = cell_ref[...]
    cell_z = (cell % GZ).astype(F32)
    values = [
        (row_ref[...] + ((col >> 11) & 1) * 256 - 256).astype(F32),
        (cell // GZ + ((col >> 10) & 1) * 256 - 256).astype(F32),
        ((col & 511) - 256).astype(F32),
        (cell % GZ + ((col >> 9) & 1) * 128).astype(F32),
        *split2(expo_ref[...]),
        *split2(pref_ref[...]),
    ]
    for index in range(FIELDS):
        fields[8 * index : 8 * index + 8, :] = values[index]
    for part in range(2 * PAIRS):
        matrix[0:FIELDS, part * LANES : part * LANES + LANES] = fields[pl.ds(part, FIELDS, stride=8), :]
    matrix[FIELDS : 2 * FIELDS, :] = jnp.zeros((FIELDS, 2 * PAIRS * LANES), F32)
    faces = jnp.concatenate([jnp.where(cell_z < R, 1.0, 0.0), jnp.where(cell_z >= GZ - R, 1.0, 0.0)], axis=0)
    place, many = ranks(faces)
    slot = iota((LANES, LANES), 0)
    for part in range(2 * PAIRS):
        lanes = pl.ds(part * LANES, LANES)
        for face in range(2):
            hit = slot == place[face * 8 + part : face * 8 + part + 1, :]
            onehot[face * LANES : face * LANES + LANES, lanes] = jnp.where(hit, 1.0, 0.0).astype(BF16)
    listed = lax.dot_general(matrix[...].astype(BF16), onehot[...], NT, preferred_element_type=F32)
    over = jnp.where(jnp.max(many, axis=0, keepdims=True) > LANES, 1.0, 0.0)
    over = jnp.concatenate([over, over], axis=1)
    listed = jnp.where(iota(listed.shape, 0) == FLAG, over, listed).astype(BF16)
    copies = outs[:3] if paired else outs[:1]
    for out in copies:
        out[0:LANES, :] = turned
        for at in range(PAIRS // 2):
            halves = [matrix[0:FIELDS, pair * UNIT : pair * UNIT + UNIT] for pair in (2 * at, 2 * at + 1)]
            out[LANES + 16 * at : LANES + 16 * at + 16, :] = jnp.concatenate(halves, axis=0).astype(BF16)
        out[LANES + 8 * PAIRS : BASE, :] = listed

    def piece(chunk):
        return h_piece(h_ref, hm_ref, chunk)

    if paired:
        outs[1][BASE:, 0:LANES] = piece(layer ^ 2)
        outs[1][BASE:, LANES:UNIT] = piece(layer ^ 3)
        outs[2][BASE:, 0:LANES] = piece(layer ^ 1)
        outs[2][BASE:, LANES:UNIT] = piece(layer)
    else:
        for back in range(h_ref.shape[1] // LANES):
            outs[1][back] = piece(lax.rem(layer + back, count))


def prepare(paired, p, p_mask, h, h_mask, *gauss):
    band = p.shape[0]
    base = jax.ShapeDtypeStruct((BASE, band), BF16)
    tall = jax.ShapeDtypeStruct((BASE + h.shape[0], band), BF16)
    if paired:
        outs = (base, tall, tall)
    else:
        outs = (base, jax.ShapeDtypeStruct((h.shape[1] // LANES, h.shape[0], LANES), BF16))
    return pl.pallas_call(
        functools.partial(prepare_kernel, paired),
        out_shape=outs,
        in_specs=[HBM] * 9,
        out_specs=(VMEM,) * len(outs),
        scratch_shapes=[
            pltpu.VMEM(p.shape, p.dtype),
            pltpu.SMEM(p_mask.shape, p_mask.dtype),
            pltpu.VMEM(h.shape, h.dtype),
            pltpu.SMEM(h_mask.shape, h_mask.dtype),
            *[pltpu.VMEM(x.shape, x.dtype) for x in gauss],
            pltpu.VMEM(p.shape, F32),
            pltpu.VMEM((FIELDS * 8, LANES), F32),
            pltpu.VMEM((2 * FIELDS, 2 * PAIRS * LANES), F32),
            pltpu.VMEM((UNIT, 2 * PAIRS * LANES), BF16),
            pltpu.SemaphoreType.DMA((9,)),
        ],
        compiler_params=pltpu.CompilerParams(vmem_limit_bytes=62 * 1024 * 1024),
        name="prepare",
    )(p, p_mask, h, h_mask, *gauss)


class Blocks:
    def __init__(self, refs, num_col, num_layer):
        self.refs = refs
        self.num_col, self.num_layer = num_col, num_layer
        self.paired = len(refs) > 1
        self.col, self.layer = lax.axis_index("col"), lax.axis_index("layer")
        self.total = num_col * num_layer
        self.col_shifts = [0, 1] if num_col == 2 else [0, -1, 1]

    def ident(self, index):
        if not self.paired:
            return index
        return (self.layer ^ (index % 4)) * 2 + (self.col ^ (index // 4))

    def matrix(self, index):
        return self.refs[index][0:LANES, :] if self.paired else self.refs[0][index, 0:LANES, :]

    def slab(self, layer, piece):
        index = layer * self.num_col + piece
        return self.refs[0][index, 0:LANES, :]

    def tile(self, which, side, at):
        rows = pl.ds(LANES + 16 * at, 16)
        if self.paired:
            return self.refs[which * 4 + side][rows, :].astype(F32)
        shift_l = 0 if side == 0 else (1 if side == 1 else -1)
        index = lax.rem(self.layer + shift_l + self.num_layer, self.num_layer) * self.num_col
        index += lax.rem(self.col + self.col_shifts[which] + self.num_col, self.num_col)
        return self.refs[0][index, rows, :].astype(F32)

    def side_shift(self, side):
        if self.paired:
            even = (self.layer % 2) == 0
            return jnp.where(even, 1.0, -1.0) if side == 1 else jnp.where(even, -1.0, 1.0)
        return 1.0 if side == 1 else -1.0

    def sides(self):
        return (1, 3) if self.paired else (1, 2)

    def units(self):
        return [(which, pair) for which in range(len(self.col_shifts)) for pair in range(PAIRS + 1)]

    def listed(self, which):
        halves = []
        for side in self.sides():
            both = self.tile(which, side, PAIRS // 2)[0:FIELDS, :]
            upward = self.side_shift(side) > 0
            halves.append(jnp.where(upward, both[:, 0:LANES], both[:, LANES:UNIT]))
        return jnp.concatenate(halves, axis=1)

    def unit(self, which, pair):
        if pair == PAIRS:
            return Gaussians(self.listed(which))
        half = (pair % 2) * FIELDS
        return Gaussians(self.tile(which, 0, pair // 2)[half : half + FIELDS, :])

    def lifts(self, pair):
        if pair < PAIRS:
            return 0.0
        lane = iota((1, UNIT), 1)
        first, second = self.sides()
        return jnp.where(lane < LANES, self.side_shift(first), self.side_shift(second)) * float(GZ)

    def over(self):
        flags = [
            self.tile(which, side, PAIRS // 2)[FLAG : FLAG + 1, :]
            for which in range(len(self.col_shifts))
            for side in self.sides()
        ]
        return functools.reduce(jnp.maximum, flags)

    def long_steps(self):
        return [(which, side) for which in range(len(self.col_shifts)) for side in self.sides()]


def weigh(blocks, whole, tile):
    band = whole.shape[1]
    onehot = jnp.where(iota((band, UNIT), 0) == tile.row, 1.0, 0.0).astype(BF16)
    found = jnp.dot(whole[...], onehot, preferred_element_type=F32)
    picked = jnp.zeros((LANES, UNIT), F32)
    for index in range(blocks.total):
        mine = tile.block == jnp.asarray(blocks.ident(index)).astype(F32)
        picked = jnp.where(mine, found[index * LANES : index * LANES + LANES, :], picked)
    value = jnp.sum(jnp.where(iota((LANES, UNIT), 0) == tile.lane, picked, 0.0), axis=0, keepdims=True)
    return tile.pref * value


def bell(dist, expo):
    square = dist * dist
    return jnp.where(square < (R + 0.5) ** 2, jnp.exp(-expo * square), 0.0)


RIM_X = tuple(range(R)) + tuple(range(GX + R, GX + 2 * R))
CORE_X = tuple(range(R, GX + R))
ALL_X = tuple(range(GX + 2 * R))


def shapes_x(tile):
    return bell(iota((GX + 2 * R, UNIT), 0) - float(R) - tile.x, tile.expo)


def shapes_y(tile, shift, wraps):
    dy = iota((GY, UNIT), 0) - tile.y - float(shift * GY)
    if wraps:
        dy = jnp.where(dy < -float(GY), dy + 2.0 * GY, dy)
    return bell(dy, tile.expo)


def shapes_z(tile, lift):
    return bell(iota((GZ, UNIT), 0) - tile.z - lift, tile.expo)


def fill_planes(ex, ey, places, at, planeh, planel):
    lanes = pl.ds(at * UNIT, UNIT)
    for spot, x in enumerate(places):
        plane = ex[x : x + 1, :] * ey
        plane_hi = plane.astype(BF16)
        planeh[spot * GY : spot * GY + GY, lanes] = plane_hi
        planel[spot * GY : spot * GY + GY, lanes] = (plane - plane_hi.astype(F32)).astype(BF16)


def fill_depth(ez, coef, at, depth):
    weighed = ez * coef
    lanes = pl.ds(at * UNIT, UNIT)
    weighed_hi = weighed.astype(BF16)
    depth[0:GZ, lanes] = weighed_hi
    depth[GZ : 2 * GZ, lanes] = (weighed - weighed_hi.astype(F32)).astype(BF16)


def set_planes(blocks, tile, which, places, at, planeh, planel):
    wraps = blocks.num_col == 2 and which == 1
    fill_planes(shapes_x(tile), shapes_y(tile, blocks.col_shifts[which], wraps), places, at, planeh, planel)


def summed(planeh, planel, depth):
    first = lax.dot_general(planeh, depth, NT, preferred_element_type=F32)
    second = lax.dot_general(planel, depth[0:GZ, :], NT, preferred_element_type=F32)
    return first[:, 0:GZ] + first[:, GZ : 2 * GZ] + second


def rims_kernel(num_col, num_layer, refs_in, *refs):
    blocks = Blocks(refs[:refs_in], num_col, num_layer)
    low_ref, high_ref, depth, extra, whole, planeh, planel, longh, longl, long_depth, acc = refs[refs_in:]
    for index in range(blocks.total):
        whole[index * LANES : index * LANES + LANES, :] = blocks.matrix(index)
    over = blocks.over()
    for at, (which, pair) in enumerate(blocks.units()):
        tile = blocks.unit(which, pair)
        coef = weigh(blocks, whole, tile)
        if pair == PAIRS:
            coef = jnp.where(over > 0, 0.0, coef)
        set_planes(blocks, tile, which, RIM_X, at, planeh, planel)
        fill_depth(shapes_z(tile, blocks.lifts(pair)), coef, at, depth)
    total = summed(planeh[...], planel[...], depth[...])
    swap = lax.rem(lax.axis_index("row"), 2) * int(lax.axis_size("row") == 4)

    def put(low, high, base_low, base_high):
        low_ref[...] = jnp.where(swap > 0, high, low) + base_low
        high_ref[...] = jnp.where(swap > 0, low, high) + base_high

    put(total[0:HALO, :], total[HALO:, :], 0.0, 0.0)

    @pl.when(jnp.max(over) > 0)
    def _():
        acc[...] = jnp.zeros_like(acc)
        for which, side in blocks.long_steps():

            def step(at, carry):
                both = blocks.tile(which, side, at)
                lift = blocks.side_shift(side) * float(GZ)
                for half in range(2):
                    tile = Gaussians(both[half * FIELDS : half * FIELDS + FIELDS, :])
                    set_planes(blocks, tile, which, ALL_X, 0, longh, longl)
                    fill_depth(shapes_z(tile, lift), weigh(blocks, whole, tile), 0, long_depth)
                    acc[...] += summed(longh[...], longl[...], long_depth[...])
                return carry

            lax.fori_loop(0, PAIRS // 2, step, 0)
        put(acc[0:HALO, :], acc[HALO + CORE : FULL, :], low_ref[...], high_ref[...])
        extra[...] = acc[HALO : HALO + CORE, :]


def rims(arrays, num_col, num_layer):
    gaussians = (2 if num_col == 2 else 3) * (PAIRS + 1) * UNIT
    return pl.pallas_call(
        functools.partial(rims_kernel, num_col, num_layer, len(arrays)),
        out_shape=(
            jax.ShapeDtypeStruct((HALO, GZ), F32),
            jax.ShapeDtypeStruct((HALO, GZ), F32),
            jax.ShapeDtypeStruct((2 * GZ, gaussians), BF16),
            jax.ShapeDtypeStruct((CORE, GZ), F32),
        ),
        in_specs=[VMEM] * len(arrays),
        out_specs=(VMEM,) * 4,
        scratch_shapes=[
            pltpu.VMEM((num_col * num_layer * LANES, arrays[0].shape[-1]), BF16),
            pltpu.VMEM((2 * HALO, gaussians), BF16),
            pltpu.VMEM((2 * HALO, gaussians), BF16),
            pltpu.VMEM((FULL, UNIT), BF16),
            pltpu.VMEM((FULL, UNIT), BF16),
            pltpu.VMEM((2 * GZ, UNIT), BF16),
            pltpu.VMEM((FULL, GZ), F32),
        ],
        compiler_params=PARAMS,
        cost_estimate=pl.CostEstimate(flops=3_000_000_000, bytes_accessed=1_000_000, transcendentals=0),
        name="rims",
    )(*arrays)


def core_kernel(num_col, num_layer, refs_in, *refs):
    blocks = Blocks(refs[:refs_in], num_col, num_layer)
    depth, extra, core_ref, planeh, planel = refs[refs_in:]
    for at, (which, pair) in enumerate(blocks.units()):
        set_planes(blocks, blocks.unit(which, pair), which, CORE_X, at, planeh, planel)
    core_ref[...] = summed(planeh[...], planel[...], depth[...])

    @pl.when(jnp.max(blocks.over()) > 0)
    def _():
        core_ref[...] += extra[...]


def core_part(arrays, depth, extra, num_col, num_layer):
    gaussians = depth.shape[1]
    return pl.pallas_call(
        functools.partial(core_kernel, num_col, num_layer, len(arrays)),
        out_shape=jax.ShapeDtypeStruct((CORE, GZ), F32),
        in_specs=[VMEM] * (len(arrays) + 2),
        out_specs=VMEM,
        scratch_shapes=[pltpu.VMEM((CORE, gaussians), BF16), pltpu.VMEM((CORE, gaussians), BF16)],
        compiler_params=PARAMS,
        cost_estimate=pl.CostEstimate(flops=1_500_000_000, bytes_accessed=1_000_000, transcendentals=0),
        name="core",
    )(*arrays, depth, extra)


def product_kernel(num_row, num_col, num_layer, refs_in, *refs):
    blocks = Blocks(refs[:refs_in], num_col, num_layer)
    h_refs = refs[refs_in : refs_in + num_row]
    out_ref, token_ref, slab = refs[refs_in + num_row :]
    token_ref[...] = jnp.zeros_like(token_ref)
    row = lax.axis_index("row")
    rows = h_refs[0].shape[1]
    for back in range(num_layer):
        for step in range(num_row):
            source = (row ^ step) if num_row == 4 else lax.rem(row - step + num_row, num_row)
            start = pl.multiple_of(source * rows, rows)
            slab[back, pl.ds(start, rows), :] = h_refs[step][back]
    total = jnp.zeros(out_ref.shape, F32)
    for back in range(num_layer):
        for piece in range(num_col):
            if blocks.paired:
                left = blocks.matrix(piece * 4 + back)
                start = pl.multiple_of((blocks.col ^ piece) * LANES, LANES)
            else:
                source = lax.rem(blocks.layer - back + num_layer, num_layer)
                left = blocks.slab(source, piece)
                start = piece * LANES
            right = slab[back, pl.ds(start, LANES), :]
            total += lax.dot_general(left, right, TN, preferred_element_type=F32)
    out_ref[...] = total.astype(BF16)


def multiply(arrays, parts, num_row, num_col, num_layer):
    return pl.pallas_call(
        functools.partial(product_kernel, num_row, num_col, num_layer, len(arrays)),
        out_shape=(
            jax.ShapeDtypeStruct((arrays[0].shape[-1], LANES), BF16),
            jax.ShapeDtypeStruct((8, LANES), F32),
        ),
        in_specs=[VMEM] * (num_row + len(arrays)),
        out_specs=(VMEM, VMEM),
        scratch_shapes=[pltpu.VMEM((num_layer, num_col * LANES, LANES), BF16)],
        compiler_params=PARAMS,
        cost_estimate=pl.CostEstimate(flops=500_000_000, bytes_accessed=1_000_000, transcendentals=0),
        name="multiply",
    )(*arrays, *parts)


def settle_kernel(block_ref, out_ref):
    out_ref[...] = block_ref[...]


def settle(block):
    return pl.pallas_call(
        settle_kernel,
        out_shape=jax.ShapeDtypeStruct(block.shape, BF16),
        in_specs=[VMEM],
        out_specs=VMEM,
        compiler_params=PARAMS,
        cost_estimate=pl.CostEstimate(flops=1000, bytes_accessed=1000, transcendentals=0),
        name="settle",
    )(block)


def stack_kernel(own_ref, near_ref, far_ref, both_ref, out_ref):
    out_ref[0] = own_ref[BASE:, LANES:UNIT]
    out_ref[1] = near_ref[BASE:, 0:LANES]
    out_ref[2] = far_ref[BASE:, 0:LANES]
    out_ref[3] = both_ref[BASE:, LANES:UNIT]


def stack(own, near, far, both):
    return pl.pallas_call(
        stack_kernel,
        out_shape=jax.ShapeDtypeStruct((4, own.shape[0] - BASE, LANES), BF16),
        in_specs=[VMEM] * 4,
        out_specs=VMEM,
        compiler_params=PARAMS,
        name="stack",
    )(own, near, far, both)


def fold_kernel(core_ref, below_ref, above_ref, after_ref, out_ref):
    swap = lax.rem(lax.axis_index("row"), 2) * int(lax.axis_size("row") == 4)
    below, above = below_ref[...], above_ref[...]
    out_ref[0:HALO, :] = core_ref[0:HALO, :] + jnp.where(swap > 0, above, below)
    out_ref[HALO : CORE - HALO, :] = core_ref[HALO : CORE - HALO, :]
    out_ref[CORE - HALO : CORE, :] = core_ref[CORE - HALO : CORE, :] + jnp.where(swap > 0, below, above)


def fold(core, below, above, after):
    return pl.pallas_call(
        fold_kernel,
        out_shape=jax.ShapeDtypeStruct((CORE, GZ), F32),
        in_specs=[VMEM] * 4,
        out_specs=VMEM,
        compiler_params=PARAMS,
        cost_estimate=pl.CostEstimate(flops=1_000_000, bytes_accessed=400_000, transcendentals=0),
        name="fold",
    )(core, below, above, after)


def shifted(value, axis, count, step):
    return lax.ppermute(value, axis, [(i, (i + step) % count) for i in range(count)])


def crossed(value, col_bit, layer_bits):
    pairs = [(c * 4 + l, (c ^ col_bit) * 4 + (l ^ layer_bits)) for c in range(2) for l in range(4)]
    return lax.ppermute(value, ("col", "layer"), pairs)


def gather_paired(base, tall_y, tall_core):
    got_x = crossed(base, 1, 0)
    got_y = crossed(tall_y, 0, 2)
    got_xy = crossed(base, 1, 2)
    near = crossed(tall_core, 0, 1)
    near_x = crossed(got_x, 0, 1)
    near_y = crossed(got_y, 0, 1)
    near_xy = crossed(got_xy, 0, 1)
    return [tall_core, near, got_y, near_y, got_x, near_x, got_xy, near_xy]


def on_device(p_slabs, p_mask, h_slabs, h_mask, gauss_row, gauss_col, gauss_cell, gauss_expo, gauss_pref):
    num_row, num_col, num_layer = (lax.axis_size(axis) for axis in ("row", "col", "layer"))
    paired = num_col == 2 and num_layer == 4
    flat = [x.reshape(8, LANES) for x in (gauss_row, gauss_col, gauss_cell, gauss_expo, gauss_pref)]
    made = prepare(paired, p_slabs[0], p_mask[0].T, h_slabs[0], h_mask[0], *flat)
    if paired:
        arrays = gather_paired(*made[:2], settle(made[2]))
        mine = stack(*arrays[:4])
    else:
        base, pieces = made
        arrays = [lax.all_gather(base, ("layer", "col"), axis=0)]
        mine = [pieces[0]] + [shifted(pieces[step], "layer", num_layer, step) for step in range(1, num_layer)]
        mine = jnp.stack(mine)
    low, high, depth, extra = rims(arrays, num_col, num_layer)
    if num_row == 4:
        near, far = (lax.ppermute(mine, "row", [(i, i ^ step) for i in range(4)]) for step in (1, 2))
        parts = [mine, near, far, lax.ppermute(far, "row", [(i, i ^ 1) for i in range(4)])]
    else:
        parts = [mine] + [shifted(mine, "row", num_row, step) for step in range(1, num_row)]
    if num_row == 4:
        below = lax.ppermute(low, "row", [(i, i ^ 3) for i in range(4)])
        above = lax.ppermute(high, "row", [(i, i ^ 1) for i in range(4)])
    else:
        below = shifted(high, "row", num_row, 1)
        above = shifted(low, "row", num_row, num_row - 1)
    core = core_part(arrays, depth, extra, num_col, num_layer)
    product, token = multiply(arrays, parts, num_row, num_col, num_layer)
    density = fold(core, below, above, token).reshape(GX, GY, GZ)
    return (product, density)


def solution(mesh):
    placed = (P("layer", "row", "col"),) * 4 + (P(("row", "col", "layer")),) * 5
    return jax.shard_map(
        on_device,
        mesh=mesh,
        in_specs=placed,
        out_specs=(P("row", ("col", "layer")), P("row", "col", "layer")),
        check_vma=False,
    )
```

```python
import functools

import jax
import jax.numpy as jnp
from jax import lax
from jax.experimental import pallas as pl
from jax.experimental.pallas import tpu as pltpu
from jax.sharding import PartitionSpec as P

BS = 32
GX = 16
GY = 16
GZ = 128
R = 4
LANES = 128
F32 = jnp.float32
BF16 = jnp.bfloat16
HALO = R * GY
CORE = GX * GY
FULL = CORE + 2 * HALO
UNIT = 2 * LANES
PAIRS = 4
META = (PAIRS // 2 + 1) * 16
BASE = LANES + META
FLAG = 8
FIELDS = 8
VMEM = pl.BlockSpec(memory_space=pltpu.VMEM)
HBM = pl.BlockSpec(memory_space=pltpu.HBM)
PARAMS = pltpu.CompilerParams(vmem_limit_bytes=40 * 1024 * 1024)
NT = (((1,), (1,)), ((), ()))
TN = (((0,), (0,)), ((), ()))


def iota(shape, axis):
    return lax.broadcasted_iota(jnp.int32, shape, axis).astype(F32)


def split2(value):
    first = value.astype(BF16).astype(F32)
    return first, value - first


class Gaussians:
    def __init__(self, tile):
        first, second, third, fourth = (tile[at : at + 1, :].astype(jnp.int32) for at in range(4))
        first, second, third = first + 256, second + 256, third + 256
        column = third + ((fourth >> 7) << 9) + ((second >> 8) << 10) + ((first >> 8) << 11)
        cell = second & 255
        self.row = (first & 255).astype(F32)
        self.block = (column // LANES).astype(F32)
        self.lane = (column % LANES).astype(F32)
        self.x = (cell // GY).astype(F32)
        self.y = (cell % GY).astype(F32)
        self.z = (fourth & 127).astype(F32)
        self.expo = tile[4:5, :] + tile[5:6, :]
        self.pref = tile[6:7, :] + tile[7:8, :]


def masked(values, bits):
    lane = lax.broadcasted_iota(jnp.int32, values.shape, 1) // BS
    keep = jnp.zeros(values.shape, jnp.int32)
    for piece, bit in enumerate(bits):
        keep = jnp.where(lane == piece, bit, keep)
    return jnp.where(keep > 0, values.astype(F32), 0.0)


def ranks(flags):
    up = (iota((LANES, LANES), 0) <= iota((LANES, LANES), 1)).astype(F32).astype(BF16)
    ones = jnp.ones((LANES, LANES), BF16)
    within = jnp.dot(flags.astype(BF16), up, preferred_element_type=F32)
    totals = jnp.dot(flags.astype(BF16), ones, preferred_element_type=F32)
    row, other = iota((16, 16), 0), iota((16, 16), 1)
    same = (row < 8) == (other < 8)
    before = jnp.where(same & (other < row), 1.0, 0.0).astype(BF16)
    every = jnp.where(same, 1.0, 0.0).astype(BF16)
    earlier = jnp.dot(before, totals.astype(BF16), preferred_element_type=F32)
    count = jnp.dot(every, totals.astype(BF16), preferred_element_type=F32)
    return jnp.where(flags > 0, within + earlier - 1.0, -1.0), count


def h_piece(h_ref, hm_ref, chunk):
    pieces = LANES // BS
    out = []
    for block in range(h_ref.shape[0] // BS):
        bits = [hm_ref[block, chunk * pieces + at] for at in range(pieces)]
        value = h_ref[pl.ds(block * BS, BS), pl.ds(pl.multiple_of(chunk * LANES, LANES), LANES)]
        out.append(masked(value, bits).astype(BF16))
    return jnp.concatenate(out, axis=0)


def prepare_kernel(paired, *refs):
    sources, outs, refs = refs[:9], refs[9:-14], refs[-14:]
    landed, (tmp, fields, matrix, onehot, sems) = refs[:9], refs[9:]
    copies = [pltpu.make_async_copy(src, dst, sems.at[at]) for at, (src, dst) in enumerate(zip(sources, landed))]
    for copy in copies:
        copy.start()
    for copy in copies:
        copy.wait()
    p_ref, pm_ref, h_ref, hm_ref, row_ref, col_ref, cell_ref, expo_ref, pref_ref = landed
    layer = lax.axis_index("layer")
    count = lax.axis_size("layer")
    band = p_ref.shape[0]
    for block in range(band // BS):
        rows = pl.ds(block * BS, BS)
        tmp[rows, :] = masked(p_ref[rows, :], [pm_ref[piece, block] for piece in range(LANES // BS)])
    turned = tmp[...].T.astype(BF16)
    col = col_ref[...]
    cell = cell_ref[...]
    cell_z = (cell % GZ).astype(F32)
    values = [
        (row_ref[...] + ((col >> 11) & 1) * 256 - 256).astype(F32),
        (cell // GZ + ((col >> 10) & 1) * 256 - 256).astype(F32),
        ((col & 511) - 256).astype(F32),
        (cell % GZ + ((col >> 9) & 1) * 128).astype(F32),
        *split2(expo_ref[...]),
        *split2(pref_ref[...]),
    ]
    for index in range(FIELDS):
        fields[8 * index : 8 * index + 8, :] = values[index]
    for part in range(2 * PAIRS):
        matrix[0:FIELDS, part * LANES : part * LANES + LANES] = fields[pl.ds(part, FIELDS, stride=8), :]
    matrix[FIELDS : 2 * FIELDS, :] = jnp.zeros((FIELDS, 2 * PAIRS * LANES), F32)
    faces = jnp.concatenate([jnp.where(cell_z < R, 1.0, 0.0), jnp.where(cell_z >= GZ - R, 1.0, 0.0)], axis=0)
    place, many = ranks(faces)
    slot = iota((LANES, LANES), 0)
    for part in range(2 * PAIRS):
        lanes = pl.ds(part * LANES, LANES)
        for face in range(2):
            hit = slot == place[face * 8 + part : face * 8 + part + 1, :]
            onehot[face * LANES : face * LANES + LANES, lanes] = jnp.where(hit, 1.0, 0.0).astype(BF16)
    listed = lax.dot_general(matrix[...].astype(BF16), onehot[...], NT, preferred_element_type=F32)
    over = jnp.where(jnp.max(many, axis=0, keepdims=True) > LANES, 1.0, 0.0)
    over = jnp.concatenate([over, over], axis=1)
    listed = jnp.where(iota(listed.shape, 0) == FLAG, over, listed).astype(BF16)
    copies = outs[:3] if paired else outs[:1]
    for out in copies:
        out[0:LANES, :] = turned
        for at in range(PAIRS // 2):
            halves = [matrix[0:FIELDS, pair * UNIT : pair * UNIT + UNIT] for pair in (2 * at, 2 * at + 1)]
            out[LANES + 16 * at : LANES + 16 * at + 16, :] = jnp.concatenate(halves, axis=0).astype(BF16)
        out[LANES + 8 * PAIRS : BASE, :] = listed

    def piece(chunk):
        return h_piece(h_ref, hm_ref, chunk)

    if paired:
        outs[1][BASE:, 0:LANES] = piece(layer ^ 2)
        outs[1][BASE:, LANES:UNIT] = piece(layer ^ 3)
        outs[2][BASE:, 0:LANES] = piece(layer ^ 1)
        outs[2][BASE:, LANES:UNIT] = piece(layer)
    else:
        for back in range(h_ref.shape[1] // LANES):
            outs[1][back] = piece(lax.rem(layer + back, count))


def prepare(paired, p, p_mask, h, h_mask, *gauss):
    band = p.shape[0]
    base = jax.ShapeDtypeStruct((BASE, band), BF16)
    tall = jax.ShapeDtypeStruct((BASE + h.shape[0], band), BF16)
    if paired:
        outs = (base, tall, tall)
    else:
        outs = (base, jax.ShapeDtypeStruct((h.shape[1] // LANES, h.shape[0], LANES), BF16))
    return pl.pallas_call(
        functools.partial(prepare_kernel, paired),
        out_shape=outs,
        in_specs=[HBM] * 9,
        out_specs=(VMEM,) * len(outs),
        scratch_shapes=[
            pltpu.VMEM(p.shape, p.dtype),
            pltpu.SMEM(p_mask.shape, p_mask.dtype),
            pltpu.VMEM(h.shape, h.dtype),
            pltpu.SMEM(h_mask.shape, h_mask.dtype),
            *[pltpu.VMEM(x.shape, x.dtype) for x in gauss],
            pltpu.VMEM(p.shape, F32),
            pltpu.VMEM((FIELDS * 8, LANES), F32),
            pltpu.VMEM((2 * FIELDS, 2 * PAIRS * LANES), F32),
            pltpu.VMEM((UNIT, 2 * PAIRS * LANES), BF16),
            pltpu.SemaphoreType.DMA((9,)),
        ],
        compiler_params=pltpu.CompilerParams(vmem_limit_bytes=62 * 1024 * 1024),
        name="prepare",
    )(p, p_mask, h, h_mask, *gauss)


class Blocks:
    def __init__(self, refs, num_col, num_layer):
        self.refs = refs
        self.num_col, self.num_layer = num_col, num_layer
        self.paired = len(refs) > 1
        self.col, self.layer = lax.axis_index("col"), lax.axis_index("layer")
        self.total = num_col * num_layer
        self.col_shifts = [0, 1] if num_col == 2 else [0, -1, 1]

    def ident(self, index):
        if not self.paired:
            return index
        return (self.layer ^ (index % 4)) * 2 + (self.col ^ (index // 4))

    def matrix(self, index):
        return self.refs[index][0:LANES, :] if self.paired else self.refs[0][index, 0:LANES, :]

    def slab(self, layer, piece):
        index = layer * self.num_col + piece
        return self.refs[0][index, 0:LANES, :]

    def tile(self, which, side, at):
        rows = pl.ds(LANES + 16 * at, 16)
        if self.paired:
            return self.refs[which * 4 + side][rows, :].astype(F32)
        shift_l = 0 if side == 0 else (1 if side == 1 else -1)
        index = lax.rem(self.layer + shift_l + self.num_layer, self.num_layer) * self.num_col
        index += lax.rem(self.col + self.col_shifts[which] + self.num_col, self.num_col)
        return self.refs[0][index, rows, :].astype(F32)

    def side_shift(self, side):
        if self.paired:
            even = (self.layer % 2) == 0
            return jnp.where(even, 1.0, -1.0) if side == 1 else jnp.where(even, -1.0, 1.0)
        return 1.0 if side == 1 else -1.0

    def sides(self):
        return (1, 3) if self.paired else (1, 2)

    def units(self):
        return [(which, pair) for which in range(len(self.col_shifts)) for pair in range(PAIRS + 1)]

    def listed(self, which):
        halves = []
        for side in self.sides():
            both = self.tile(which, side, PAIRS // 2)[0:FIELDS, :]
            upward = self.side_shift(side) > 0
            halves.append(jnp.where(upward, both[:, 0:LANES], both[:, LANES:UNIT]))
        return jnp.concatenate(halves, axis=1)

    def unit(self, which, pair):
        if pair == PAIRS:
            return Gaussians(self.listed(which))
        half = (pair % 2) * FIELDS
        return Gaussians(self.tile(which, 0, pair // 2)[half : half + FIELDS, :])

    def lifts(self, pair):
        if pair < PAIRS:
            return 0.0
        lane = iota((1, UNIT), 1)
        first, second = self.sides()
        return jnp.where(lane < LANES, self.side_shift(first), self.side_shift(second)) * float(GZ)

    def over(self):
        flags = [
            self.tile(which, side, PAIRS // 2)[FLAG : FLAG + 1, :]
            for which in range(len(self.col_shifts))
            for side in self.sides()
        ]
        return functools.reduce(jnp.maximum, flags)

    def long_steps(self):
        return [(which, side) for which in range(len(self.col_shifts)) for side in self.sides()]


def weigh(blocks, whole, tile):
    band = whole.shape[1]
    onehot = jnp.where(iota((band, UNIT), 0) == tile.row, 1.0, 0.0).astype(BF16)
    found = jnp.dot(whole[...], onehot, preferred_element_type=F32)
    picked = jnp.zeros((LANES, UNIT), F32)
    for index in range(blocks.total):
        mine = tile.block == jnp.asarray(blocks.ident(index)).astype(F32)
        picked = jnp.where(mine, found[index * LANES : index * LANES + LANES, :], picked)
    value = jnp.sum(jnp.where(iota((LANES, UNIT), 0) == tile.lane, picked, 0.0), axis=0, keepdims=True)
    return tile.pref * value


def bell(dist, expo):
    square = dist * dist
    return jnp.where(square < (R + 0.5) ** 2, jnp.exp(-expo * square), 0.0)


RIM_X = tuple(range(R)) + tuple(range(GX + R, GX + 2 * R))
CORE_X = tuple(range(R, GX + R))
ALL_X = tuple(range(GX + 2 * R))


def shapes_x(tile):
    return bell(iota((GX + 2 * R, UNIT), 0) - float(R) - tile.x, tile.expo)


def shapes_y(tile, shift, wraps):
    dy = iota((GY, UNIT), 0) - tile.y - float(shift * GY)
    if wraps:
        dy = jnp.where(dy < -float(GY), dy + 2.0 * GY, dy)
    return bell(dy, tile.expo)


def shapes_z(tile, lift):
    return bell(iota((GZ, UNIT), 0) - tile.z - lift, tile.expo)


def fill_planes(ex, ey, places, at, planeh, planel):
    lanes = pl.ds(at * UNIT, UNIT)
    for spot, x in enumerate(places):
        plane = ex[x : x + 1, :] * ey
        plane_hi = plane.astype(BF16)
        planeh[spot * GY : spot * GY + GY, lanes] = plane_hi
        planel[spot * GY : spot * GY + GY, lanes] = (plane - plane_hi.astype(F32)).astype(BF16)


def fill_depth(ez, coef, at, depth):
    weighed = ez * coef
    lanes = pl.ds(at * UNIT, UNIT)
    weighed_hi = weighed.astype(BF16)
    depth[0:GZ, lanes] = weighed_hi
    depth[GZ : 2 * GZ, lanes] = (weighed - weighed_hi.astype(F32)).astype(BF16)


def set_planes(blocks, tile, which, places, at, planeh, planel):
    wraps = blocks.num_col == 2 and which == 1
    fill_planes(shapes_x(tile), shapes_y(tile, blocks.col_shifts[which], wraps), places, at, planeh, planel)


def summed(planeh, planel, depth):
    first = lax.dot_general(planeh, depth, NT, preferred_element_type=F32)
    second = lax.dot_general(planel, depth[0:GZ, :], NT, preferred_element_type=F32)
    return first[:, 0:GZ] + first[:, GZ : 2 * GZ] + second


def rims_kernel(num_col, num_layer, refs_in, *refs):
    blocks = Blocks(refs[:refs_in], num_col, num_layer)
    low_ref, high_ref, depth, extra, whole, planeh, planel, longh, longl, long_depth, acc = refs[refs_in:]
    for index in range(blocks.total):
        whole[index * LANES : index * LANES + LANES, :] = blocks.matrix(index)
    over = blocks.over()
    for at, (which, pair) in enumerate(blocks.units()):
        tile = blocks.unit(which, pair)
        coef = weigh(blocks, whole, tile)
        if pair == PAIRS:
            coef = jnp.where(over > 0, 0.0, coef)
        set_planes(blocks, tile, which, RIM_X, at, planeh, planel)
        fill_depth(shapes_z(tile, blocks.lifts(pair)), coef, at, depth)
    total = summed(planeh[...], planel[...], depth[...])
    swap = lax.rem(lax.axis_index("row"), 2) * int(lax.axis_size("row") == 4)

    def put(low, high, base_low, base_high):
        low_ref[...] = jnp.where(swap > 0, high, low) + base_low
        high_ref[...] = jnp.where(swap > 0, low, high) + base_high

    put(total[0:HALO, :], total[HALO:, :], 0.0, 0.0)

    @pl.when(jnp.max(over) > 0)
    def _():
        acc[...] = jnp.zeros_like(acc)
        for which, side in blocks.long_steps():

            def step(at, carry):
                both = blocks.tile(which, side, at)
                lift = blocks.side_shift(side) * float(GZ)
                for half in range(2):
                    tile = Gaussians(both[half * FIELDS : half * FIELDS + FIELDS, :])
                    set_planes(blocks, tile, which, ALL_X, 0, longh, longl)
                    fill_depth(shapes_z(tile, lift), weigh(blocks, whole, tile), 0, long_depth)
                    acc[...] += summed(longh[...], longl[...], long_depth[...])
                return carry

            lax.fori_loop(0, PAIRS // 2, step, 0)
        put(acc[0:HALO, :], acc[HALO + CORE : FULL, :], low_ref[...], high_ref[...])
        extra[...] = acc[HALO : HALO + CORE, :]


def rims(arrays, num_col, num_layer):
    gaussians = (2 if num_col == 2 else 3) * (PAIRS + 1) * UNIT
    return pl.pallas_call(
        functools.partial(rims_kernel, num_col, num_layer, len(arrays)),
        out_shape=(
            jax.ShapeDtypeStruct((HALO, GZ), F32),
            jax.ShapeDtypeStruct((HALO, GZ), F32),
            jax.ShapeDtypeStruct((2 * GZ, gaussians), BF16),
            jax.ShapeDtypeStruct((CORE, GZ), F32),
        ),
        in_specs=[VMEM] * len(arrays),
        out_specs=(VMEM,) * 4,
        scratch_shapes=[
            pltpu.VMEM((num_col * num_layer * LANES, arrays[0].shape[-1]), BF16),
            pltpu.VMEM((2 * HALO, gaussians), BF16),
            pltpu.VMEM((2 * HALO, gaussians), BF16),
            pltpu.VMEM((FULL, UNIT), BF16),
            pltpu.VMEM((FULL, UNIT), BF16),
            pltpu.VMEM((2 * GZ, UNIT), BF16),
            pltpu.VMEM((FULL, GZ), F32),
        ],
        compiler_params=PARAMS,
        cost_estimate=pl.CostEstimate(flops=3_000_000_000, bytes_accessed=1_000_000, transcendentals=0),
        name="rims",
    )(*arrays)


def core_kernel(num_col, num_layer, refs_in, *refs):
    blocks = Blocks(refs[:refs_in], num_col, num_layer)
    depth, extra, core_ref, planeh, planel = refs[refs_in:]
    for at, (which, pair) in enumerate(blocks.units()):
        set_planes(blocks, blocks.unit(which, pair), which, CORE_X, at, planeh, planel)
    core_ref[...] = summed(planeh[...], planel[...], depth[...])

    @pl.when(jnp.max(blocks.over()) > 0)
    def _():
        core_ref[...] += extra[...]


def core_part(arrays, depth, extra, num_col, num_layer):
    gaussians = depth.shape[1]
    return pl.pallas_call(
        functools.partial(core_kernel, num_col, num_layer, len(arrays)),
        out_shape=jax.ShapeDtypeStruct((CORE, GZ), F32),
        in_specs=[VMEM] * (len(arrays) + 2),
        out_specs=VMEM,
        scratch_shapes=[pltpu.VMEM((CORE, gaussians), BF16), pltpu.VMEM((CORE, gaussians), BF16)],
        compiler_params=PARAMS,
        cost_estimate=pl.CostEstimate(flops=1_500_000_000, bytes_accessed=1_000_000, transcendentals=0),
        name="core",
    )(*arrays, depth, extra)


def row_steps(num_row):
    return [0, 1, num_row - 1] + list(range(2, num_row - 1))


def product_kernel(num_row, num_col, num_layer, refs_in, *refs):
    blocks = Blocks(refs[:refs_in], num_col, num_layer)
    h_refs = refs[refs_in : refs_in + num_row]
    out_ref, token_ref, slab = refs[refs_in + num_row :]
    token_ref[...] = jnp.zeros_like(token_ref)
    row = lax.axis_index("row")
    rows = h_refs[0].shape[1]
    for back in range(num_layer):
        for spot, step in enumerate(row_steps(num_row)):
            start = pl.multiple_of((row ^ step) * rows, rows)
            slab[back, pl.ds(start, rows), :] = h_refs[spot][back]
    total = jnp.zeros(out_ref.shape, F32)
    for back in range(num_layer):
        for piece in range(num_col):
            if blocks.paired:
                left = blocks.matrix(piece * 4 + back)
                start = pl.multiple_of((blocks.col ^ piece) * LANES, LANES)
            else:
                source = lax.rem(blocks.layer - back + num_layer, num_layer)
                left = blocks.slab(source, piece)
                start = piece * LANES
            right = slab[back, pl.ds(start, LANES), :]
            total += lax.dot_general(left, right, TN, preferred_element_type=F32)
    out_ref[...] = total.astype(BF16)


def multiply(arrays, parts, num_row, num_col, num_layer):
    return pl.pallas_call(
        functools.partial(product_kernel, num_row, num_col, num_layer, len(arrays)),
        out_shape=(
            jax.ShapeDtypeStruct((arrays[0].shape[-1], LANES), BF16),
            jax.ShapeDtypeStruct((8, LANES), F32),
        ),
        in_specs=[VMEM] * (num_row + len(arrays)),
        out_specs=(VMEM, VMEM),
        scratch_shapes=[pltpu.VMEM((num_layer, num_col * LANES, LANES), BF16)],
        compiler_params=PARAMS,
        cost_estimate=pl.CostEstimate(flops=500_000_000, bytes_accessed=1_000_000, transcendentals=0),
        name="multiply",
    )(*arrays, *parts)


def settle_kernel(block_ref, out_ref):
    out_ref[...] = block_ref[...]


def settle(block):
    return pl.pallas_call(
        settle_kernel,
        out_shape=jax.ShapeDtypeStruct(block.shape, BF16),
        in_specs=[VMEM],
        out_specs=VMEM,
        compiler_params=PARAMS,
        cost_estimate=pl.CostEstimate(flops=1000, bytes_accessed=1000, transcendentals=0),
        name="settle",
    )(block)


def stack_kernel(own_ref, near_ref, far_ref, both_ref, out_ref):
    out_ref[0] = own_ref[BASE:, LANES:UNIT]
    out_ref[1] = near_ref[BASE:, 0:LANES]
    out_ref[2] = far_ref[BASE:, 0:LANES]
    out_ref[3] = both_ref[BASE:, LANES:UNIT]


def stack(own, near, far, both):
    return pl.pallas_call(
        stack_kernel,
        out_shape=jax.ShapeDtypeStruct((4, own.shape[0] - BASE, LANES), BF16),
        in_specs=[VMEM] * 4,
        out_specs=VMEM,
        compiler_params=PARAMS,
        name="stack",
    )(own, near, far, both)


def fold_kernel(core_ref, below_ref, above_ref, after_ref, out_ref):
    swap = lax.rem(lax.axis_index("row"), 2) * int(lax.axis_size("row") == 4)
    below, above = below_ref[...], above_ref[...]
    out_ref[0:HALO, :] = core_ref[0:HALO, :] + jnp.where(swap > 0, above, below)
    out_ref[HALO : CORE - HALO, :] = core_ref[HALO : CORE - HALO, :]
    out_ref[CORE - HALO : CORE, :] = core_ref[CORE - HALO : CORE, :] + jnp.where(swap > 0, below, above)


def fold(core, below, above, after):
    return pl.pallas_call(
        fold_kernel,
        out_shape=jax.ShapeDtypeStruct((CORE, GZ), F32),
        in_specs=[VMEM] * 4,
        out_specs=VMEM,
        compiler_params=PARAMS,
        cost_estimate=pl.CostEstimate(flops=1_000_000, bytes_accessed=400_000, transcendentals=0),
        name="fold",
    )(core, below, above, after)


def shifted(value, axis, count, step):
    return lax.ppermute(value, axis, [(i, (i + step) % count) for i in range(count)])


def crossed(value, col_bit, layer_bits):
    pairs = [(c * 4 + l, (c ^ col_bit) * 4 + (l ^ layer_bits)) for c in range(2) for l in range(4)]
    return lax.ppermute(value, ("col", "layer"), pairs)


def gather_paired(base, tall_y, tall_core):
    got_x = crossed(base, 1, 0)
    got_y = crossed(tall_y, 0, 2)
    got_xy = crossed(base, 1, 2)
    near = crossed(tall_core, 0, 1)
    near_x = crossed(got_x, 0, 1)
    near_y = crossed(got_y, 0, 1)
    near_xy = crossed(got_xy, 0, 1)
    return [tall_core, near, got_y, near_y, got_x, near_x, got_xy, near_xy]


def on_device(p_slabs, p_mask, h_slabs, h_mask, gauss_row, gauss_col, gauss_cell, gauss_expo, gauss_pref):
    num_row, num_col, num_layer = (lax.axis_size(axis) for axis in ("row", "col", "layer"))
    paired = num_col == 2 and num_layer == 4
    flat = [x.reshape(8, LANES) for x in (gauss_row, gauss_col, gauss_cell, gauss_expo, gauss_pref)]
    made = prepare(paired, p_slabs[0], p_mask[0].T, h_slabs[0], h_mask[0], *flat)
    if paired:
        arrays = gather_paired(*made[:2], settle(made[2]))
        mine = stack(*arrays[:4])
    else:
        base, pieces = made
        arrays = [lax.all_gather(base, ("layer", "col"), axis=0)]
        mine = [pieces[0]] + [shifted(pieces[step], "layer", num_layer, step) for step in range(1, num_layer)]
        mine = jnp.stack(mine)
    low, high, depth, extra = rims(arrays, num_col, num_layer)
    parts = [mine] + [
        lax.ppermute(mine, "row", [(i, i ^ step) for i in range(num_row)]) for step in row_steps(num_row)[1:]
    ]
    if num_row == 4:
        below = lax.ppermute(low, "row", [(i, i ^ 3) for i in range(4)])
        above = lax.ppermute(high, "row", [(i, i ^ 1) for i in range(4)])
    else:
        below = shifted(high, "row", num_row, 1)
        above = shifted(low, "row", num_row, num_row - 1)
    core = core_part(arrays, depth, extra, num_col, num_layer)
    product, token = multiply(arrays, parts, num_row, num_col, num_layer)
    density = fold(core, below, above, token).reshape(GX, GY, GZ)
    return (product, density)


def solution(mesh):
    placed = (P("layer", "row", "col"),) * 4 + (P(("row", "col", "layer")),) * 5
    return jax.shard_map(
        on_device,
        mesh=mesh,
        in_specs=placed,
        out_specs=(P("row", ("col", "layer")), P("row", "col", "layer")),
        check_vma=False,
    )
```

```python
import functools

import jax
import jax.numpy as jnp
from jax import lax
from jax.experimental import pallas as pl
from jax.experimental.pallas import tpu as pltpu
from jax.sharding import PartitionSpec as P

BS = 32
GX = 16
GY = 16
GZ = 128
R = 4
LANES = 128
F32 = jnp.float32
BF16 = jnp.bfloat16
HALO = R * GY
CORE = GX * GY
FULL = CORE + 2 * HALO
UNIT = 2 * LANES
PAIRS = 4
META = (PAIRS // 2 + 1) * 16
BASE = LANES + META
FLAG = 8
FIELDS = 8
VMEM = pl.BlockSpec(memory_space=pltpu.VMEM)
HBM = pl.BlockSpec(memory_space=pltpu.HBM)
PARAMS = pltpu.CompilerParams(vmem_limit_bytes=40 * 1024 * 1024)
NT = (((1,), (1,)), ((), ()))
TN = (((0,), (0,)), ((), ()))


def iota(shape, axis):
    return lax.broadcasted_iota(jnp.int32, shape, axis).astype(F32)


def split2(value):
    first = value.astype(BF16).astype(F32)
    return first, value - first


class Gaussians:
    def __init__(self, tile):
        first, second, third, fourth = (tile[at : at + 1, :].astype(jnp.int32) for at in range(4))
        first, second, third = first + 256, second + 256, third + 256
        column = third + ((fourth >> 7) << 9) + ((second >> 8) << 10) + ((first >> 8) << 11)
        cell = second & 255
        self.row = (first & 255).astype(F32)
        self.block = (column // LANES).astype(F32)
        self.lane = (column % LANES).astype(F32)
        self.x = (cell // GY).astype(F32)
        self.y = (cell % GY).astype(F32)
        self.z = (fourth & 127).astype(F32)
        self.expo = tile[4:5, :] + tile[5:6, :]
        self.pref = tile[6:7, :] + tile[7:8, :]


def masked(values, bits):
    lane = lax.broadcasted_iota(jnp.int32, values.shape, 1) // BS
    keep = jnp.zeros(values.shape, jnp.int32)
    for piece, bit in enumerate(bits):
        keep = jnp.where(lane == piece, bit, keep)
    return jnp.where(keep > 0, values.astype(F32), 0.0)


def ranks(flags):
    up = (iota((LANES, LANES), 0) <= iota((LANES, LANES), 1)).astype(F32).astype(BF16)
    ones = jnp.ones((LANES, LANES), BF16)
    within = jnp.dot(flags.astype(BF16), up, preferred_element_type=F32)
    totals = jnp.dot(flags.astype(BF16), ones, preferred_element_type=F32)
    row, other = iota((16, 16), 0), iota((16, 16), 1)
    same = (row < 8) == (other < 8)
    before = jnp.where(same & (other < row), 1.0, 0.0).astype(BF16)
    every = jnp.where(same, 1.0, 0.0).astype(BF16)
    earlier = jnp.dot(before, totals.astype(BF16), preferred_element_type=F32)
    count = jnp.dot(every, totals.astype(BF16), preferred_element_type=F32)
    return jnp.where(flags > 0, within + earlier - 1.0, -1.0), count


def h_piece(h_ref, hm_ref, chunk):
    pieces = LANES // BS
    out = []
    for block in range(h_ref.shape[0] // BS):
        bits = [hm_ref[block, chunk * pieces + at] for at in range(pieces)]
        value = h_ref[pl.ds(block * BS, BS), pl.ds(pl.multiple_of(chunk * LANES, LANES), LANES)]
        out.append(masked(value, bits).astype(BF16))
    return jnp.concatenate(out, axis=0)


def prepare_kernel(paired, *refs):
    sources, outs, refs = refs[:9], refs[9:-14], refs[-14:]
    landed, (tmp, fields, matrix, onehot, sems) = refs[:9], refs[9:]
    copies = [pltpu.make_async_copy(src, dst, sems.at[at]) for at, (src, dst) in enumerate(zip(sources, landed))]
    for copy in copies:
        copy.start()
    for copy in copies:
        copy.wait()
    p_ref, pm_ref, h_ref, hm_ref, row_ref, col_ref, cell_ref, expo_ref, pref_ref = landed
    layer = lax.axis_index("layer")
    count = lax.axis_size("layer")
    band = p_ref.shape[0]
    for block in range(band // BS):
        rows = pl.ds(block * BS, BS)
        tmp[rows, :] = masked(p_ref[rows, :], [pm_ref[piece, block] for piece in range(LANES // BS)])
    turned = tmp[...].T.astype(BF16)
    col = col_ref[...]
    cell = cell_ref[...]
    cell_z = (cell % GZ).astype(F32)
    values = [
        (row_ref[...] + ((col >> 11) & 1) * 256 - 256).astype(F32),
        (cell // GZ + ((col >> 10) & 1) * 256 - 256).astype(F32),
        ((col & 511) - 256).astype(F32),
        (cell % GZ + ((col >> 9) & 1) * 128).astype(F32),
        *split2(expo_ref[...]),
        *split2(pref_ref[...]),
    ]
    for index in range(FIELDS):
        fields[8 * index : 8 * index + 8, :] = values[index]
    for part in range(2 * PAIRS):
        matrix[0:FIELDS, part * LANES : part * LANES + LANES] = fields[pl.ds(part, FIELDS, stride=8), :]
    matrix[FIELDS : 2 * FIELDS, :] = jnp.zeros((FIELDS, 2 * PAIRS * LANES), F32)
    faces = jnp.concatenate([jnp.where(cell_z < R, 1.0, 0.0), jnp.where(cell_z >= GZ - R, 1.0, 0.0)], axis=0)
    place, many = ranks(faces)
    slot = iota((LANES, LANES), 0)
    for part in range(2 * PAIRS):
        lanes = pl.ds(part * LANES, LANES)
        for face in range(2):
            hit = slot == place[face * 8 + part : face * 8 + part + 1, :]
            onehot[face * LANES : face * LANES + LANES, lanes] = jnp.where(hit, 1.0, 0.0).astype(BF16)
    listed = lax.dot_general(matrix[...].astype(BF16), onehot[...], NT, preferred_element_type=F32)
    over = jnp.where(jnp.max(many, axis=0, keepdims=True) > LANES, 1.0, 0.0)
    over = jnp.concatenate([over, over], axis=1)
    listed = jnp.where(iota(listed.shape, 0) == FLAG, over, listed).astype(BF16)
    copies = outs[:3] if paired else outs[:1]
    for out in copies:
        out[0:LANES, :] = turned
        for at in range(PAIRS // 2):
            halves = [matrix[0:FIELDS, pair * UNIT : pair * UNIT + UNIT] for pair in (2 * at, 2 * at + 1)]
            out[LANES + 16 * at : LANES + 16 * at + 16, :] = jnp.concatenate(halves, axis=0).astype(BF16)
        out[LANES + 8 * PAIRS : BASE, :] = listed

    def piece(chunk):
        return h_piece(h_ref, hm_ref, chunk)

    if paired:
        outs[1][BASE:, 0:LANES] = piece(layer ^ 2)
        outs[1][BASE:, LANES:UNIT] = piece(layer ^ 3)
        outs[2][BASE:, 0:LANES] = piece(layer ^ 1)
        outs[2][BASE:, LANES:UNIT] = piece(layer)
    else:
        for back in range(h_ref.shape[1] // LANES):
            outs[1][back] = piece(lax.rem(layer + back, count))


def prepare(paired, p, p_mask, h, h_mask, *gauss):
    band = p.shape[0]
    base = jax.ShapeDtypeStruct((BASE, band), BF16)
    tall = jax.ShapeDtypeStruct((BASE + h.shape[0], band), BF16)
    if paired:
        outs = (base, tall, tall)
    else:
        outs = (base, jax.ShapeDtypeStruct((h.shape[1] // LANES, h.shape[0], LANES), BF16))
    return pl.pallas_call(
        functools.partial(prepare_kernel, paired),
        out_shape=outs,
        in_specs=[HBM] * 9,
        out_specs=(VMEM,) * len(outs),
        scratch_shapes=[
            pltpu.VMEM(p.shape, p.dtype),
            pltpu.SMEM(p_mask.shape, p_mask.dtype),
            pltpu.VMEM(h.shape, h.dtype),
            pltpu.SMEM(h_mask.shape, h_mask.dtype),
            *[pltpu.VMEM(x.shape, x.dtype) for x in gauss],
            pltpu.VMEM(p.shape, F32),
            pltpu.VMEM((FIELDS * 8, LANES), F32),
            pltpu.VMEM((2 * FIELDS, 2 * PAIRS * LANES), F32),
            pltpu.VMEM((UNIT, 2 * PAIRS * LANES), BF16),
            pltpu.SemaphoreType.DMA((9,)),
        ],
        compiler_params=pltpu.CompilerParams(vmem_limit_bytes=62 * 1024 * 1024),
        name="prepare",
    )(p, p_mask, h, h_mask, *gauss)


class Blocks:
    def __init__(self, refs, num_col, num_layer):
        self.refs = refs
        self.num_col, self.num_layer = num_col, num_layer
        self.paired = len(refs) > 1
        self.col, self.layer = lax.axis_index("col"), lax.axis_index("layer")
        self.total = num_col * num_layer
        self.col_shifts = [0, 1] if num_col == 2 else [0, -1, 1]

    def ident(self, index):
        if not self.paired:
            return index
        return (self.layer ^ (index % 4)) * 2 + (self.col ^ (index // 4))

    def matrix(self, index):
        return self.refs[index][0:LANES, :] if self.paired else self.refs[0][index, 0:LANES, :]

    def slab(self, layer, piece):
        index = layer * self.num_col + piece
        return self.refs[0][index, 0:LANES, :]

    def tile(self, which, side, at):
        rows = pl.ds(LANES + 16 * at, 16)
        if self.paired:
            return self.refs[which * 4 + side][rows, :].astype(F32)
        shift_l = 0 if side == 0 else (1 if side == 1 else -1)
        index = lax.rem(self.layer + shift_l + self.num_layer, self.num_layer) * self.num_col
        index += lax.rem(self.col + self.col_shifts[which] + self.num_col, self.num_col)
        return self.refs[0][index, rows, :].astype(F32)

    def side_shift(self, side):
        if self.paired:
            even = (self.layer % 2) == 0
            return jnp.where(even, 1.0, -1.0) if side == 1 else jnp.where(even, -1.0, 1.0)
        return 1.0 if side == 1 else -1.0

    def sides(self):
        return (1, 3) if self.paired else (1, 2)

    def units(self):
        return [(which, pair) for which in range(len(self.col_shifts)) for pair in range(PAIRS + 1)]

    def listed(self, which):
        halves = []
        for side in self.sides():
            both = self.tile(which, side, PAIRS // 2)[0:FIELDS, :]
            upward = self.side_shift(side) > 0
            halves.append(jnp.where(upward, both[:, 0:LANES], both[:, LANES:UNIT]))
        return jnp.concatenate(halves, axis=1)

    def unit(self, which, pair):
        if pair == PAIRS:
            return Gaussians(self.listed(which))
        half = (pair % 2) * FIELDS
        return Gaussians(self.tile(which, 0, pair // 2)[half : half + FIELDS, :])

    def lifts(self, pair):
        if pair < PAIRS:
            return 0.0
        lane = iota((1, UNIT), 1)
        first, second = self.sides()
        return jnp.where(lane < LANES, self.side_shift(first), self.side_shift(second)) * float(GZ)

    def over(self):
        flags = [
            self.tile(which, side, PAIRS // 2)[FLAG : FLAG + 1, :]
            for which in range(len(self.col_shifts))
            for side in self.sides()
        ]
        return functools.reduce(jnp.maximum, flags)

    def long_steps(self):
        return [(which, side) for which in range(len(self.col_shifts)) for side in self.sides()]


def weigh(blocks, whole, tile):
    band = whole.shape[1]
    onehot = jnp.where(iota((band, UNIT), 0) == tile.row, 1.0, 0.0).astype(BF16)
    found = jnp.dot(whole[...], onehot, preferred_element_type=F32)
    picked = jnp.zeros((LANES, UNIT), F32)
    for index in range(blocks.total):
        mine = tile.block == jnp.asarray(blocks.ident(index)).astype(F32)
        picked = jnp.where(mine, found[index * LANES : index * LANES + LANES, :], picked)
    value = jnp.sum(jnp.where(iota((LANES, UNIT), 0) == tile.lane, picked, 0.0), axis=0, keepdims=True)
    return tile.pref * value


def bell(dist, expo):
    square = dist * dist
    return jnp.where(square < (R + 0.5) ** 2, jnp.exp(-expo * square), 0.0)


RIM_X = tuple(range(R)) + tuple(range(GX + R, GX + 2 * R))
CORE_X = tuple(range(R, GX + R))
ALL_X = tuple(range(GX + 2 * R))


def shapes_x(tile):
    return bell(iota((GX + 2 * R, UNIT), 0) - float(R) - tile.x, tile.expo)


def shapes_y(tile, shift, wraps):
    dy = iota((GY, UNIT), 0) - tile.y - float(shift * GY)
    if wraps:
        dy = jnp.where(dy < -float(GY), dy + 2.0 * GY, dy)
    return bell(dy, tile.expo)


def shapes_z(tile, lift):
    return bell(iota((GZ, UNIT), 0) - tile.z - lift, tile.expo)


def fill_planes(ex, ey, places, at, planeh, planel):
    lanes = pl.ds(at * UNIT, UNIT)
    for spot, x in enumerate(places):
        plane = ex[x : x + 1, :] * ey
        plane_hi = plane.astype(BF16)
        planeh[spot * GY : spot * GY + GY, lanes] = plane_hi
        planel[spot * GY : spot * GY + GY, lanes] = (plane - plane_hi.astype(F32)).astype(BF16)


def fill_depth(ez, coef, at, depth):
    weighed = ez * coef
    lanes = pl.ds(at * UNIT, UNIT)
    weighed_hi = weighed.astype(BF16)
    depth[0:GZ, lanes] = weighed_hi
    depth[GZ : 2 * GZ, lanes] = (weighed - weighed_hi.astype(F32)).astype(BF16)


def set_planes(blocks, tile, which, places, at, planeh, planel):
    wraps = blocks.num_col == 2 and which == 1
    fill_planes(shapes_x(tile), shapes_y(tile, blocks.col_shifts[which], wraps), places, at, planeh, planel)


def summed(planeh, planel, depth):
    first = lax.dot_general(planeh, depth, NT, preferred_element_type=F32)
    second = lax.dot_general(planel, depth[0:GZ, :], NT, preferred_element_type=F32)
    return first[:, 0:GZ] + first[:, GZ : 2 * GZ] + second


def rims_kernel(num_col, num_layer, refs_in, *refs):
    blocks = Blocks(refs[:refs_in], num_col, num_layer)
    low_ref, high_ref, depth, extra, whole, planeh, planel, longh, longl, long_depth, acc = refs[refs_in:]
    for index in range(blocks.total):
        whole[index * LANES : index * LANES + LANES, :] = blocks.matrix(index)
    over = blocks.over()
    for at, (which, pair) in enumerate(blocks.units()):
        tile = blocks.unit(which, pair)
        coef = weigh(blocks, whole, tile)
        if pair == PAIRS:
            coef = jnp.where(over > 0, 0.0, coef)
        set_planes(blocks, tile, which, RIM_X, at, planeh, planel)
        fill_depth(shapes_z(tile, blocks.lifts(pair)), coef, at, depth)
    total = summed(planeh[...], planel[...], depth[...])
    low_ref[...] = total[0:HALO, :]
    high_ref[...] = total[HALO:, :]

    @pl.when(jnp.max(over) > 0)
    def _():
        acc[...] = jnp.zeros_like(acc)
        for which, side in blocks.long_steps():

            def step(at, carry):
                both = blocks.tile(which, side, at)
                lift = blocks.side_shift(side) * float(GZ)
                for half in range(2):
                    tile = Gaussians(both[half * FIELDS : half * FIELDS + FIELDS, :])
                    set_planes(blocks, tile, which, ALL_X, 0, longh, longl)
                    fill_depth(shapes_z(tile, lift), weigh(blocks, whole, tile), 0, long_depth)
                    acc[...] += summed(longh[...], longl[...], long_depth[...])
                return carry

            lax.fori_loop(0, PAIRS // 2, step, 0)
        low_ref[...] += acc[0:HALO, :]
        extra[...] = acc[HALO : HALO + CORE, :]
        high_ref[...] += acc[HALO + CORE : FULL, :]


def rims(arrays, num_col, num_layer):
    gaussians = (2 if num_col == 2 else 3) * (PAIRS + 1) * UNIT
    return pl.pallas_call(
        functools.partial(rims_kernel, num_col, num_layer, len(arrays)),
        out_shape=(
            jax.ShapeDtypeStruct((HALO, GZ), F32),
            jax.ShapeDtypeStruct((HALO, GZ), F32),
            jax.ShapeDtypeStruct((2 * GZ, gaussians), BF16),
            jax.ShapeDtypeStruct((CORE, GZ), F32),
        ),
        in_specs=[VMEM] * len(arrays),
        out_specs=(VMEM,) * 4,
        scratch_shapes=[
            pltpu.VMEM((num_col * num_layer * LANES, arrays[0].shape[-1]), BF16),
            pltpu.VMEM((2 * HALO, gaussians), BF16),
            pltpu.VMEM((2 * HALO, gaussians), BF16),
            pltpu.VMEM((FULL, UNIT), BF16),
            pltpu.VMEM((FULL, UNIT), BF16),
            pltpu.VMEM((2 * GZ, UNIT), BF16),
            pltpu.VMEM((FULL, GZ), F32),
        ],
        compiler_params=PARAMS,
        cost_estimate=pl.CostEstimate(flops=3_000_000_000, bytes_accessed=1_000_000, transcendentals=0),
        name="rims",
    )(*arrays)


def core_kernel(num_col, num_layer, refs_in, *refs):
    blocks = Blocks(refs[:refs_in], num_col, num_layer)
    depth, extra, core_ref, planeh, planel = refs[refs_in:]
    for at, (which, pair) in enumerate(blocks.units()):
        set_planes(blocks, blocks.unit(which, pair), which, CORE_X, at, planeh, planel)
    core_ref[...] = summed(planeh[...], planel[...], depth[...])

    @pl.when(jnp.max(blocks.over()) > 0)
    def _():
        core_ref[...] += extra[...]


def core_part(arrays, depth, extra, num_col, num_layer):
    gaussians = depth.shape[1]
    return pl.pallas_call(
        functools.partial(core_kernel, num_col, num_layer, len(arrays)),
        out_shape=jax.ShapeDtypeStruct((CORE, GZ), F32),
        in_specs=[VMEM] * (len(arrays) + 2),
        out_specs=VMEM,
        scratch_shapes=[pltpu.VMEM((CORE, gaussians), BF16), pltpu.VMEM((CORE, gaussians), BF16)],
        compiler_params=PARAMS,
        cost_estimate=pl.CostEstimate(flops=1_500_000_000, bytes_accessed=1_000_000, transcendentals=0),
        name="core",
    )(*arrays, depth, extra)


def row_steps(num_row):
    return [0, 1, num_row - 1] + list(range(2, num_row - 1))


def product_kernel(num_row, num_col, num_layer, refs_in, *refs):
    blocks = Blocks(refs[:refs_in], num_col, num_layer)
    h_refs = refs[refs_in : refs_in + num_row]
    out_ref, token_ref, slab = refs[refs_in + num_row :]
    token_ref[...] = jnp.zeros_like(token_ref)
    row = lax.axis_index("row")
    rows = h_refs[0].shape[1]
    for back in range(num_layer):
        for spot, step in enumerate(row_steps(num_row)):
            start = pl.multiple_of(lax.rem(row - step + num_row, num_row) * rows, rows)
            slab[back, pl.ds(start, rows), :] = h_refs[spot][back]
    total = jnp.zeros(out_ref.shape, F32)
    for back in range(num_layer):
        for piece in range(num_col):
            if blocks.paired:
                left = blocks.matrix(piece * 4 + back)
                start = pl.multiple_of((blocks.col ^ piece) * LANES, LANES)
            else:
                source = lax.rem(blocks.layer - back + num_layer, num_layer)
                left = blocks.slab(source, piece)
                start = piece * LANES
            right = slab[back, pl.ds(start, LANES), :]
            total += lax.dot_general(left, right, TN, preferred_element_type=F32)
    out_ref[...] = total.astype(BF16)


def multiply(arrays, parts, num_row, num_col, num_layer):
    return pl.pallas_call(
        functools.partial(product_kernel, num_row, num_col, num_layer, len(arrays)),
        out_shape=(
            jax.ShapeDtypeStruct((arrays[0].shape[-1], LANES), BF16),
            jax.ShapeDtypeStruct((8, LANES), F32),
        ),
        in_specs=[VMEM] * (num_row + len(arrays)),
        out_specs=(VMEM, VMEM),
        scratch_shapes=[pltpu.VMEM((num_layer, num_col * LANES, LANES), BF16)],
        compiler_params=PARAMS,
        cost_estimate=pl.CostEstimate(flops=500_000_000, bytes_accessed=1_000_000, transcendentals=0),
        name="multiply",
    )(*arrays, *parts)


def settle_kernel(block_ref, out_ref):
    out_ref[...] = block_ref[...]


def settle(block):
    return pl.pallas_call(
        settle_kernel,
        out_shape=jax.ShapeDtypeStruct(block.shape, BF16),
        in_specs=[VMEM],
        out_specs=VMEM,
        compiler_params=PARAMS,
        cost_estimate=pl.CostEstimate(flops=1000, bytes_accessed=1000, transcendentals=0),
        name="settle",
    )(block)


def stack_kernel(own_ref, near_ref, far_ref, both_ref, out_ref):
    out_ref[0] = own_ref[BASE:, LANES:UNIT]
    out_ref[1] = near_ref[BASE:, 0:LANES]
    out_ref[2] = far_ref[BASE:, 0:LANES]
    out_ref[3] = both_ref[BASE:, LANES:UNIT]


def stack(own, near, far, both):
    return pl.pallas_call(
        stack_kernel,
        out_shape=jax.ShapeDtypeStruct((4, own.shape[0] - BASE, LANES), BF16),
        in_specs=[VMEM] * 4,
        out_specs=VMEM,
        compiler_params=PARAMS,
        name="stack",
    )(own, near, far, both)


def fold_kernel(core_ref, below_ref, above_ref, after_ref, out_ref):
    out_ref[0:HALO, :] = core_ref[0:HALO, :] + below_ref[...]
    out_ref[HALO : CORE - HALO, :] = core_ref[HALO : CORE - HALO, :]
    out_ref[CORE - HALO : CORE, :] = core_ref[CORE - HALO : CORE, :] + above_ref[...]


def fold(core, below, above, after):
    return pl.pallas_call(
        fold_kernel,
        out_shape=jax.ShapeDtypeStruct((CORE, GZ), F32),
        in_specs=[VMEM] * 4,
        out_specs=VMEM,
        compiler_params=PARAMS,
        cost_estimate=pl.CostEstimate(flops=1_000_000, bytes_accessed=400_000, transcendentals=0),
        name="fold",
    )(core, below, above, after)


def shifted(value, axis, count, step):
    return lax.ppermute(value, axis, [(i, (i + step) % count) for i in range(count)])


def crossed(value, col_bit, layer_bits):
    pairs = [(c * 4 + l, (c ^ col_bit) * 4 + (l ^ layer_bits)) for c in range(2) for l in range(4)]
    return lax.ppermute(value, ("col", "layer"), pairs)


def gather_paired(base, tall_y, tall_core):
    got_x = crossed(base, 1, 0)
    got_y = crossed(tall_y, 0, 2)
    got_xy = crossed(base, 1, 2)
    near = crossed(tall_core, 0, 1)
    near_x = crossed(got_x, 0, 1)
    near_y = crossed(got_y, 0, 1)
    near_xy = crossed(got_xy, 0, 1)
    return [tall_core, near, got_y, near_y, got_x, near_x, got_xy, near_xy]


def on_device(p_slabs, p_mask, h_slabs, h_mask, gauss_row, gauss_col, gauss_cell, gauss_expo, gauss_pref):
    num_row, num_col, num_layer = (lax.axis_size(axis) for axis in ("row", "col", "layer"))
    paired = num_col == 2 and num_layer == 4
    flat = [x.reshape(8, LANES) for x in (gauss_row, gauss_col, gauss_cell, gauss_expo, gauss_pref)]
    made = prepare(paired, p_slabs[0], p_mask[0].T, h_slabs[0], h_mask[0], *flat)
    if paired:
        arrays = gather_paired(*made[:2], settle(made[2]))
        mine = stack(*arrays[:4])
    else:
        base, pieces = made
        arrays = [lax.all_gather(base, ("layer", "col"), axis=0)]
        mine = [pieces[0]] + [shifted(pieces[step], "layer", num_layer, step) for step in range(1, num_layer)]
        mine = jnp.stack(mine)
    low, high, depth, extra = rims(arrays, num_col, num_layer)
    parts = [mine] + [shifted(mine, "row", num_row, step) for step in row_steps(num_row)[1:]]
    below = shifted(high, "row", num_row, 1)
    above = shifted(low, "row", num_row, num_row - 1)
    core = core_part(arrays, depth, extra, num_col, num_layer)
    product, token = multiply(arrays, parts, num_row, num_col, num_layer)
    density = fold(core, below, above, token).reshape(GX, GY, GZ)
    return (product, density)


def solution(mesh):
    placed = (P("layer", "row", "col"),) * 4 + (P(("row", "col", "layer")),) * 5
    return jax.shard_map(
        on_device,
        mesh=mesh,
        in_specs=placed,
        out_specs=(P("row", ("col", "layer")), P("row", "col", "layer")),
        check_vma=False,
    )
```
